32 devices in a mesh: chaos: 4 (over x, core), tile: 8 (over z, y).
Axes of the slice: x: 2, y: 2, z: 4, core: 2. Of those that a mesh axis runs over, the one named last changes fastest.
Arguments:
- slot_field: float32 [288, 64, 1024], P('chaos', 'tile'), may hold values from -6 to 6
- stiffness: float32 [11, 64, 1024], P(None, 'tile'), may hold values from -6 to 6
- triple_modes: int32 [1606], replicated, may hold values from 0 to 10, as said below
- triple_rows: int32 [1606], replicated, may hold values from 0 to 285
- triple_cols: int32 [1606], replicated, may hold values from 0 to 285
- triple_weights: bfloat16 [1606], replicated
- slot_of: int32 [288], replicated, may hold values from 0 to 287, each once
Outputs:
- first_apply: float32 [288, 64, 1024], P('chaos', 'tile')
- second_apply: float32 [288, 64, 1024], P('chaos', 'tile')
The draws below stay inside these ranges and needn't reach their ends.
Inputs may be any that keep to these rules, and one draw needn't show every extreme that they name: slot_of is a permutation of the slots; entry c for c < 286 is the slot of chaos index c, the remaining slots hold no chaos index. `triple_modes`: the entries list the nonzero Galerkin triple products of the order-3 Hermite chaos in 10 variables, each (mode, row, col) once, in some order: mode 0 pairs each chaos index with itself, mode k pairs chaos indices whose multi-indices differ by one in variable k.
All inputs are finite; a program needn't handle non-finite values.
Results may differ from the reference program's by a relative error of at most 0.0034.
Values may be sent and summed in bfloat16 or wider, within the bound.
No kernel may reach another device: no remote copies, remote signals or barrier semaphores. Data moves between devices by JAX's collectives and lax.ppermute only.
A program may use at most 64 MiB of HBM per device.

```python
import math
import jax
import jax.numpy as jnp
import numpy as np
from jax import lax

MODES = 10
TERMS = 11
SLOTS = 288
NNZ = 1606
COLS = 1024
NX = 64


def chaos_lists():
    anchor = [0] * MODES
    basis = [tuple(anchor)]
    for first in range(MODES):
        vector = list(anchor)
        vector[first] += 1
        basis.append(tuple(vector))
    for first in range(MODES):
        for second in range(first, MODES):
            vector = list(anchor)
            vector[first] += 1
            vector[second] += 1
            basis.append(tuple(vector))
    for first in range(MODES):
        for second in range(first, MODES):
            for third in range(second, MODES):
                vector = list(anchor)
                vector[first] += 1
                vector[second] += 1
                vector[third] += 1
                basis.append(tuple(vector))
    lookup = {}
    for place in range(len(basis)):
        lookup[basis[place]] = place
    mode_list = []
    row_list = []
    col_list = []
    factor_list = []
    for place in range(len(basis)):
        mode_list.append(0)
        row_list.append(place)
        col_list.append(place)
        factor_list.append(1.0)
    for place in range(len(basis)):
        for dimension in range(MODES):
            raised = list(basis[place])
            raised[dimension] += 1
            raised = tuple(raised)
            if raised in lookup:
                other = lookup[raised]
                factor = math.sqrt(raised[dimension])
                mode_list.extend([dimension + 1, dimension + 1])
                row_list.extend([place, other])
                col_list.extend([other, place])
                factor_list.extend([factor, factor])
    return (np.array(mode_list, np.int32), np.array(row_list, np.int32), np.array(col_list, np.int32), np.array(factor_list, np.float32))


def entry_order(key):
    return jax.random.permutation(key, NNZ)


def draw_triple_modes(key, part):
    order = entry_order(key)
    return jnp.asarray(chaos_lists()[0])[order]


def draw_triple_rows(key, part):
    order = entry_order(key)
    return jnp.asarray(chaos_lists()[1])[order]


def draw_triple_cols(key, part):
    order = entry_order(key)
    return jnp.asarray(chaos_lists()[2])[order]


def draw_triple_weights(key, part):
    order = entry_order(key)
    key = jax.random.fold_in(key, 14)
    lists = chaos_lists()
    uniform_draw = jax.random.uniform(key, (TERMS,), jnp.float32)
    mode_scale = jnp.exp(jnp.log(0.25) + (jnp.log(1.0) - jnp.log(0.25)) * uniform_draw)
    modes_now = jnp.asarray(lists[0])[order]
    factors = jnp.asarray(lists[3])[order]
    return (mode_scale[modes_now] * factors).astype(jnp.bfloat16)


def levels(own_key, shape, pieces, smallest, largest):
    def one(position, shards_of):
        heights = jax.random.uniform(jax.random.fold_in(jax.random.fold_in(own_key, 6), position), (shards_of,), jnp.float32, smallest / len(pieces), largest / len(pieces))
        return jnp.repeat(jnp.exp(heights), shape[position] // shards_of).reshape((-1,) + (1,) * (len(shape) - position - 1))

    gain = one(*pieces[0])
    for cut in pieces[1:]:
        gain = gain * one(*cut)
    return gain


def scatter_about(rng, shape, deviation, limit, split=(), kind=jnp.bfloat16):
    factor_of = levels(rng, shape, split, -0.22, 0.18) if split else 1.0
    drawn = jax.random.normal(rng, shape, jnp.float32) * deviation * factor_of
    return jnp.minimum(jnp.maximum(drawn, -limit), limit).astype(kind)


def setup_inputs(seed: int = 0) -> dict:
    seeds = jax.random.split(jax.random.key(seed), 8)
    return {
        "slot_field": scatter_about(seeds[0], (SLOTS, NX, COLS), 1.0, 6.0, ((0, 4), (1, 8)), jnp.float32),
        "stiffness": scatter_about(seeds[1], (TERMS, NX, COLS), 1.0, 6.0, ((1, 8),), jnp.float32),
        "triple_modes": draw_triple_modes(jax.random.fold_in(seeds[7], 71), 0),
        "triple_rows": draw_triple_rows(jax.random.fold_in(seeds[7], 71), 0),
        "triple_cols": draw_triple_cols(jax.random.fold_in(seeds[7], 71), 0),
        "triple_weights": draw_triple_weights(jax.random.fold_in(seeds[7], 71), 0),
        "slot_of": jax.random.permutation(seeds[6], SLOTS).astype(jnp.int32),
    }


def five_point(slot_field):
    padded = jnp.pad(slot_field, ((0, 0), (1, 1), (1, 1)))
    center = padded[:, 1:-1, 1:-1]
    return padded[:, 2:, 1:-1] + padded[:, :-2, 1:-1] + padded[:, 1:-1, 2:] + padded[:, 1:-1, :-2] - 4.0 * center


def operator_apply(slot_field, tables, stiffness):
    bent = five_point(slot_field).astype(jnp.bfloat16)
    flattened = bent.reshape(bent.shape[0], -1).astype(jnp.float32)
    stiff_flat = stiffness.reshape(stiffness.shape[0], -1)

    def add_mode(total, inputs):
        table_mode, stiff_mode = inputs
        product = jnp.dot(table_mode.astype(jnp.float32), flattened, precision=lax.Precision.HIGHEST)
        return total + stiff_mode[None, :] * product, None

    start_total = jnp.zeros(flattened.shape, jnp.float32)
    moment, unused = lax.scan(add_mode, start_total, (tables, stiff_flat))
    return five_point(moment.reshape(slot_field.shape))


def reference(slot_field, stiffness, triple_modes, triple_rows, triple_cols, triple_weights, slot_of):
    tables = jnp.zeros((TERMS, SLOTS, SLOTS), jnp.float32)
    tables = tables.at[triple_modes, slot_of[triple_rows], slot_of[triple_cols]].add(triple_weights.astype(jnp.float32))
    tables = tables.astype(jnp.bfloat16)
    first_apply = operator_apply(slot_field, tables, stiffness)
    second_apply = operator_apply(first_apply, tables, stiffness)
    return first_apply, second_apply
```

```python
import functools
import jax
import jax.numpy as jnp
from jax import lax
from jax.experimental import pallas as pl
from jax.experimental.pallas import tpu as pltpu
from jax.sharding import PartitionSpec as P

F32, BF16 = jnp.float32, jnp.bfloat16
VMEM = pl.BlockSpec(memory_space=pltpu.VMEM)
PARAMS = pltpu.CompilerParams(vmem_limit_bytes=48 * 1024 * 1024)
NT = (((1,), (1,)), ((), ()))
STEP = 16


def call(kernel, outs, scratch=(), flops=0, moved=0):
    return pl.pallas_call(
        kernel,
        out_shape=outs,
        scratch_shapes=scratch,
        compiler_params=PARAMS,
        cost_estimate=pl.CostEstimate(flops=flops, bytes_accessed=moved, transcendentals=0),
    )


def shape(dims, kind):
    return jax.ShapeDtypeStruct(dims, kind)


def core_side():
    return lax.rem(lax.axis_index("chaos"), 2)


def table_kernel(terms, pair, hubs, slot_total, entries, main_ref, send_ref, picks, cols):
    wide = entries.shape[1]
    modes = entries[0:1, :]
    rows = entries[1:2, :]
    colv = entries[2:3, :]
    weights = entries[3:4, :]
    slots = entries[4:5, :slot_total]
    chip = lax.axis_index("chaos") // 2
    base = (chip * pair).astype(F32)

    index_col = lax.broadcasted_iota(jnp.int32, (slot_total, wide), 0).astype(F32)
    row_hot = jnp.where(index_col == rows, 1.0, 0.0).astype(BF16)
    col_hot = jnp.where(index_col == colv, 1.0, 0.0).astype(BF16)
    ones = jnp.ones((8, wide), BF16)
    degree = lax.dot_general(ones, row_hot, NT, preferred_element_type=F32)
    zeroth = jnp.where(degree == float(terms), 1.0, 0.0)
    col_zeroth = lax.dot_general(
        zeroth.astype(BF16), col_hot, (((1,), (0,)), ((), ())), preferred_element_type=F32
    )
    beside = lax.dot_general(col_zeroth.astype(BF16), row_hot, NT, preferred_element_type=F32)
    even = jnp.where(degree > 5.0, jnp.where(beside > 0.5, zeroth, 1.0), 0.0)
    before = jnp.where(
        lax.broadcasted_iota(jnp.int32, (slot_total, slot_total), 0)
        < lax.broadcasted_iota(jnp.int32, (slot_total, slot_total), 1),
        1.0,
        0.0,
    ).astype(BF16)
    rank = lax.dot_general(
        even.astype(BF16), before, (((1,), (0,)), ((), ())), preferred_element_type=F32
    )
    rank = jnp.where(even > 0.5, rank, -1.0)[0:1, :]
    lane_index = lax.broadcasted_iota(jnp.int32, (hubs, slot_total), 1).astype(F32)
    hub_hit = lax.broadcasted_iota(jnp.int32, (hubs, slot_total), 0).astype(F32) == rank
    hub_index = jnp.sum(jnp.where(hub_hit, lane_index, 0.0), axis=1, keepdims=True)
    hub_slot = jnp.sum(jnp.where(hub_hit, slots, 0.0), axis=1, keepdims=True)
    hub_here = jnp.logical_and(hub_slot >= base, hub_slot < base + float(pair))
    hub_far = jnp.where(hub_here, -5.0, hub_index)
    hub_near = jnp.where(hub_here, hub_index, -5.0)

    place = lax.broadcasted_iota(jnp.int32, (pair, slot_total), 0).astype(F32) + base
    lanes = lax.broadcasted_iota(jnp.int32, (pair, slot_total), 1).astype(F32)
    own_index = jnp.sum(jnp.where(place == slots, lanes, 0.0), axis=1, keepdims=True)

    cols[0:pair, :] = jnp.where(own_index == colv, 1.0, 0.0).astype(BF16)
    tail = cols.shape[0] - pair
    far_pad = jnp.concatenate([hub_far, jnp.full((tail - hubs, 1), -5.0, F32)], axis=0)
    cols[pair:, :] = jnp.where(far_pad == colv, 1.0, 0.0).astype(BF16)

    for mode in range(terms):
        keyed = jnp.where(modes == float(mode), rows, -1.0)
        picks[mode * pair : (mode + 1) * pair, :] = jnp.where(
            own_index == keyed, weights, 0.0
        ).astype(BF16)
    start = terms * pair
    far16 = jnp.concatenate([hub_far, jnp.full((64 - hubs, 1), -5.0, F32)], axis=0)
    for mode in range(1, terms):
        keyed = jnp.where(modes == float(mode), rows, -1.0)
        at = start + (mode - 1) * 64
        picks[at : at + 64, :] = jnp.where(far16 == keyed, weights, 0.0).astype(BF16)

    for mode in range(terms):
        main_ref[mode] = lax.dot_general(
            picks[mode * pair : (mode + 1) * pair, :], cols[...], NT, preferred_element_type=F32
        ).astype(BF16)
    for mode in range(1, terms):
        at = start + (mode - 1) * 64
        send_ref[mode] = lax.dot_general(
            picks[at : at + 64, :], cols[0:pair, :], NT, preferred_element_type=F32
        ).astype(BF16)
    hub_lane = lax.broadcasted_iota(jnp.int32, (pair, cols.shape[0]), 1).astype(F32) - float(pair)
    own_rank = jnp.sum(
        jnp.where(lanes == own_index, rank, 0.0), axis=1, keepdims=True
    )
    main_ref[terms] = jnp.where(
        jnp.logical_and(own_rank >= 0.0, hub_lane == own_rank), 1.0, 0.0
    ).astype(BF16)
    near_rank = lax.broadcasted_iota(jnp.int32, (64, slot_total), 0).astype(F32)
    slot_row = slots
    near_slot = jnp.sum(jnp.where(near_rank == rank, slot_row, 0.0), axis=1, keepdims=True)
    near_has = jnp.sum(jnp.where(near_rank == rank, 1.0, 0.0), axis=1, keepdims=True)
    near_slot = jnp.where(near_has > 0.5, near_slot - base, -5.0)
    send_ref[0] = jnp.where(
        lax.broadcasted_iota(jnp.int32, (64, pair), 1).astype(F32) == near_slot, 1.0, 0.0
    ).astype(BF16)


def split_kernel(slots, rows, half, field, keep, send):
    side = core_side()
    lanes = 128
    tiles = keep.shape[2] // lanes
    for i in range(half + 1):
        near = jnp.where(side == 0, i, rows - 1 - i)
        far = rows - 1 - near
        for j in range(tiles):
            cut = slice(j * lanes, (j + 1) * lanes)
            keep[i, :, cut] = field[pl.ds(j * rows + near, slots, stride=tiles * rows), :]
            send[i, :, cut] = field[pl.ds(j * rows + far, slots, stride=tiles * rows), :]


def merge_kernel(slots, rows, half, keep, got, out):
    side = core_side()
    lanes = 128
    tiles = keep.shape[2] // lanes
    for i in range(half):
        near = jnp.where(side == 0, i, rows - 1 - i)
        far = rows - 1 - near
        for j in range(tiles):
            cut = slice(j * lanes, (j + 1) * lanes)
            out[pl.ds(j * rows + near, slots, stride=tiles * rows), :] = keep[i, :, cut]
            out[pl.ds(j * rows + far, slots, stride=tiles * rows), :] = got[i, :, cut]


def five_point(above, center, below):
    width = center.shape[1]
    lane = lax.broadcasted_iota(jnp.int32, center.shape, 1)
    left = jnp.where(lane == 0, 0.0, pltpu.roll(center, 1, 1))
    right = jnp.where(lane == width - 1, 0.0, pltpu.roll(center, width - 1, 1))
    return above + below + left + right - 4.0 * center


def fill_buffer(bent, stiff, send_table, buffer, row):
    hubs = buffer.shape[1]
    width = bent.shape[2]
    terms = send_table.shape[0]
    side = core_side()
    half = bent.shape[0]
    place = jnp.where(side == 0, row, 2 * half - 1 - row)
    for start in range(0, width, 256):
        cut = slice(start, start + 256)
        value = bent[row, :, cut]
        total = jnp.dot(send_table[0], value, preferred_element_type=F32)
        for mode in range(1, terms):
            part = jnp.dot(send_table[mode], value, preferred_element_type=F32)
            total = total + stiff[mode, pl.ds(place, 1), cut] * part
        buffer[row, :, cut] = total[:hubs].astype(BF16)


def first_bend_kernel(keep, got, halo, stiff, send_table, bent, buffer):
    side = core_side()
    half, pair, width = bent.shape
    own = keep.shape[1]

    def load(row, at, group):
        if row < 0:
            return halo[pl.ds(group * own + at, 8), :]
        mine = group == side
        return jnp.where(mine, keep[row, pl.ds(at, 8), :], got[row, pl.ds(at, 8), :])

    for group in range(2):

        def chunk(k, carry):
            at = pl.multiple_of(k * 8, 8)
            lines = [load(row, at, group) for row in range(-1, half + 1)]
            for row in range(half):
                value = five_point(lines[row], lines[row + 1], lines[row + 2])
                bent[row, pl.ds(group * own + at, 8), :] = value.astype(BF16)
            return carry

        lax.fori_loop(0, own // 8, chunk, 0)
    for row in range(half):
        fill_buffer(bent, stiff, send_table, buffer, row)


def couple_kernel(depth, bent, got, stiff, table, moment, outer, inner, stacked):
    half, pair, width = bent.shape
    hubs = got.shape[1]
    terms = stiff.shape[0]
    side = core_side()
    room = stacked.shape[0]
    stacked[pair + hubs :, :] = jnp.zeros((room - pair - hubs, width), BF16)
    for row in range(half):
        place = jnp.where(side == 0, row, 2 * half - 1 - row)
        stacked[0:pair, :] = bent[row]
        stacked[pair : pair + hubs, :] = got[row]
        for start in range(0, width, 256):
            cut = slice(start, start + 256)
            value = stacked[:, cut]
            total = jnp.dot(table[terms], value, preferred_element_type=F32)
            for mode in range(terms):
                part = jnp.dot(table[mode], value, preferred_element_type=F32)
                total = total + stiff[mode, pl.ds(place, 1), cut] * part
            moment[row, :, cut] = total
            if row < depth:
                outer[row, :, cut] = total.astype(BF16)
            if row >= half - depth:
                inner[half - 1 - row, :, cut] = total.astype(BF16)


def second_bend_kernel(moment, outer, inner, stiff, send_table, keep, send, bent, buffer, held):
    half, pair, width = moment.shape
    own = pair // 2
    side = core_side()
    tile = lax.axis_index("tile")
    last = lax.axis_size("tile") - 1
    at_edge = jnp.where(side == 0, tile == 0, tile == last)

    def chunk(k, carry):
        at = pl.multiple_of(k * STEP, STEP)
        cut = pl.ds(at, STEP)

        def load(row):
            if row < 0:
                return outer[-1 - row, cut, :].astype(F32)
            if row >= half:
                return inner[row - half, cut, :].astype(F32)
            return moment[row, cut, :]

        for row in range(-1, half + 1):
            value = five_point(load(row - 1), load(row), load(row + 1))
            if row < 0:
                value = jnp.where(at_edge, 0.0, value)
            held[row + 1, cut, :] = value
        for row in range(half):
            value = five_point(held[row, cut, :], held[row + 1, cut, :], held[row + 2, cut, :])
            bent[row, cut, :] = value.astype(BF16)
        return carry

    lax.fori_loop(0, pair // STEP, chunk, 0)
    near = pl.multiple_of(side * own, 8)
    far = pl.multiple_of((1 - side) * own, 8)
    for row in range(half):
        keep[row] = held[row + 1, pl.ds(near, own), :]
        send[row] = held[row + 1, pl.ds(far, own), :]
    for row in range(half):
        fill_buffer(bent, stiff, send_table, buffer, row)


def last_kernel(moment, outer, inner, keep, send):
    half, pair, width = moment.shape
    own = pair // 2
    side = core_side()

    for target, group in ((keep, side), (send, 1 - side)):

        def chunk(k, carry):
            at = pl.multiple_of(k * 8, 8)
            cut = pl.ds(pl.multiple_of(group * own + at, 8), 8)

            def load(row):
                if row < 0:
                    return outer[0, cut, :].astype(F32)
                if row >= half:
                    return inner[0, cut, :].astype(F32)
                return moment[row, cut, :]

            for row in range(half):
                target[row, pl.ds(at, 8), :] = five_point(load(row - 1), load(row), load(row + 1))
            return carry

        lax.fori_loop(0, own // 8, chunk, 0)


def body(slot_field, stiffness, triple_modes, triple_rows, triple_cols, triple_weights, slot_of):
    own, rows, width = slot_field.shape
    terms = stiffness.shape[0]
    pair = 2 * own
    half = rows // 2
    chaos = lax.axis_size("chaos")
    tiles = lax.axis_size("tile")
    slot_total = own * chaos
    modes = terms - 1
    hubs = 1 + modes * (modes + 1) // 2
    room = -(-(pair + hubs) // 16) * 16
    side = core_side()

    core_swap = [(i, i ^ 1) for i in range(chaos)]
    chip_swap = [(i, i ^ 2) for i in range(chaos)]
    tile_swap = []
    for high in range(0, chaos, 2):
        for tile in range(tiles - 1):
            one, two = (high + 1) * tiles + tile, high * tiles + tile + 1
            tile_swap += [(one, two), (two, one)]

    def by_core(value):
        return lax.ppermute(value, "chaos", core_swap)

    def by_chip(value):
        return lax.ppermute(value, "chaos", chip_swap)

    def by_tile(value):
        return lax.ppermute(value, ("chaos", "tile"), tile_swap)

    count = triple_modes.shape[0]
    wide = -(-count // 128) * 128

    def line(value, fill):
        value = value.astype(F32)
        return jnp.pad(value, (0, wide - value.shape[0]), constant_values=fill)

    entries = jnp.stack(
        [
            line(triple_modes, -1.0),
            line(triple_rows, -1.0),
            line(triple_cols, -1.0),
            line(triple_weights, 0.0),
            line(slot_of, -1.0),
        ]
        + [jnp.zeros((wide,), F32)] * 3
    )
    main_table, send_table = call(
        functools.partial(table_kernel, terms, pair, hubs, slot_total),
        (shape((terms + 1, pair, room), BF16), shape((terms, 64, pair), BF16)),
        [
            pltpu.VMEM((terms * pair + modes * 64, wide), BF16),
            pltpu.VMEM((room, wide), BF16),
        ],
        4 * 10**9,
        10**6,
    )(entries)

    lanes = width // 128
    flat = slot_field.reshape(own, rows, lanes, 128).transpose(0, 2, 1, 3).reshape(-1, 128)
    line_block = shape((half + 1, own, width), F32)
    keep, send = call(
        functools.partial(split_kernel, own, rows, half), (line_block, line_block), (), 0, 4 * 10**6
    )(flat)
    got = by_core(send)
    edge = jnp.where(
        side == 0,
        jnp.concatenate([keep[0], got[0]], axis=0),
        jnp.concatenate([got[0], keep[0]], axis=0),
    )
    halo = by_tile(edge)
    bent_shape = shape((half, pair, width), BF16)
    buffer_shape = shape((half, hubs, width), BF16)
    moment_shape = shape((half, pair, width), F32)
    out_block = shape((half, own, width), F32)
    bent, buffer = call(first_bend_kernel, (bent_shape, buffer_shape), (), 2 * 10**9, 4 * 10**6)(
        keep, got, halo, stiffness, send_table
    )

    def couple(bent, buffer, depth):
        other = by_chip(buffer)
        edge_shape = shape((depth, pair, width), BF16)
        moment, outer, inner = call(
            functools.partial(couple_kernel, depth),
            (moment_shape, edge_shape, edge_shape),
            [pltpu.VMEM((room, width), BF16)],
            4 * 10**9,
            4 * 10**6,
        )(bent, other, stiffness, main_table)
        return moment, by_tile(outer), by_core(inner)

    def assemble(keep, send):
        flat = call(
            functools.partial(merge_kernel, own, rows, half),
            shape((own * rows * lanes, 128), F32),
            (),
            0,
            4 * 10**6,
        )(keep, by_core(send))
        return flat.reshape(own, lanes, rows, 128).transpose(0, 2, 1, 3).reshape(own, rows, width)

    moment, outer, inner = couple(bent, buffer, 2)
    keep_one, send_one, bent, buffer = call(
        second_bend_kernel,
        (out_block, out_block, bent_shape, buffer_shape),
        [pltpu.VMEM((half + 2, pair, width), F32)],
        2 * 10**9,
        8 * 10**6,
    )(moment, outer, inner, stiffness, send_table)
    first_apply = assemble(keep_one, send_one)
    moment, outer, inner = couple(bent, buffer, 1)
    keep_two, send_two = call(last_kernel, (out_block, out_block), (), 10**7, 4 * 10**6)(
        moment, outer, inner
    )
    second_apply = assemble(keep_two, send_two)
    return first_apply, second_apply


def solution(mesh):
    return jax.shard_map(
        body,
        mesh=mesh,
        in_specs=(P("chaos", "tile", None), P(None, "tile", None), P(), P(), P(), P(), P()),
        out_specs=(P("chaos", "tile", None), P("chaos", "tile", None)),
        check_vma=False,
    )
```

```python
import functools
import jax
import jax.numpy as jnp
from jax import lax
from jax.experimental import pallas as pl
from jax.experimental.pallas import tpu as pltpu
from jax.sharding import PartitionSpec as P

F32, BF16 = jnp.float32, jnp.bfloat16
VMEM = pl.BlockSpec(memory_space=pltpu.VMEM)
TOKEN = jax.ShapeDtypeStruct((8, 128), jnp.float32)
NT = (((1,), (1,)), ((), ()))
STEP = 16


def call(kernel, outs, scratch=(), us=1.0, specs=None, room=12):
    extra = {} if specs is None else {"in_specs": specs}
    return pl.pallas_call(
        kernel,
        out_shape=outs,
        scratch_shapes=scratch,
        compiler_params=pltpu.CompilerParams(vmem_limit_bytes=room * 1024 * 1024),
        cost_estimate=pl.CostEstimate(
            flops=int(us * 1e10), bytes_accessed=10, transcendentals=0
        ),
        **extra,
    )


def shape(dims, kind):
    return jax.ShapeDtypeStruct(dims, kind)


def core_side():
    return lax.rem(lax.axis_index("chaos"), 2)


def table_kernel(terms, pair, hubs, slot_total, entries, unused, main_ref, send_ref, picks, cols):
    wide = entries.shape[1]
    modes = entries[0:1, :]
    rows = entries[1:2, :]
    colv = entries[2:3, :]
    weights = entries[3:4, :]
    slots = entries[4:5, :slot_total]
    chip = lax.axis_index("chaos") // 2
    base = (chip * pair).astype(F32)

    index_col = lax.broadcasted_iota(jnp.int32, (slot_total, wide), 0).astype(F32)
    row_hot = jnp.where(index_col == rows, 1.0, 0.0).astype(BF16)
    col_hot = jnp.where(index_col == colv, 1.0, 0.0).astype(BF16)
    ones = jnp.ones((8, wide), BF16)
    degree = lax.dot_general(ones, row_hot, NT, preferred_element_type=F32)
    zeroth = jnp.where(degree == float(terms), 1.0, 0.0)
    col_zeroth = lax.dot_general(
        zeroth.astype(BF16), col_hot, (((1,), (0,)), ((), ())), preferred_element_type=F32
    )
    beside = lax.dot_general(col_zeroth.astype(BF16), row_hot, NT, preferred_element_type=F32)
    even = jnp.where(degree > 5.0, jnp.where(beside > 0.5, zeroth, 1.0), 0.0)
    before = jnp.where(
        lax.broadcasted_iota(jnp.int32, (slot_total, slot_total), 0)
        < lax.broadcasted_iota(jnp.int32, (slot_total, slot_total), 1),
        1.0,
        0.0,
    ).astype(BF16)
    rank = lax.dot_general(
        even.astype(BF16), before, (((1,), (0,)), ((), ())), preferred_element_type=F32
    )
    rank = jnp.where(even > 0.5, rank, -1.0)[0:1, :]
    lane_index = lax.broadcasted_iota(jnp.int32, (hubs, slot_total), 1).astype(F32)
    hub_hit = lax.broadcasted_iota(jnp.int32, (hubs, slot_total), 0).astype(F32) == rank
    hub_index = jnp.sum(jnp.where(hub_hit, lane_index, 0.0), axis=1, keepdims=True)
    hub_slot = jnp.sum(jnp.where(hub_hit, slots, 0.0), axis=1, keepdims=True)
    hub_here = jnp.logical_and(hub_slot >= base, hub_slot < base + float(pair))
    hub_far = jnp.where(hub_here, -5.0, hub_index)
    hub_near = jnp.where(hub_here, hub_index, -5.0)

    place = lax.broadcasted_iota(jnp.int32, (pair, slot_total), 0).astype(F32) + base
    lanes = lax.broadcasted_iota(jnp.int32, (pair, slot_total), 1).astype(F32)
    own_index = jnp.sum(jnp.where(place == slots, lanes, 0.0), axis=1, keepdims=True)

    cols[0:pair, :] = jnp.where(own_index == colv, 1.0, 0.0).astype(BF16)
    tail = cols.shape[0] - pair
    far_pad = jnp.concatenate([hub_far, jnp.full((tail - hubs, 1), -5.0, F32)], axis=0)
    cols[pair:, :] = jnp.where(far_pad == colv, 1.0, 0.0).astype(BF16)

    for mode in range(terms):
        keyed = jnp.where(modes == float(mode), rows, -1.0)
        picks[mode * pair : (mode + 1) * pair, :] = jnp.where(
            own_index == keyed, weights, 0.0
        ).astype(BF16)
    start = terms * pair
    far16 = jnp.concatenate([hub_far, jnp.full((64 - hubs, 1), -5.0, F32)], axis=0)
    for mode in range(1, terms):
        keyed = jnp.where(modes == float(mode), rows, -1.0)
        at = start + (mode - 1) * 64
        picks[at : at + 64, :] = jnp.where(far16 == keyed, weights, 0.0).astype(BF16)

    for mode in range(terms):
        main_ref[mode] = lax.dot_general(
            picks[mode * pair : (mode + 1) * pair, :], cols[...], NT, preferred_element_type=F32
        ).astype(BF16)
    for mode in range(1, terms):
        at = start + (mode - 1) * 64
        send_ref[mode] = lax.dot_general(
            picks[at : at + 64, :], cols[0:pair, :], NT, preferred_element_type=F32
        ).astype(BF16)
    hub_lane = lax.broadcasted_iota(jnp.int32, (pair, cols.shape[0]), 1).astype(F32) - float(pair)
    own_rank = jnp.sum(
        jnp.where(lanes == own_index, rank, 0.0), axis=1, keepdims=True
    )
    main_ref[terms] = jnp.where(
        jnp.logical_and(own_rank >= 0.0, hub_lane == own_rank), 1.0, 0.0
    ).astype(BF16)
    near_rank = lax.broadcasted_iota(jnp.int32, (64, slot_total), 0).astype(F32)
    slot_row = slots
    near_slot = jnp.sum(jnp.where(near_rank == rank, slot_row, 0.0), axis=1, keepdims=True)
    near_has = jnp.sum(jnp.where(near_rank == rank, 1.0, 0.0), axis=1, keepdims=True)
    near_slot = jnp.where(near_has > 0.5, near_slot - base, -5.0)
    send_ref[0] = jnp.where(
        lax.broadcasted_iota(jnp.int32, (64, pair), 1).astype(F32) == near_slot, 1.0, 0.0
    ).astype(BF16)


def split_kernel(slots, rows, half, field, keep, send):
    side = core_side()
    lanes = 128
    tiles = keep.shape[2] // lanes
    for i in range(half + 1):
        near = jnp.where(side == 0, i, rows - 1 - i)
        far = rows - 1 - near
        for j in range(tiles):
            cut = slice(j * lanes, (j + 1) * lanes)
            keep[i, :, cut] = field[pl.ds(j * rows + near, slots, stride=tiles * rows), :]
            send[i, :, cut] = field[pl.ds(j * rows + far, slots, stride=tiles * rows), :]


def five_point(above, center, below):
    width = center.shape[1]
    lane = lax.broadcasted_iota(jnp.int32, center.shape, 1)
    left = jnp.where(lane == 0, 0.0, pltpu.roll(center, 1, 1))
    right = jnp.where(lane == width - 1, 0.0, pltpu.roll(center, width - 1, 1))
    return above + below + left + right - 4.0 * center


def row_place(index, rows):
    return jnp.where(core_side() == 0, index, rows - 1 - index)


def fill_buffer(value_ref, stiff, send_table, buffer, row, place):
    hubs = buffer.shape[1]
    width = buffer.shape[2]
    terms = send_table.shape[0]
    for start in range(0, width, 256):
        cut = slice(start, start + 256)
        value = value_ref[row, :, cut]
        total = jnp.dot(send_table[0], value, preferred_element_type=F32)
        for mode in range(1, terms):
            part = jnp.dot(send_table[mode], value, preferred_element_type=F32)
            total = total + stiff[mode, pl.ds(place, 1), cut] * part
        buffer[row, :, cut] = total[:hubs].astype(BF16)


def first_inner_kernel(keep, got, stiff, send_table, bent, buffer):
    side = core_side()
    count, pair, width = bent.shape
    own = keep.shape[1]
    for group in range(2):

        def chunk(k, carry):
            at = pl.multiple_of(k * 8, 8)
            cut = pl.ds(at, 8)
            lines = [
                jnp.where(side == group, keep[row, cut, :], got[row, cut, :])
                for row in range(count + 2)
            ]
            for row in range(count):
                value = five_point(lines[row], lines[row + 1], lines[row + 2])
                bent[row, pl.ds(group * own + at, 8), :] = value.astype(BF16)
            return carry

        lax.fori_loop(0, own // 8, chunk, 0)
    for row in range(count):
        fill_buffer(bent, stiff, send_table, buffer, row, row_place(row + 1, stiff.shape[1]))


def first_outer_kernel(keep, got, halo, stiff, send_table, bent, buffer):
    side = core_side()
    own = keep.shape[1]
    for group in range(2):

        def chunk(k, carry):
            at = pl.multiple_of(k * 8, 8)
            cut = pl.ds(at, 8)
            here, below = [
                jnp.where(side == group, keep[row, cut, :], got[row, cut, :]) for row in range(2)
            ]
            far = pl.ds(group * own + at, 8)
            bent[0, far, :] = five_point(halo[far, :], here, below).astype(BF16)
            return carry

        lax.fori_loop(0, own // 8, chunk, 0)
    fill_buffer(bent, stiff, send_table, buffer, 0, row_place(0, stiff.shape[1]))


def couple_kernel(first, outer_row, inner_rows, bent, got, stiff, table, moment, *rest):
    stacked = rest[-1]
    edges = list(rest[:-1])
    outer = edges.pop(0) if outer_row is not None else None
    inner = edges.pop(0) if inner_rows else None
    count, pair, width = bent.shape
    hubs = got.shape[1]
    terms = stiff.shape[0]
    room = stacked.shape[0]
    stacked[pair + hubs :, :] = jnp.zeros((room - pair - hubs, width), BF16)
    for row in range(count):
        place = row_place(first + row, stiff.shape[1])
        stacked[0:pair, :] = bent[row]
        stacked[pair : pair + hubs, :] = got[row]
        for start in range(0, width, 256):
            cut = slice(start, start + 256)
            value = stacked[:, cut]
            total = jnp.dot(table[terms], value, preferred_element_type=F32)
            for mode in range(terms):
                part = jnp.dot(table[mode], value, preferred_element_type=F32)
                total = total + stiff[mode, pl.ds(place, 1), cut] * part
            moment[row, :, cut] = total
            if first + row == outer_row:
                outer[0, :, cut] = total.astype(BF16)
            if first + row in inner_rows:
                inner[inner_rows.index(first + row), :, cut] = total.astype(BF16)


def share(held, keep, send, rows, own):
    side = core_side()
    near = pl.multiple_of(side * own, 8)
    far = pl.multiple_of((1 - side) * own, 8)
    for target, row in enumerate(rows):
        keep[target] = held[row, pl.ds(near, own), :]
        send[target] = held[row, pl.ds(far, own), :]


def second_inner_kernel(row_zero, others, inner, stiff, send_table, held, keep, send, bent, buffer):
    count, pair, width = bent.shape

    def chunk(k, carry):
        cut = pl.ds(pl.multiple_of(k * STEP, STEP), STEP)
        lines = [row_zero[0, cut, :]] + [others[row, cut, :] for row in range(3)]
        lines += [inner[row, cut, :].astype(F32) for row in range(2)]
        for row in range(4):
            held[row, cut, :] = five_point(lines[row], lines[row + 1], lines[row + 2])
        for row in range(2):
            value = five_point(
                held[row, cut, :], held[row + 1, cut, :], held[row + 2, cut, :]
            )
            bent[row, cut, :] = value.astype(BF16)
        return carry

    lax.fori_loop(0, pair // STEP, chunk, 0)
    share(held, keep, send, (0, 1, 2), pair // 2)
    for row in range(count):
        fill_buffer(bent, stiff, send_table, buffer, row, row_place(row + 2, stiff.shape[1]))


def second_outer_kernel(
    row_zero, others, near, next_near, held, stiff, send_table, keep, send, bent, buffer, zero
):
    count, pair, width = bent.shape
    tile = lax.axis_index("tile")
    last = lax.axis_size("tile") - 1
    at_edge = jnp.where(core_side() == 0, tile == 0, tile == last)

    def chunk(k, carry):
        cut = pl.ds(pl.multiple_of(k * STEP, STEP), STEP)
        above = near[0, cut, :].astype(F32)
        beyond = next_near[0, cut, :].astype(F32)
        here = row_zero[0, cut, :]
        outside = jnp.where(at_edge, 0.0, five_point(beyond, above, here))
        zero[0, cut, :] = five_point(above, here, others[0, cut, :])
        bent[0, cut, :] = five_point(outside, zero[0, cut, :], held[0, cut, :]).astype(BF16)
        bent[1, cut, :] = five_point(
            zero[0, cut, :], held[0, cut, :], held[1, cut, :]
        ).astype(BF16)
        return carry

    lax.fori_loop(0, pair // STEP, chunk, 0)
    share(zero, keep, send, (0,), pair // 2)
    for row in range(count):
        fill_buffer(bent, stiff, send_table, buffer, row, row_place(row, stiff.shape[1]))


def last_kernel(rows, load, own, keep, send):
    side = core_side()
    for target, group in ((send, 1 - side), (keep, side)):

        def chunk(k, carry):
            at = pl.multiple_of(k * 8, 8)
            cut = pl.ds(pl.multiple_of(group * own + at, 8), 8)
            for place, row in enumerate(rows):
                target[place, pl.ds(at, 8), :] = five_point(
                    load(row - 1, cut), load(row, cut), load(row + 1, cut)
                )
            return carry

        lax.fori_loop(0, own // 8, chunk, 0)


def last_inner_kernel(outers, inners, inner, keep, send):
    def load(row, cut):
        if row < 2:
            return outers[row, cut, :]
        if row < 4:
            return inners[row - 2, cut, :]
        return inner[0, cut, :].astype(F32)

    last_kernel((1, 2, 3), load, keep.shape[1], keep, send)


def last_outer_kernel(outers, near, unused, keep, send):
    def load(row, cut):
        if row < 0:
            return near[0, cut, :].astype(F32)
        return outers[row, cut, :]

    last_kernel((0,), load, keep.shape[1], keep, send)


def merge_kernel(slots, rows, keep_zero, keep, got_zero, got, out, token):
    token[...] = jnp.zeros_like(token)
    lanes = 128
    tiles = keep.shape[2] // lanes
    for i in range(rows // 2):
        near = row_place(i, rows)
        far = rows - 1 - near
        for source, place in (((keep_zero, keep), near), ((got_zero, got), far)):
            ref, row = (source[0], 0) if i == 0 else (source[1], i - 1)
            for j in range(tiles):
                cut = slice(j * lanes, (j + 1) * lanes)
                out[pl.ds(j * rows + place, slots, stride=tiles * rows), :] = ref[row, :, cut]


def body(slot_field, stiffness, triple_modes, triple_rows, triple_cols, triple_weights, slot_of):
    own, rows, width = slot_field.shape
    terms = stiffness.shape[0]
    pair = 2 * own
    half = rows // 2
    chaos = lax.axis_size("chaos")
    tiles = lax.axis_size("tile")
    slot_total = own * chaos
    modes = terms - 1
    hubs = 1 + modes * (modes + 1) // 2
    room = -(-(pair + hubs) // 16) * 16
    side = core_side()

    core_swap = [(i, i ^ 1) for i in range(chaos)]
    chip_swap = [(i, i ^ 2) for i in range(chaos)]
    tile_swap = []
    for high in range(0, chaos, 2):
        for tile in range(tiles - 1):
            one, two = (high + 1) * tiles + tile, high * tiles + tile + 1
            tile_swap += [(one, two), (two, one)]

    def by_core(value):
        return lax.ppermute(value, "chaos", core_swap)

    def by_chip(value):
        return lax.ppermute(value, "chaos", chip_swap)

    def by_tile(value):
        return lax.ppermute(value, ("chaos", "tile"), tile_swap)

    count = triple_modes.shape[0]
    wide = -(-count // 128) * 128

    def line(value, fill):
        value = value.astype(F32)
        return jnp.pad(value, (0, wide - value.shape[0]), constant_values=fill)

    entries = jnp.stack(
        [
            line(triple_modes, -1.0),
            line(triple_rows, -1.0),
            line(triple_cols, -1.0),
            line(triple_weights, 0.0),
            line(slot_of, -1.0),
        ]
        + [jnp.zeros((wide,), F32)] * 3
    )
    first_row, last_row = slot_field[:, 0, :], slot_field[:, rows - 1, :]
    got_edge = by_core(jnp.where(side == 0, last_row, first_row))
    own_edge = jnp.where(side == 0, first_row, last_row)
    edge = jnp.where(
        side == 0,
        jnp.concatenate([own_edge, got_edge], axis=0),
        jnp.concatenate([got_edge, own_edge], axis=0),
    )
    halo = by_tile(edge)

    main_table, send_table = call(
        functools.partial(table_kernel, terms, pair, hubs, slot_total),
        (shape((terms + 1, pair, room), BF16), shape((terms, 64, pair), BF16)),
        [
            pltpu.VMEM((terms * pair + modes * 64, wide), BF16),
            pltpu.VMEM((room, wide), BF16),
        ],
        6.0,
        [VMEM, pl.BlockSpec(memory_space=pl.ANY)],
        16,
    )(entries, edge)

    lanes = width // 128
    flat = slot_field.reshape(own, rows, lanes, 128).transpose(0, 2, 1, 3).reshape(-1, 128)
    line_block = shape((half + 1, own, width), F32)
    keep, send = call(
        functools.partial(split_kernel, own, rows, half), (line_block, line_block), (), 3.0
    )(flat)
    got = by_core(send)

    def bents(count):
        return (shape((count, pair, width), BF16), shape((count, hubs, width), BF16))

    def outs(count):
        return (shape((count, own, width), F32),) * 2

    def couple(bent, other, first, outer_row, inner_rows):
        count = bent.shape[0]
        out = [shape((count, pair, width), F32)]
        if outer_row is not None:
            out.append(shape((1, pair, width), BF16))
        if inner_rows:
            out.append(shape((len(inner_rows), pair, width), BF16))
        return call(
            functools.partial(couple_kernel, first, outer_row, inner_rows),
            tuple(out),
            [pltpu.VMEM((room, width), BF16)],
            1.2 * count,
        )(bent, other, stiffness, main_table)

    bent_in, buffer_in = call(first_inner_kernel, bents(3), (), 4.0)(
        keep, got, stiffness, send_table
    )
    cross_in = by_chip(buffer_in)
    bent_out, buffer_out = call(first_outer_kernel, bents(1), (), 1.5)(
        keep, got, halo, stiffness, send_table
    )
    cross_out = by_chip(buffer_out)
    moment_in, edge_one, inner = couple(bent_in, cross_in, 1, 1, (3, 2))
    next_near = by_tile(edge_one)
    inner = by_core(inner)
    moment_out, edge_zero = couple(bent_out, cross_out, 0, 0, ())
    near = by_tile(edge_zero)

    held, keep_in, send_in, bent_in, buffer_in = call(
        second_inner_kernel, (shape((4, pair, width), F32),) + outs(3) + bents(2), (), 4.0
    )(moment_out, moment_in, inner, stiffness, send_table)
    got_in = by_core(send_in)
    cross_in = by_chip(buffer_in)
    keep_out, send_out, bent_out, buffer_out = call(
        second_outer_kernel,
        outs(1) + bents(2),
        [pltpu.VMEM((1, pair, width), F32)],
        3.0,
    )(moment_out, moment_in, near, next_near, held, stiffness, send_table)
    cross_out = by_chip(buffer_out)
    got_out = by_core(send_out)
    moment_in, inner = couple(bent_in, cross_in, 2, None, (3,))
    inner = by_core(inner)
    moment_out, edge_zero = couple(bent_out, cross_out, 0, 0, ())
    near = by_tile(edge_zero)

    def assemble(*parts):
        return call(
            functools.partial(merge_kernel, own, rows),
            (shape((own * rows * lanes, 128), F32), TOKEN),
            (),
            3.5,
        )(*parts)

    def restore(flat):
        return flat.reshape(own, lanes, rows, 128).transpose(0, 2, 1, 3).reshape(own, rows, width)

    first_flat, token = assemble(keep_out, keep_in, got_out, got_in)
    keep_in, send_in = call(last_inner_kernel, outs(3), (), 2.0)(moment_out, moment_in, inner)
    got_in = by_core(send_in)
    keep_out, send_out = call(
        last_outer_kernel, outs(1), (), 1.0
    )(moment_out, near, token)
    got_out = by_core(send_out)
    second_flat, unused = assemble(keep_out, keep_in, got_out, got_in)
    return restore(first_flat), restore(second_flat)


def solution(mesh):
    return jax.shard_map(
        body,
        mesh=mesh,
        in_specs=(P("chaos", "tile", None), P(None, "tile", None), P(), P(), P(), P(), P()),
        out_specs=(P("chaos", "tile", None), P("chaos", "tile", None)),
        check_vma=False,
    )
```

```python
import functools
import jax
import jax.numpy as jnp
from jax import lax
from jax.experimental import pallas as pl
from jax.experimental.pallas import tpu as pltpu
from jax.sharding import PartitionSpec as P

F32, BF16 = jnp.float32, jnp.bfloat16
VMEM = pl.BlockSpec(memory_space=pltpu.VMEM)
TOKEN = jax.ShapeDtypeStruct((8, 128), jnp.int32)
ANY = pl.BlockSpec(memory_space=pl.ANY)
NT = (((1,), (1,)), ((), ()))
STEP = 16


def call(kernel, outs, scratch=(), us=1.0, specs=None, room=12):
    extra = {} if specs is None else {"in_specs": specs}
    return pl.pallas_call(
        kernel,
        out_shape=outs,
        scratch_shapes=scratch,
        compiler_params=pltpu.CompilerParams(vmem_limit_bytes=room * 1024 * 1024),
        cost_estimate=pl.CostEstimate(
            flops=int(us * 1e10), bytes_accessed=10, transcendentals=0
        ),
        **extra,
    )


def shape(dims, kind):
    return jax.ShapeDtypeStruct(dims, kind)


def core_side():
    return lax.rem(lax.axis_index("chaos"), 2)


def table_kernel(terms, pair, hubs, slot_total, entries, unused, main_ref, send_ref, picks, cols):
    wide = entries.shape[1]
    modes = entries[0:1, :]
    rows = entries[1:2, :]
    colv = entries[2:3, :]
    weights = entries[3:4, :]
    slots = entries[4:5, :slot_total]
    chip = lax.axis_index("chaos") // 2
    base = (chip * pair).astype(F32)

    index_col = lax.broadcasted_iota(jnp.int32, (slot_total, wide), 0).astype(F32)
    row_hot = jnp.where(index_col == rows, 1.0, 0.0).astype(BF16)
    col_hot = jnp.where(index_col == colv, 1.0, 0.0).astype(BF16)
    ones = jnp.ones((8, wide), BF16)
    degree = lax.dot_general(ones, row_hot, NT, preferred_element_type=F32)
    zeroth = jnp.where(degree == float(terms), 1.0, 0.0)
    col_zeroth = lax.dot_general(
        zeroth.astype(BF16), col_hot, (((1,), (0,)), ((), ())), preferred_element_type=F32
    )
    beside = lax.dot_general(col_zeroth.astype(BF16), row_hot, NT, preferred_element_type=F32)
    even = jnp.where(degree > 5.0, jnp.where(beside > 0.5, zeroth, 1.0), 0.0)
    before = jnp.where(
        lax.broadcasted_iota(jnp.int32, (slot_total, slot_total), 0)
        < lax.broadcasted_iota(jnp.int32, (slot_total, slot_total), 1),
        1.0,
        0.0,
    ).astype(BF16)
    rank = lax.dot_general(
        even.astype(BF16), before, (((1,), (0,)), ((), ())), preferred_element_type=F32
    )
    rank = jnp.where(even > 0.5, rank, -1.0)[0:1, :]
    lane_index = lax.broadcasted_iota(jnp.int32, (hubs, slot_total), 1).astype(F32)
    hub_hit = lax.broadcasted_iota(jnp.int32, (hubs, slot_total), 0).astype(F32) == rank
    hub_index = jnp.sum(jnp.where(hub_hit, lane_index, 0.0), axis=1, keepdims=True)
    hub_slot = jnp.sum(jnp.where(hub_hit, slots, 0.0), axis=1, keepdims=True)
    hub_here = jnp.logical_and(hub_slot >= base, hub_slot < base + float(pair))
    hub_far = jnp.where(hub_here, -5.0, hub_index)
    hub_near = jnp.where(hub_here, hub_index, -5.0)

    place = lax.broadcasted_iota(jnp.int32, (pair, slot_total), 0).astype(F32) + base
    lanes = lax.broadcasted_iota(jnp.int32, (pair, slot_total), 1).astype(F32)
    own_index = jnp.sum(jnp.where(place == slots, lanes, 0.0), axis=1, keepdims=True)

    cols[0:pair, :] = jnp.where(own_index == colv, 1.0, 0.0).astype(BF16)
    tail = cols.shape[0] - pair
    far_pad = jnp.concatenate([hub_far, jnp.full((tail - hubs, 1), -5.0, F32)], axis=0)
    cols[pair:, :] = jnp.where(far_pad == colv, 1.0, 0.0).astype(BF16)

    for mode in range(terms):
        keyed = jnp.where(modes == float(mode), rows, -1.0)
        picks[mode * pair : (mode + 1) * pair, :] = jnp.where(
            own_index == keyed, weights, 0.0
        ).astype(BF16)
    start = terms * pair
    far16 = jnp.concatenate([hub_far, jnp.full((64 - hubs, 1), -5.0, F32)], axis=0)
    for mode in range(1, terms):
        keyed = jnp.where(modes == float(mode), rows, -1.0)
        at = start + (mode - 1) * 64
        picks[at : at + 64, :] = jnp.where(far16 == keyed, weights, 0.0).astype(BF16)

    for mode in range(terms):
        main_ref[mode] = lax.dot_general(
            picks[mode * pair : (mode + 1) * pair, :], cols[...], NT, preferred_element_type=F32
        ).astype(BF16)
    for mode in range(1, terms):
        at = start + (mode - 1) * 64
        send_ref[mode] = lax.dot_general(
            picks[at : at + 64, :], cols[0:pair, :], NT, preferred_element_type=F32
        ).astype(BF16)
    hub_lane = lax.broadcasted_iota(jnp.int32, (pair, cols.shape[0]), 1).astype(F32) - float(pair)
    own_rank = jnp.sum(
        jnp.where(lanes == own_index, rank, 0.0), axis=1, keepdims=True
    )
    main_ref[terms] = jnp.where(
        jnp.logical_and(own_rank >= 0.0, hub_lane == own_rank), 1.0, 0.0
    ).astype(BF16)
    near_rank = lax.broadcasted_iota(jnp.int32, (64, slot_total), 0).astype(F32)
    slot_row = slots
    near_slot = jnp.sum(jnp.where(near_rank == rank, slot_row, 0.0), axis=1, keepdims=True)
    near_has = jnp.sum(jnp.where(near_rank == rank, 1.0, 0.0), axis=1, keepdims=True)
    near_slot = jnp.where(near_has > 0.5, near_slot - base, -5.0)
    send_ref[0] = jnp.where(
        lax.broadcasted_iota(jnp.int32, (64, pair), 1).astype(F32) == near_slot, 1.0, 0.0
    ).astype(BF16)


def edge_kernel(field, near, far, lines, arrived):
    rows = field.shape[1]
    copies = [
        pltpu.make_async_copy(field.at[:, row, :], lines.at[k], arrived.at[k])
        for k, row in enumerate((0, rows - 1))
    ]
    for copy in copies:
        copy.start()
    for copy in copies:
        copy.wait()
    first = core_side() == 0
    near[...] = jnp.where(first, lines[0], lines[1])
    far[...] = jnp.where(first, lines[1], lines[0])


def split_kernel(field, unused, keep, send):
    slots, rows, width = field.shape
    first = core_side() == 0
    for at in range(0, slots, 8):
        lines = jnp.swapaxes(field[at : at + 8], 0, 1)
        for i in range(keep.shape[0]):
            keep[i, at : at + 8, :] = jnp.where(first, lines[i], lines[rows - 1 - i])
            send[i, at : at + 8, :] = jnp.where(first, lines[rows - 1 - i], lines[i])


def five_point(above, center, below):
    width = center.shape[1]
    lane = lax.broadcasted_iota(jnp.int32, center.shape, 1)
    left = jnp.where(lane == 0, 0.0, pltpu.roll(center, 1, 1))
    right = jnp.where(lane == width - 1, 0.0, pltpu.roll(center, width - 1, 1))
    return above + below + left + right - 4.0 * center


def row_place(index, rows):
    return jnp.where(core_side() == 0, index, rows - 1 - index)


def fill_buffer(value_ref, stiff, send_table, buffer, row, place):
    hubs = buffer.shape[1]
    width = buffer.shape[2]
    terms = send_table.shape[0]
    for start in range(0, width, 256):
        cut = slice(start, start + 256)
        value = value_ref[row, :, cut]
        total = jnp.dot(send_table[0], value, preferred_element_type=F32)
        for mode in range(1, terms):
            part = jnp.dot(send_table[mode], value, preferred_element_type=F32)
            total = total + stiff[mode, pl.ds(place, 1), cut] * part
        buffer[row, :, cut] = total[:hubs].astype(BF16)


def first_kernel(first_row, keep, got, *rest):
    halo = rest[0] if first_row == 0 else None
    stiff, send_table, unused, bent, buffer = rest[-5:]
    side = core_side()
    count, pair, width = bent.shape
    own = keep.shape[1]
    for group in range(2):

        def chunk(k, carry):
            at = pl.multiple_of(k * 8, 8)
            cut = pl.ds(at, 8)
            far = pl.ds(group * own + at, 8)
            lines = [
                halo[far, :]
                if row < 0
                else jnp.where(side == group, keep[row, cut, :], got[row, cut, :])
                for row in range(first_row - 1, first_row + count + 1)
            ]
            for row in range(count):
                value = five_point(lines[row], lines[row + 1], lines[row + 2])
                bent[row, far, :] = value.astype(BF16)
            return carry

        lax.fori_loop(0, own // 8, chunk, 0, unroll=3)
    for row in range(count):
        fill_buffer(bent, stiff, send_table, buffer, row, row_place(first_row + row, stiff.shape[1]))


def couple_kernel(first, outer_row, inner_rows, bent, got, stiff, table, moment, *rest):
    stacked = rest[-1]
    edges = list(rest[:-1])
    outer = edges.pop(0) if outer_row is not None else None
    inner = edges.pop(0) if inner_rows else None
    count, pair, width = bent.shape
    hubs = got.shape[1]
    terms = stiff.shape[0]
    room = stacked.shape[0]
    stacked[pair + hubs :, :] = jnp.zeros((room - pair - hubs, width), BF16)
    for row in range(count):
        place = row_place(first + row, stiff.shape[1])
        stacked[0:pair, :] = bent[row]
        stacked[pair : pair + hubs, :] = got[row]
        for start in range(0, width, 256):
            cut = slice(start, start + 256)
            value = stacked[:, cut]
            total = jnp.dot(table[terms], value, preferred_element_type=F32)
            for mode in range(terms):
                part = jnp.dot(table[mode], value, preferred_element_type=F32)
                total = total + stiff[mode, pl.ds(place, 1), cut] * part
            moment[row, :, cut] = total
            if first + row == outer_row:
                outer[0, :, cut] = total.astype(BF16)
            if first + row in inner_rows:
                inner[inner_rows.index(first + row), :, cut] = total.astype(BF16)


def share(held, keep, send, rows, own):
    side = core_side()
    near = pl.multiple_of(side * own, 8)
    far = pl.multiple_of((1 - side) * own, 8)
    for target, row in enumerate(rows):
        keep[target] = held[row, pl.ds(near, own), :]
        send[target] = held[row, pl.ds(far, own), :]


def second_inner_kernel(
    row_zero, row_one, others, inner, stiff, send_table, held, keep, send, bent, buffer
):
    count, pair, width = bent.shape

    def chunk(k, carry):
        cut = pl.ds(pl.multiple_of(k * STEP, STEP), STEP)
        lines = [row_zero[0, cut, :], row_one[0, cut, :]] + [others[row, cut, :] for row in range(2)]
        lines += [inner[row, cut, :].astype(F32) for row in range(2)]
        for row in range(4):
            held[row, cut, :] = five_point(lines[row], lines[row + 1], lines[row + 2])
        for row in range(2):
            value = five_point(
                held[row, cut, :], held[row + 1, cut, :], held[row + 2, cut, :]
            )
            bent[row, cut, :] = value.astype(BF16)
        return carry

    lax.fori_loop(0, pair // STEP, chunk, 0, unroll=3)
    share(held, keep, send, (0, 1, 2), pair // 2)
    for row in range(count):
        fill_buffer(bent, stiff, send_table, buffer, row, row_place(row + 2, stiff.shape[1]))


def second_edge_kernel(
    row_zero, others, near, next_near, held, stiff, send_table, unused, zero, keep, send, bent, buffer
):
    pair = bent.shape[1]
    tile = lax.axis_index("tile")
    last = lax.axis_size("tile") - 1
    at_edge = jnp.where(core_side() == 0, tile == 0, tile == last)

    def chunk(k, carry):
        cut = pl.ds(pl.multiple_of(k * STEP, STEP), STEP)
        above = near[0, cut, :].astype(F32)
        beyond = next_near[0, cut, :].astype(F32)
        here = row_zero[0, cut, :]
        outside = jnp.where(at_edge, 0.0, five_point(beyond, above, here))
        value = five_point(above, here, others[0, cut, :])
        zero[0, cut, :] = value
        bent[0, cut, :] = five_point(outside, value, held[0, cut, :]).astype(BF16)
        return carry

    lax.fori_loop(0, pair // STEP, chunk, 0, unroll=3)
    fill_buffer(bent, stiff, send_table, buffer, 0, row_place(0, stiff.shape[1]))
    share(zero, keep, send, (0,), pair // 2)


def second_next_kernel(zero, held, stiff, send_table, bent, buffer):
    pair = bent.shape[1]

    def chunk(k, carry):
        cut = pl.ds(pl.multiple_of(k * STEP, STEP), STEP)
        value = five_point(zero[0, cut, :], held[0, cut, :], held[1, cut, :])
        bent[0, cut, :] = value.astype(BF16)
        return carry

    lax.fori_loop(0, pair // STEP, chunk, 0, unroll=3)
    fill_buffer(bent, stiff, send_table, buffer, 0, row_place(1, stiff.shape[1]))


def last_kernel(zero, one, inners, inner, keep, send):
    side = core_side()
    count, own, width = keep.shape
    for target, group in ((send, 1 - side), (keep, side)):

        def chunk(k, carry):
            at = pl.multiple_of(k * 8, 8)
            cut = pl.ds(pl.multiple_of(group * own + at, 8), 8)
            lines = [jnp.zeros((8, width), F32), zero[0, cut, :], one[0, cut, :]]
            lines += [inners[row, cut, :] for row in range(2)]
            lines += [inner[0, cut, :].astype(F32)]
            for row in range(count):
                target[row, pl.ds(at, 8), :] = five_point(
                    lines[row], lines[row + 1], lines[row + 2]
                )
            return carry

        lax.fori_loop(0, own // 8, chunk, 0, unroll=3)


def write_tiles(out, at, near, far):
    first = core_side() == 0
    lines = [jnp.where(first, a, b) for a, b in zip(near, far)]
    lines += [jnp.where(first, b, a) for a, b in zip(near[::-1], far[::-1])]
    out[at : at + 8] = jnp.swapaxes(jnp.stack(lines, axis=0), 0, 1)


def merge_kernel(keep_zero, keep, got_zero, got, unused, out, token):
    token[...] = jnp.zeros_like(token)
    for at in range(0, out.shape[0], 8):
        cut = slice(at, at + 8)
        near = [keep_zero[0, cut, :]] + [keep[i, cut, :] for i in range(keep.shape[0])]
        far = [got_zero[0, cut, :]] + [got[i, cut, :] for i in range(keep.shape[0])]
        write_tiles(out, at, near, far)


def last_merge_kernel(keep, got, near_halo, far_halo, out):
    for at in range(0, out.shape[0], 8):
        cut = slice(at, at + 8)
        near = [keep[i, cut, :] for i in range(keep.shape[0])]
        far = [got[i, cut, :] for i in range(keep.shape[0])]
        near[0] = near[0] + near_halo[cut, :].astype(F32)
        far[0] = far[0] + far_halo[cut, :].astype(F32)
        write_tiles(out, at, near, far)


def body(slot_field, stiffness, triple_modes, triple_rows, triple_cols, triple_weights, slot_of):
    own, rows, width = slot_field.shape
    terms = stiffness.shape[0]
    pair = 2 * own
    half = rows // 2
    chaos = lax.axis_size("chaos")
    tiles = lax.axis_size("tile")
    slot_total = own * chaos
    modes = terms - 1
    hubs = 1 + modes * (modes + 1) // 2
    room = -(-(pair + hubs) // 16) * 16
    side = core_side()

    core_swap = [(i, i ^ 1) for i in range(chaos)]
    chip_swap = [(i, i ^ 2) for i in range(chaos)]
    tile_swap = []
    for high in range(0, chaos, 2):
        for tile in range(tiles - 1):
            one, two = (high + 1) * tiles + tile, high * tiles + tile + 1
            tile_swap += [(one, two), (two, one)]

    def by_core(value):
        return lax.ppermute(value, "chaos", core_swap)

    def by_chip(value):
        return lax.ppermute(value, "chaos", chip_swap)

    def by_tile(value):
        return lax.ppermute(value, ("chaos", "tile"), tile_swap)

    count = triple_modes.shape[0]
    wide = -(-count // 128) * 128

    def line(value, fill):
        value = value.astype(F32)
        return jnp.pad(value, (0, wide - value.shape[0]), constant_values=fill)

    entries = jnp.stack(
        [
            line(triple_modes, -1.0),
            line(triple_rows, -1.0),
            line(triple_cols, -1.0),
            line(triple_weights, 0.0),
            line(slot_of, -1.0),
        ]
        + [jnp.zeros((wide,), F32)] * 3
    )
    row_block = shape((own, width), F32)
    near_edge, far_edge = call(
        edge_kernel,
        (row_block, row_block),
        [pltpu.VMEM((2, own, width), F32), pltpu.SemaphoreType.DMA((2,))],
        2.0,
        [ANY],
        60,
    )(slot_field)
    got_edge = by_core(far_edge)
    edge = jnp.where(
        side == 0,
        jnp.concatenate([near_edge, got_edge], axis=0),
        jnp.concatenate([got_edge, near_edge], axis=0),
    )
    halo = by_tile(edge)

    main_table, send_table = call(
        functools.partial(table_kernel, terms, pair, hubs, slot_total),
        (shape((terms + 1, pair, room), BF16), shape((terms, 64, pair), BF16)),
        [
            pltpu.VMEM((terms * pair + modes * 64, wide), BF16),
            pltpu.VMEM((room, wide), BF16),
        ],
        6.0,
        [VMEM, ANY],
        24,
    )(entries, edge)

    line_block = shape((half + 1, own, width), F32)
    keep, send = call(split_kernel, (line_block, line_block), (), 2.5, [VMEM, ANY])(
        slot_field, edge
    )
    got = by_core(send)

    def bents(count):
        return (shape((count, pair, width), BF16), shape((count, hubs, width), BF16))

    def outs(count):
        return (shape((count, own, width), F32),) * 2

    def bend(first, count, after, *halo):
        bent, buffer = call(
            functools.partial(first_kernel, first),
            bents(count),
            (),
            0.9 * count,
            [VMEM] * (4 + len(halo)) + [ANY],
        )(keep, got, *halo, stiffness, send_table, after)
        return bent, buffer, by_chip(buffer)

    def couple(bent, other, first, outer_row, inner_rows, weight=1.0):
        count = bent.shape[0]
        out = [shape((count, pair, width), F32)]
        if outer_row is not None:
            out.append(shape((1, pair, width), BF16))
        if inner_rows:
            out.append(shape((len(inner_rows), pair, width), BF16))
        return call(
            functools.partial(couple_kernel, first, outer_row, inner_rows),
            tuple(out),
            [pltpu.VMEM((room, width), BF16)],
            weight * count,
        )(bent, other, stiffness, main_table)

    bent_one, sent, cross_one = bend(1, 1, got)
    bent_in, sent, cross_in = bend(2, 2, sent)
    moment_one, edge_one = couple(bent_one, cross_one, 1, 1, ())
    next_near = by_tile(edge_one)
    bent_out, sent, cross_out = bend(0, 1, edge_one, halo)
    moment_in, inner = couple(bent_in, cross_in, 2, None, (3, 2))
    inner = by_core(inner)
    moment_out, edge_zero = couple(bent_out, cross_out, 0, 0, ())
    near = by_tile(edge_zero)

    held, keep_in, send_in, bent_in, buffer_in = call(
        second_inner_kernel, (shape((4, pair, width), F32),) + outs(3) + bents(2), (), 3.5
    )(moment_out, moment_one, moment_in, inner, stiffness, send_table)
    got_in = by_core(send_in)
    cross_in = by_chip(buffer_in)
    zero, keep_out, send_out, bent_out, buffer_out = call(
        second_edge_kernel,
        (shape((1, pair, width), F32),) + outs(1) + bents(1),
        (),
        1.6,
        [VMEM] * 7 + [ANY],
    )(moment_out, moment_one, near, next_near, held, stiffness, send_table, cross_in)
    cross_out = by_chip(buffer_out)
    bent_one, buffer_one = call(second_next_kernel, bents(1), (), 0.01)(
        zero, held, stiffness, send_table
    )
    cross_one = by_chip(buffer_one)
    got_out = by_core(send_out)
    moment_in, inner = couple(bent_in, cross_in, 2, None, (3,), 0.01)
    inner = by_core(inner)
    moment_out, edge_zero = couple(bent_out, cross_out, 0, 0, ())
    near = by_tile(edge_zero)
    (moment_one,) = couple(bent_one, cross_one, 1, None, ())

    keep, send = call(last_kernel, outs(half), (), 2.5)(
        moment_out, moment_one, moment_in, inner
    )
    got = by_core(send)
    first_apply, token = call(
        merge_kernel, (shape(slot_field.shape, F32), TOKEN), (), 1.9, [VMEM] * 4 + [ANY]
    )(keep_out, keep_in, got_out, got_in, keep)
    late_side = side + token[0, 0]
    lower, upper = near[0, :own], near[0, own:]
    near_halo = jnp.where(late_side == 0, lower, upper)
    far_halo = by_core(jnp.where(late_side == 0, upper, lower))
    second_apply = call(last_merge_kernel, shape(slot_field.shape, F32), (), 1.9)(
        keep, got, near_halo, far_halo
    )
    return first_apply, second_apply


def solution(mesh):
    return jax.shard_map(
        body,
        mesh=mesh,
        in_specs=(P("chaos", "tile", None), P(None, "tile", None), P(), P(), P(), P(), P()),
        out_specs=(P("chaos", "tile", None), P("chaos", "tile", None)),
        check_vma=False,
    )
```

```python
import functools
import jax
import jax.numpy as jnp
from jax import lax
from jax.experimental import pallas as pl
from jax.experimental.pallas import tpu as pltpu
from jax.sharding import PartitionSpec as P

F32, BF16 = jnp.float32, jnp.bfloat16
VMEM = pl.BlockSpec(memory_space=pltpu.VMEM)
TOKEN = jax.ShapeDtypeStruct((8, 128), jnp.int32)
ANY = pl.BlockSpec(memory_space=pl.ANY)
NT = (((1,), (1,)), ((), ()))
STEP = 16


def call(kernel, outs, scratch=(), us=1.0, specs=None, room=12, into=None):
    extra = {} if specs is None else {"in_specs": specs}
    if into is not None:
        extra["out_specs"] = into
    return pl.pallas_call(
        kernel,
        out_shape=outs,
        scratch_shapes=scratch,
        compiler_params=pltpu.CompilerParams(vmem_limit_bytes=room * 1024 * 1024),
        cost_estimate=pl.CostEstimate(
            flops=int(us * 1e10), bytes_accessed=10, transcendentals=0
        ),
        **extra,
    )


def shape(dims, kind):
    return jax.ShapeDtypeStruct(dims, kind)


def core_side():
    return lax.rem(lax.axis_index("chaos"), 2)


def table_kernel(
    terms, pair, hubs, slot_total, entries, unused, main_ref, send_ref, picks, codes, cols
):
    wide = entries.shape[1]
    modes = entries[0:1, :]
    rows = entries[1:2, :]
    colv = entries[2:3, :]
    weights = entries[3:4, :]
    slots = entries[4:5, :slot_total]
    chip = lax.axis_index("chaos") // 2
    base = (chip * pair).astype(F32)

    index_col = lax.broadcasted_iota(jnp.int32, (slot_total, wide), 0).astype(F32)
    row_hot = jnp.where(index_col == rows, 1.0, 0.0).astype(BF16)
    col_hot = jnp.where(index_col == colv, 1.0, 0.0).astype(BF16)
    ones = jnp.ones((8, wide), BF16)
    degree = lax.dot_general(ones, row_hot, NT, preferred_element_type=F32)
    zeroth = jnp.where(degree == float(terms), 1.0, 0.0)
    col_zeroth = lax.dot_general(
        zeroth.astype(BF16), col_hot, (((1,), (0,)), ((), ())), preferred_element_type=F32
    )
    beside = lax.dot_general(col_zeroth.astype(BF16), row_hot, NT, preferred_element_type=F32)
    even = jnp.where(degree > 5.0, jnp.where(beside > 0.5, zeroth, 1.0), 0.0)
    before = jnp.where(
        lax.broadcasted_iota(jnp.int32, (slot_total, slot_total), 0)
        < lax.broadcasted_iota(jnp.int32, (slot_total, slot_total), 1),
        1.0,
        0.0,
    ).astype(BF16)
    rank = lax.dot_general(
        even.astype(BF16), before, (((1,), (0,)), ((), ())), preferred_element_type=F32
    )
    rank = jnp.where(even > 0.5, rank, -1.0)[0:1, :]
    lane_index = lax.broadcasted_iota(jnp.int32, (hubs, slot_total), 1).astype(F32)
    hub_hit = lax.broadcasted_iota(jnp.int32, (hubs, slot_total), 0).astype(F32) == rank
    hub_index = jnp.sum(jnp.where(hub_hit, lane_index, 0.0), axis=1, keepdims=True)
    hub_slot = jnp.sum(jnp.where(hub_hit, slots, 0.0), axis=1, keepdims=True)
    hub_here = jnp.logical_and(hub_slot >= base, hub_slot < base + float(pair))
    hub_far = jnp.where(hub_here, -5.0, hub_index)
    hub_near = jnp.where(hub_here, hub_index, -5.0)

    place = lax.broadcasted_iota(jnp.int32, (pair, slot_total), 0).astype(F32) + base
    lanes = lax.broadcasted_iota(jnp.int32, (pair, slot_total), 1).astype(F32)
    own_index = jnp.sum(jnp.where(place == slots, lanes, 0.0), axis=1, keepdims=True)

    tail = cols.shape[0] - pair
    far_cols = jnp.concatenate([hub_far, jnp.full((tail - hubs, 1), -5.0, F32)], axis=0)
    far_rows = jnp.concatenate([hub_far, jnp.full((64 - hubs, 1), -5.0, F32)], axis=0)
    cols[0:pair, :] = jnp.where(own_index == colv, 1.0, 0.0).astype(BF16)
    cols[pair:, :] = jnp.where(far_cols == colv, 1.0, 0.0).astype(BF16)
    coded = modes + 1.0
    for index, start, stop in ((own_index, 0, pair), (far_rows, pair, pair + 64)):
        hit = index == rows
        picks[start:stop, :] = jnp.where(hit, weights, 0.0).astype(BF16)
        codes[start:stop, :] = jnp.where(hit, coded, 0.0).astype(BF16)
    weight = lax.dot_general(picks[...], cols[...], NT, preferred_element_type=F32)
    code = lax.dot_general(codes[...], cols[...], NT, preferred_element_type=F32)
    for mode in range(terms):
        table = jnp.where(code == float(mode + 1), weight, 0.0).astype(BF16)
        main_ref[mode] = table[:pair]
        if mode > 0:
            send_ref[mode] = table[pair:, :pair]
    hub_lane = lax.broadcasted_iota(jnp.int32, (pair, cols.shape[0]), 1).astype(F32) - float(pair)
    own_rank = jnp.sum(
        jnp.where(lanes == own_index, rank, 0.0), axis=1, keepdims=True
    )
    main_ref[terms] = jnp.where(
        jnp.logical_and(own_rank >= 0.0, hub_lane == own_rank), 1.0, 0.0
    ).astype(BF16)
    near_rank = lax.broadcasted_iota(jnp.int32, (64, slot_total), 0).astype(F32)
    slot_row = slots
    near_slot = jnp.sum(jnp.where(near_rank == rank, slot_row, 0.0), axis=1, keepdims=True)
    near_has = jnp.sum(jnp.where(near_rank == rank, 1.0, 0.0), axis=1, keepdims=True)
    near_slot = jnp.where(near_has > 0.5, near_slot - base, -5.0)
    send_ref[0] = jnp.where(
        lax.broadcasted_iota(jnp.int32, (64, pair), 1).astype(F32) == near_slot, 1.0, 0.0
    ).astype(BF16)


def edge_kernel(field, near, far, lines, arrived):
    rows = field.shape[1]
    copies = [
        pltpu.make_async_copy(field.at[:, row, :], lines.at[k], arrived.at[k])
        for k, row in enumerate((0, rows - 1))
    ]
    for copy in copies:
        copy.start()
    for copy in copies:
        copy.wait()
    first = core_side() == 0
    near[...] = jnp.where(first, lines[0], lines[1])
    far[...] = jnp.where(first, lines[1], lines[0])


def split_kernel(field, unused, keep, send):
    slots, rows, width = field.shape
    first = core_side() == 0
    for at in range(0, slots, 8):
        lines = jnp.swapaxes(field[at : at + 8], 0, 1)
        for i in range(keep.shape[0]):
            keep[i, at : at + 8, :] = jnp.where(first, lines[i], lines[rows - 1 - i])
            send[i, at : at + 8, :] = jnp.where(first, lines[rows - 1 - i], lines[i])


def five_point(above, center, below):
    width = center.shape[1]
    lane = lax.broadcasted_iota(jnp.int32, center.shape, 1)
    left = jnp.where(lane == 0, 0.0, pltpu.roll(center, 1, 1))
    right = jnp.where(lane == width - 1, 0.0, pltpu.roll(center, width - 1, 1))
    return above + below + left + right - 4.0 * center


def row_place(index, rows):
    return jnp.where(core_side() == 0, index, rows - 1 - index)


def fill_buffer(value_ref, stiff, send_table, buffer, row, place):
    hubs = buffer.shape[1]
    width = buffer.shape[2]
    terms = send_table.shape[0]
    for start in range(0, width, 256):
        cut = slice(start, start + 256)
        value = value_ref[row, :, cut]
        total = jnp.dot(send_table[0], value, preferred_element_type=F32)
        for mode in range(1, terms):
            part = jnp.dot(send_table[mode], value, preferred_element_type=F32)
            total = total + stiff[mode, pl.ds(place, 1), cut] * part
        buffer[row, :, cut] = total[:hubs].astype(BF16)


def first_kernel(first_row, keep, got, *rest):
    halo = rest[0] if first_row == 0 else None
    stiff, send_table, unused, bent, buffer = rest[-5:]
    side = core_side()
    count, pair, width = bent.shape
    own = keep.shape[1]
    for group in range(2):

        def chunk(k, carry):
            at = pl.multiple_of(k * 8, 8)
            cut = pl.ds(at, 8)
            far = pl.ds(group * own + at, 8)
            lines = [
                halo[far, :]
                if row < 0
                else jnp.where(side == group, keep[row, cut, :], got[row, cut, :])
                for row in range(first_row - 1, first_row + count + 1)
            ]
            for row in range(count):
                value = five_point(lines[row], lines[row + 1], lines[row + 2])
                bent[row, far, :] = value.astype(BF16)
            return carry

        lax.fori_loop(0, own // 8, chunk, 0, unroll=3)
    for row in range(count):
        fill_buffer(bent, stiff, send_table, buffer, row, row_place(first_row + row, stiff.shape[1]))


def couple_kernel(first, outer_row, inner_rows, bent, got, stiff, table, unused, moment, *rest):
    stacked = rest[-1]
    edges = list(rest[:-1])
    outer = edges.pop(0) if outer_row is not None else None
    inner = edges.pop(0) if inner_rows else None
    count, pair, width = bent.shape
    hubs = got.shape[1]
    terms = stiff.shape[0]
    room = stacked.shape[0]
    stacked[pair + hubs :, :] = jnp.zeros((room - pair - hubs, width), BF16)
    for row in range(count):
        place = row_place(first + row, stiff.shape[1])
        stacked[0:pair, :] = bent[row]
        stacked[pair : pair + hubs, :] = got[row]
        for start in range(0, width, 256):
            cut = slice(start, start + 256)
            value = stacked[:, cut]
            total = jnp.dot(table[terms], value, preferred_element_type=F32)
            for mode in range(terms):
                part = jnp.dot(table[mode], value, preferred_element_type=F32)
                total = total + stiff[mode, pl.ds(place, 1), cut] * part
            moment[row, :, cut] = total
            if first + row == outer_row:
                outer[0, :, cut] = total.astype(BF16)
            if first + row in inner_rows:
                inner[inner_rows.index(first + row), :, cut] = total.astype(BF16)


def share(held, keep, send, rows, own):
    side = core_side()
    near = pl.multiple_of(side * own, 8)
    far = pl.multiple_of((1 - side) * own, 8)
    for target, row in enumerate(rows):
        keep[target] = held[row, pl.ds(near, own), :]
        send[target] = held[row, pl.ds(far, own), :]


def second_inner_kernel(
    row_zero, row_one, others, inner, stiff, send_table, held, keep, send, bent, buffer
):
    count, pair, width = bent.shape

    def chunk(k, carry):
        cut = pl.ds(pl.multiple_of(k * STEP, STEP), STEP)
        lines = [row_zero[0, cut, :], row_one[0, cut, :]] + [others[row, cut, :] for row in range(2)]
        lines += [inner[row, cut, :].astype(F32) for row in range(2)]
        for row in range(4):
            held[row, cut, :] = five_point(lines[row], lines[row + 1], lines[row + 2])
        for row in range(2):
            value = five_point(
                held[row, cut, :], held[row + 1, cut, :], held[row + 2, cut, :]
            )
            bent[row, cut, :] = value.astype(BF16)
        return carry

    lax.fori_loop(0, pair // STEP, chunk, 0, unroll=3)
    share(held, keep, send, (0, 1, 2), pair // 2)
    for row in range(count):
        fill_buffer(bent, stiff, send_table, buffer, row, row_place(row + 2, stiff.shape[1]))


def second_edge_kernel(
    row_zero, others, near, next_near, held, stiff, send_table, zero, keep, send, bent, buffer
):
    pair = bent.shape[1]
    tile = lax.axis_index("tile")
    last = lax.axis_size("tile") - 1
    at_edge = jnp.where(core_side() == 0, tile == 0, tile == last)

    def chunk(k, carry):
        cut = pl.ds(pl.multiple_of(k * STEP, STEP), STEP)
        above = near[0, cut, :].astype(F32)
        beyond = next_near[0, cut, :].astype(F32)
        here = row_zero[0, cut, :]
        outside = jnp.where(at_edge, 0.0, five_point(beyond, above, here))
        value = five_point(above, here, others[0, cut, :])
        zero[0, cut, :] = value
        bent[0, cut, :] = five_point(outside, value, held[0, cut, :]).astype(BF16)
        return carry

    lax.fori_loop(0, pair // STEP, chunk, 0, unroll=3)
    fill_buffer(bent, stiff, send_table, buffer, 0, row_place(0, stiff.shape[1]))
    share(zero, keep, send, (0,), pair // 2)


def second_next_kernel(zero, held, stiff, send_table, unused, bent, buffer):
    pair = bent.shape[1]

    def chunk(k, carry):
        cut = pl.ds(pl.multiple_of(k * STEP, STEP), STEP)
        value = five_point(zero[0, cut, :], held[0, cut, :], held[1, cut, :])
        bent[0, cut, :] = value.astype(BF16)
        return carry

    lax.fori_loop(0, pair // STEP, chunk, 0, unroll=3)
    fill_buffer(bent, stiff, send_table, buffer, 0, row_place(1, stiff.shape[1]))


def last_kernel(zero, one, inners, inner, keep, send):
    side = core_side()
    count, own, width = keep.shape
    for target, group in ((send, 1 - side), (keep, side)):

        def chunk(k, carry):
            at = pl.multiple_of(k * 8, 8)
            cut = pl.ds(pl.multiple_of(group * own + at, 8), 8)
            lines = [jnp.zeros((8, width), F32), zero[0, cut, :], one[0, cut, :]]
            lines += [inners[row, cut, :] for row in range(2)]
            lines += [inner[0, cut, :].astype(F32)]
            for row in range(count):
                target[row, pl.ds(at, 8), :] = five_point(
                    lines[row], lines[row + 1], lines[row + 2]
                )
            return carry

        lax.fori_loop(0, own // 8, chunk, 0, unroll=3)


def write_tiles(near, far, out, lines, done):
    first = core_side() == 0
    half = out.shape[1] // 2
    step = 24
    copies = []
    for k, at in enumerate(range(0, out.shape[0], step)):
        for start in range(at, at + step, 8):
            ours = [near(i, slice(start, start + 8)) for i in range(half)]
            theirs = [far(i, slice(start, start + 8)) for i in range(half)]
            rows = [jnp.where(first, a, b) for a, b in zip(ours, theirs)]
            rows += [jnp.where(first, b, a) for a, b in zip(ours[::-1], theirs[::-1])]
            lines[start : start + 8] = jnp.swapaxes(jnp.stack(rows, axis=0), 0, 1)
        cut = pl.ds(at, step)
        copies.append(pltpu.make_async_copy(lines.at[cut], out.at[cut], done.at[k]))
        copies[-1].start()
    for copy in copies:
        copy.wait()


def merge_kernel(keep_zero, keep, got_zero, got, unused, out, token, lines, done):
    token[...] = jnp.zeros_like(token)

    def near(i, cut):
        return keep_zero[0, cut, :] if i == 0 else keep[i - 1, cut, :]

    def far(i, cut):
        return got_zero[0, cut, :] if i == 0 else got[i - 1, cut, :]

    write_tiles(near, far, out, lines, done)


def last_merge_kernel(keep, got, halo, far_halo, out, lines, done):
    own = keep.shape[1]
    first = core_side() == 0
    halos = halo[0].astype(F32)
    near_line = jnp.where(first, halos[:own], halos[own:])
    far_line = far_halo[...].astype(F32)

    def near(i, cut):
        return keep[0, cut, :] + near_line[cut] if i == 0 else keep[i, cut, :]

    def far(i, cut):
        return got[0, cut, :] + far_line[cut] if i == 0 else got[i, cut, :]

    write_tiles(near, far, out, lines, done)


def body(slot_field, stiffness, triple_modes, triple_rows, triple_cols, triple_weights, slot_of):
    own, rows, width = slot_field.shape
    terms = stiffness.shape[0]
    pair = 2 * own
    half = rows // 2
    chaos = lax.axis_size("chaos")
    tiles = lax.axis_size("tile")
    slot_total = own * chaos
    modes = terms - 1
    hubs = 1 + modes * (modes + 1) // 2
    room = -(-(pair + hubs) // 16) * 16
    side = core_side()

    core_swap = [(i, i ^ 1) for i in range(chaos)]
    chip_swap = [(i, i ^ 2) for i in range(chaos)]
    tile_swap = []
    for high in range(0, chaos, 2):
        for tile in range(tiles - 1):
            one, two = (high + 1) * tiles + tile, high * tiles + tile + 1
            tile_swap += [(one, two), (two, one)]

    def by_core(value):
        return lax.ppermute(value, "chaos", core_swap)

    def by_chip(value):
        return lax.ppermute(value, "chaos", chip_swap)

    def by_tile(value):
        return lax.ppermute(value, ("chaos", "tile"), tile_swap)

    count = triple_modes.shape[0]
    wide = -(-count // 128) * 128

    def line(value, fill):
        value = value.astype(F32)
        return jnp.pad(value, (0, wide - value.shape[0]), constant_values=fill)

    entries = jnp.stack(
        [
            line(triple_modes, -1.0),
            line(triple_rows, -1.0),
            line(triple_cols, -1.0),
            line(triple_weights, 0.0),
            line(slot_of, -1.0),
        ]
        + [jnp.zeros((wide,), F32)] * 3
    )
    row_block = shape((own, width), F32)
    near_edge, far_edge = call(
        edge_kernel,
        (row_block, row_block),
        [pltpu.VMEM((2, own, width), F32), pltpu.SemaphoreType.DMA((2,))],
        2.0,
        [ANY],
        60,
    )(slot_field)
    got_edge = by_core(far_edge)
    edge = jnp.where(
        side == 0,
        jnp.concatenate([near_edge, got_edge], axis=0),
        jnp.concatenate([got_edge, near_edge], axis=0),
    )
    halo = by_tile(edge)

    main_table, send_table = call(
        functools.partial(table_kernel, terms, pair, hubs, slot_total),
        (shape((terms + 1, pair, room), BF16), shape((terms, 64, pair), BF16)),
        [
            pltpu.VMEM((pair + 64, wide), BF16),
            pltpu.VMEM((pair + 64, wide), BF16),
            pltpu.VMEM((room, wide), BF16),
        ],
        3.0,
        [VMEM, ANY],
        12,
    )(entries, edge)

    line_block = shape((half + 1, own, width), F32)
    keep, send = call(split_kernel, (line_block, line_block), (), 2.5, [VMEM, ANY])(
        slot_field, edge
    )
    got = by_core(send)

    def bents(count):
        return (shape((count, pair, width), BF16), shape((count, hubs, width), BF16))

    def outs(count):
        return (shape((count, own, width), F32),) * 2

    def bend(first, count, after, *halo):
        bent, buffer = call(
            functools.partial(first_kernel, first),
            bents(count),
            (),
            0.9 * count,
            [VMEM] * (4 + len(halo)) + [ANY],
        )(keep, got, *halo, stiffness, send_table, after)
        return bent, buffer, by_chip(buffer)

    def couple(bent, other, first, outer_row, inner_rows, after, weight=1.0):
        count = bent.shape[0]
        out = [shape((count, pair, width), F32)]
        if outer_row is not None:
            out.append(shape((1, pair, width), BF16))
        if inner_rows:
            out.append(shape((len(inner_rows), pair, width), BF16))
        return call(
            functools.partial(couple_kernel, first, outer_row, inner_rows),
            tuple(out),
            [pltpu.VMEM((room, width), BF16)],
            weight * count,
            [VMEM] * 4 + [ANY],
        )(bent, other, stiffness, main_table, after)

    bent_one, sent, cross_one = bend(1, 1, got)
    bent_in, sent, cross_in = bend(2, 2, sent)
    moment_one, edge_one = couple(bent_one, cross_one, 1, 1, (), sent)
    next_near = by_tile(edge_one)
    bent_out, sent, cross_out = bend(0, 1, edge_one, halo)
    moment_in, edge_in = couple(bent_in, cross_in, 2, None, (3, 2), sent)
    inner = by_core(edge_in)
    moment_out, edge_zero = couple(bent_out, cross_out, 0, 0, (), edge_in)
    near = by_tile(edge_zero)

    held, keep_in, send_in, bent_in, buffer_in = call(
        second_inner_kernel, (shape((4, pair, width), F32),) + outs(3) + bents(2), (), 3.5
    )(moment_out, moment_one, moment_in, inner, stiffness, send_table)
    got_in = by_core(send_in)
    cross_in = by_chip(buffer_in)
    zero, keep_out, send_out, bent_out, buffer_out = call(
        second_edge_kernel,
        (shape((1, pair, width), F32),) + outs(1) + bents(1),
        (),
        0.01,
    )(moment_out, moment_one, near, next_near, held, stiffness, send_table)
    cross_out = by_chip(buffer_out)
    bent_one, buffer_one = call(second_next_kernel, bents(1), (), 0.01, [VMEM] * 4 + [ANY])(
        zero, held, stiffness, send_table, cross_in
    )
    cross_one = by_chip(buffer_one)
    got_out = by_core(send_out)
    moment_out, edge_zero = couple(bent_out, cross_out, 0, 0, (), buffer_one)
    near = by_tile(edge_zero)
    moment_in, inner = couple(bent_in, cross_in, 2, None, (3,), edge_zero)
    inner = by_core(inner)
    (moment_one,) = couple(bent_one, cross_one, 1, None, (), edge_zero)

    keep, send = call(last_kernel, outs(half), (), 2.5)(
        moment_out, moment_one, moment_in, inner
    )
    got = by_core(send)
    whole = shape(slot_field.shape, F32)
    writers = [pltpu.VMEM(slot_field.shape, F32), pltpu.SemaphoreType.DMA((own // 24,))]
    first_apply, token = call(
        merge_kernel, (whole, TOKEN), writers, 1.9, [VMEM] * 4 + [ANY], 6, (ANY, VMEM)
    )(keep_out, keep_in, got_out, got_in, keep)
    late_side = side + token[0, 0]
    far_halo = by_core(jnp.where(late_side == 0, near[0, own:], near[0, :own]))
    second_apply = call(last_merge_kernel, whole, writers, 1.9, [VMEM] * 4, 6, ANY)(
        keep, got, near, far_halo
    )
    return first_apply, second_apply


def solution(mesh):
    return jax.shard_map(
        body,
        mesh=mesh,
        in_specs=(P("chaos", "tile", None), P(None, "tile", None), P(), P(), P(), P(), P()),
        out_specs=(P("chaos", "tile", None), P("chaos", "tile", None)),
        check_vma=False,
    )
```

```python
import functools
import jax
import jax.numpy as jnp
from jax import lax
from jax.experimental import pallas as pl
from jax.experimental.pallas import tpu as pltpu
from jax.sharding import PartitionSpec as P

F32, BF16 = jnp.float32, jnp.bfloat16
VMEM = pl.BlockSpec(memory_space=pltpu.VMEM)
TOKEN = jax.ShapeDtypeStruct((8, 128), jnp.int32)
ANY = pl.BlockSpec(memory_space=pl.ANY)
NT = (((1,), (1,)), ((), ()))
STEP = 16


def call(kernel, outs, scratch=(), us=1.0, specs=None, room=12, into=None):
    extra = {} if specs is None else {"in_specs": specs}
    if into is not None:
        extra["out_specs"] = into
    return pl.pallas_call(
        kernel,
        out_shape=outs,
        scratch_shapes=scratch,
        compiler_params=pltpu.CompilerParams(vmem_limit_bytes=room * 1024 * 1024),
        cost_estimate=pl.CostEstimate(
            flops=int(us * 1e10), bytes_accessed=10, transcendentals=0
        ),
        **extra,
    )


def shape(dims, kind):
    return jax.ShapeDtypeStruct(dims, kind)


def core_side():
    return lax.rem(lax.axis_index("chaos"), 2)


def table_kernel(
    terms, pair, hubs, slot_total, entries, unused, main_ref, send_ref, picks, codes, cols
):
    wide = entries.shape[1]
    modes = entries[0:1, :]
    rows = entries[1:2, :]
    colv = entries[2:3, :]
    weights = entries[3:4, :]
    slots = entries[4:5, :slot_total]
    chip = lax.axis_index("chaos") // 2
    base = (chip * pair).astype(F32)

    index_col = lax.broadcasted_iota(jnp.int32, (slot_total, wide), 0).astype(F32)
    row_hot = jnp.where(index_col == rows, 1.0, 0.0).astype(BF16)
    col_hot = jnp.where(index_col == colv, 1.0, 0.0).astype(BF16)
    ones = jnp.ones((8, wide), BF16)
    degree = lax.dot_general(ones, row_hot, NT, preferred_element_type=F32)
    zeroth = jnp.where(degree == float(terms), 1.0, 0.0)
    col_zeroth = lax.dot_general(
        zeroth.astype(BF16), col_hot, (((1,), (0,)), ((), ())), preferred_element_type=F32
    )
    beside = lax.dot_general(col_zeroth.astype(BF16), row_hot, NT, preferred_element_type=F32)
    even = jnp.where(degree > 5.0, jnp.where(beside > 0.5, zeroth, 1.0), 0.0)
    before = jnp.where(
        lax.broadcasted_iota(jnp.int32, (slot_total, slot_total), 0)
        < lax.broadcasted_iota(jnp.int32, (slot_total, slot_total), 1),
        1.0,
        0.0,
    ).astype(BF16)
    rank = lax.dot_general(
        even.astype(BF16), before, (((1,), (0,)), ((), ())), preferred_element_type=F32
    )
    rank = jnp.where(even > 0.5, rank, -1.0)[0:1, :]
    lane_index = lax.broadcasted_iota(jnp.int32, (hubs, slot_total), 1).astype(F32)
    hub_hit = lax.broadcasted_iota(jnp.int32, (hubs, slot_total), 0).astype(F32) == rank
    hub_index = jnp.sum(jnp.where(hub_hit, lane_index, 0.0), axis=1, keepdims=True)
    hub_slot = jnp.sum(jnp.where(hub_hit, slots, 0.0), axis=1, keepdims=True)
    hub_here = jnp.logical_and(hub_slot >= base, hub_slot < base + float(pair))
    hub_far = jnp.where(hub_here, -5.0, hub_index)
    hub_near = jnp.where(hub_here, hub_index, -5.0)

    place = lax.broadcasted_iota(jnp.int32, (pair, slot_total), 0).astype(F32) + base
    lanes = lax.broadcasted_iota(jnp.int32, (pair, slot_total), 1).astype(F32)
    own_index = jnp.sum(jnp.where(place == slots, lanes, 0.0), axis=1, keepdims=True)

    tail = cols.shape[0] - pair
    far_cols = jnp.concatenate([hub_far, jnp.full((tail - hubs, 1), -5.0, F32)], axis=0)
    far_rows = jnp.concatenate([hub_far, jnp.full((64 - hubs, 1), -5.0, F32)], axis=0)
    cols[0:pair, :] = jnp.where(own_index == colv, 1.0, 0.0).astype(BF16)
    cols[pair:, :] = jnp.where(far_cols == colv, 1.0, 0.0).astype(BF16)
    coded = modes + 1.0
    for index, start, stop in ((own_index, 0, pair), (far_rows, pair, pair + 64)):
        hit = index == rows
        picks[start:stop, :] = jnp.where(hit, weights, 0.0).astype(BF16)
        codes[start:stop, :] = jnp.where(hit, coded, 0.0).astype(BF16)
    weight = lax.dot_general(picks[...], cols[...], NT, preferred_element_type=F32)
    code = lax.dot_general(codes[...], cols[...], NT, preferred_element_type=F32)
    for mode in range(terms):
        table = jnp.where(code == float(mode + 1), weight, 0.0).astype(BF16)
        main_ref[mode] = table[:pair]
        if mode > 0:
            send_ref[mode] = table[pair:, :pair]
    hub_lane = lax.broadcasted_iota(jnp.int32, (pair, cols.shape[0]), 1).astype(F32) - float(pair)
    own_rank = jnp.sum(
        jnp.where(lanes == own_index, rank, 0.0), axis=1, keepdims=True
    )
    main_ref[terms] = jnp.where(
        jnp.logical_and(own_rank >= 0.0, hub_lane == own_rank), 1.0, 0.0
    ).astype(BF16)
    near_rank = lax.broadcasted_iota(jnp.int32, (64, slot_total), 0).astype(F32)
    slot_row = slots
    near_slot = jnp.sum(jnp.where(near_rank == rank, slot_row, 0.0), axis=1, keepdims=True)
    near_has = jnp.sum(jnp.where(near_rank == rank, 1.0, 0.0), axis=1, keepdims=True)
    near_slot = jnp.where(near_has > 0.5, near_slot - base, -5.0)
    send_ref[0] = jnp.where(
        lax.broadcasted_iota(jnp.int32, (64, pair), 1).astype(F32) == near_slot, 1.0, 0.0
    ).astype(BF16)


def edge_kernel(field, near, far, lines, arrived):
    rows = field.shape[1]
    copies = [
        pltpu.make_async_copy(field.at[:, row, :], lines.at[k], arrived.at[k])
        for k, row in enumerate((0, rows - 1))
    ]
    for copy in copies:
        copy.start()
    for copy in copies:
        copy.wait()
    first = core_side() == 0
    near[...] = jnp.where(first, lines[0], lines[1])
    far[...] = jnp.where(first, lines[1], lines[0])


def split_kernel(field, unused, keep, send):
    slots, rows, width = field.shape
    first = core_side() == 0
    for at in range(0, slots, 8):
        lines = jnp.swapaxes(field[at : at + 8], 0, 1)
        for i in range(keep.shape[0]):
            keep[i, at : at + 8, :] = jnp.where(first, lines[i], lines[rows - 1 - i])
            send[i, at : at + 8, :] = jnp.where(first, lines[rows - 1 - i], lines[i])


def five_point(above, center, below):
    width = center.shape[1]
    lane = lax.broadcasted_iota(jnp.int32, center.shape, 1)
    left = jnp.where(lane == 0, 0.0, pltpu.roll(center, 1, 1))
    right = jnp.where(lane == width - 1, 0.0, pltpu.roll(center, width - 1, 1))
    return above + below + left + right - 4.0 * center


def row_place(index, rows):
    return jnp.where(core_side() == 0, index, rows - 1 - index)


def fill_buffer(value_ref, stiff, send_table, buffer, row, place):
    hubs = buffer.shape[1]
    width = buffer.shape[2]
    terms = send_table.shape[0]
    for start in range(0, width, 256):
        cut = slice(start, start + 256)
        value = value_ref[row, :, cut]
        total = jnp.dot(send_table[0], value, preferred_element_type=F32)
        for mode in range(1, terms):
            part = jnp.dot(send_table[mode], value, preferred_element_type=F32)
            total = total + stiff[mode, pl.ds(place, 1), cut] * part
        buffer[row, :, cut] = total[:hubs].astype(BF16)


def first_kernel(first_row, keep, got, *rest):
    halos = rest[:2] if first_row == 0 else None
    stiff, send_table, unused, bent, buffer = rest[-5:]
    side = core_side()
    count, pair, width = bent.shape
    own = keep.shape[1]
    for group in range(2):

        def chunk(k, carry):
            at = pl.multiple_of(k * 8, 8)
            cut = pl.ds(at, 8)
            far = pl.ds(group * own + at, 8)
            lines = [
                jnp.where(side == group, halos[0][cut, :], halos[1][cut, :])
                if row < 0
                else jnp.where(side == group, keep[row, cut, :], got[row, cut, :])
                for row in range(first_row - 1, first_row + count + 1)
            ]
            for row in range(count):
                value = five_point(lines[row], lines[row + 1], lines[row + 2])
                bent[row, far, :] = value.astype(BF16)
            return carry

        lax.fori_loop(0, own // 8, chunk, 0, unroll=3)
    for row in range(count):
        fill_buffer(bent, stiff, send_table, buffer, row, row_place(first_row + row, stiff.shape[1]))


def couple_kernel(first, outer_row, inner_rows, bent, got, stiff, table, unused, moment, *rest):
    stacked = rest[-1]
    edges = list(rest[:-1])
    outer = edges.pop(0) if outer_row is not None else None
    inner = edges.pop(0) if inner_rows else None
    count, pair, width = bent.shape
    hubs = got.shape[1]
    terms = stiff.shape[0]
    room = stacked.shape[0]
    stacked[pair + hubs :, :] = jnp.zeros((room - pair - hubs, width), BF16)
    for row in range(count):
        place = row_place(first + row, stiff.shape[1])
        stacked[0:pair, :] = bent[row]
        stacked[pair : pair + hubs, :] = got[row]
        for start in range(0, width, 256):
            cut = slice(start, start + 256)
            value = stacked[:, cut]
            total = jnp.dot(table[terms], value, preferred_element_type=F32)
            for mode in range(terms):
                part = jnp.dot(table[mode], value, preferred_element_type=F32)
                total = total + stiff[mode, pl.ds(place, 1), cut] * part
            moment[row, :, cut] = total
            if first + row == outer_row:
                outer[0, :, cut] = total.astype(BF16)
            if first + row in inner_rows:
                inner[inner_rows.index(first + row), :, cut] = total.astype(BF16)


def share(held, keep, send, rows, own):
    side = core_side()
    near = pl.multiple_of(side * own, 8)
    far = pl.multiple_of((1 - side) * own, 8)
    for target, row in enumerate(rows):
        keep[target] = held[row, pl.ds(near, own), :]
        send[target] = held[row, pl.ds(far, own), :]


def second_inner_kernel(
    row_zero, row_one, others, inner, stiff, send_table, held, keep, send, bent, buffer
):
    count, pair, width = bent.shape

    def chunk(k, carry):
        cut = pl.ds(pl.multiple_of(k * STEP, STEP), STEP)
        lines = [row_zero[0, cut, :], row_one[0, cut, :]] + [others[row, cut, :] for row in range(2)]
        lines += [inner[row, cut, :].astype(F32) for row in range(2)]
        for row in range(4):
            held[row, cut, :] = five_point(lines[row], lines[row + 1], lines[row + 2])
        for row in range(2):
            value = five_point(
                held[row, cut, :], held[row + 1, cut, :], held[row + 2, cut, :]
            )
            bent[row, cut, :] = value.astype(BF16)
        return carry

    lax.fori_loop(0, pair // STEP, chunk, 0, unroll=3)
    share(held, keep, send, (0, 1, 2), pair // 2)
    for row in range(count):
        fill_buffer(bent, stiff, send_table, buffer, row, row_place(row + 2, stiff.shape[1]))


def second_edge_kernel(
    row_zero, others, near, next_near, held, stiff, send_table, zero, keep, send, bent, buffer
):
    pair = bent.shape[1]
    tile = lax.axis_index("tile")
    last = lax.axis_size("tile") - 1
    at_edge = jnp.where(core_side() == 0, tile == 0, tile == last)

    def chunk(k, carry):
        cut = pl.ds(pl.multiple_of(k * STEP, STEP), STEP)
        above = near[0, cut, :].astype(F32)
        beyond = next_near[0, cut, :].astype(F32)
        here = row_zero[0, cut, :]
        outside = jnp.where(at_edge, 0.0, five_point(beyond, above, here))
        value = five_point(above, here, others[0, cut, :])
        zero[0, cut, :] = value
        bent[0, cut, :] = five_point(outside, value, held[0, cut, :]).astype(BF16)
        return carry

    lax.fori_loop(0, pair // STEP, chunk, 0, unroll=3)
    fill_buffer(bent, stiff, send_table, buffer, 0, row_place(0, stiff.shape[1]))
    share(zero, keep, send, (0,), pair // 2)


def second_next_kernel(zero, held, stiff, send_table, unused, bent, buffer):
    pair = bent.shape[1]

    def chunk(k, carry):
        cut = pl.ds(pl.multiple_of(k * STEP, STEP), STEP)
        value = five_point(zero[0, cut, :], held[0, cut, :], held[1, cut, :])
        bent[0, cut, :] = value.astype(BF16)
        return carry

    lax.fori_loop(0, pair // STEP, chunk, 0, unroll=3)
    fill_buffer(bent, stiff, send_table, buffer, 0, row_place(1, stiff.shape[1]))


def last_kernel(zero, one, inners, inner, keep, send):
    side = core_side()
    count, own, width = keep.shape
    for target, group in ((send, 1 - side), (keep, side)):

        def chunk(k, carry):
            at = pl.multiple_of(k * 8, 8)
            cut = pl.ds(pl.multiple_of(group * own + at, 8), 8)
            lines = [jnp.zeros((8, width), F32), zero[0, cut, :], one[0, cut, :]]
            lines += [inners[row, cut, :] for row in range(2)]
            lines += [inner[0, cut, :].astype(F32)]
            for row in range(count):
                target[row, pl.ds(at, 8), :] = five_point(
                    lines[row], lines[row + 1], lines[row + 2]
                )
            return carry

        lax.fori_loop(0, own // 8, chunk, 0, unroll=3)


def write_tiles(near, far, out, lines, done):
    first = core_side() == 0
    half = out.shape[1] // 2
    step = 24
    copies = []
    for k, at in enumerate(range(0, out.shape[0], step)):
        for start in range(at, at + step, 8):
            ours = [near(i, slice(start, start + 8)) for i in range(half)]
            theirs = [far(i, slice(start, start + 8)) for i in range(half)]
            rows = [jnp.where(first, a, b) for a, b in zip(ours, theirs)]
            rows += [jnp.where(first, b, a) for a, b in zip(ours[::-1], theirs[::-1])]
            lines[start : start + 8] = jnp.swapaxes(jnp.stack(rows, axis=0), 0, 1)
        cut = pl.ds(at, step)
        copies.append(pltpu.make_async_copy(lines.at[cut], out.at[cut], done.at[k]))
        copies[-1].start()
    for copy in copies:
        copy.wait()


def merge_kernel(keep_zero, keep, got_zero, got, unused, out, token, lines, done):
    token[...] = jnp.zeros_like(token)

    def near(i, cut):
        return keep_zero[0, cut, :] if i == 0 else keep[i - 1, cut, :]

    def far(i, cut):
        return got_zero[0, cut, :] if i == 0 else got[i - 1, cut, :]

    write_tiles(near, far, out, lines, done)


def last_merge_kernel(keep, got, halo, far_halo, out, lines, done):
    own = keep.shape[1]
    first = core_side() == 0
    halos, others = halo[0].astype(F32), far_halo[0].astype(F32)
    near_line = jnp.where(first, halos[:own], halos[own:])
    far_line = jnp.where(first, others[:own], others[own:])

    def near(i, cut):
        return keep[0, cut, :] + near_line[cut] if i == 0 else keep[i, cut, :]

    def far(i, cut):
        return got[0, cut, :] + far_line[cut] if i == 0 else got[i, cut, :]

    write_tiles(near, far, out, lines, done)


def body(slot_field, stiffness, triple_modes, triple_rows, triple_cols, triple_weights, slot_of):
    own, rows, width = slot_field.shape
    terms = stiffness.shape[0]
    pair = 2 * own
    half = rows // 2
    chaos = lax.axis_size("chaos")
    tiles = lax.axis_size("tile")
    slot_total = own * chaos
    modes = terms - 1
    hubs = 1 + modes * (modes + 1) // 2
    room = -(-(pair + hubs) // 16) * 16
    side = core_side()

    core_swap = [(i, i ^ 1) for i in range(chaos)]
    chip_swap = [(i, i ^ 2) for i in range(chaos)]
    tile_swap = []
    for high in range(0, chaos, 2):
        for tile in range(tiles - 1):
            one, two = (high + 1) * tiles + tile, high * tiles + tile + 1
            tile_swap += [(one, two), (two, one)]

    def by_core(value):
        return lax.ppermute(value, "chaos", core_swap)

    def by_chip(value):
        return lax.ppermute(value, "chaos", chip_swap)

    def by_tile(value):
        return lax.ppermute(value, ("chaos", "tile"), tile_swap)

    count = triple_modes.shape[0]
    wide = -(-count // 128) * 128

    def line(value, fill):
        value = value.astype(F32)
        return jnp.pad(value, (0, wide - value.shape[0]), constant_values=fill)

    entries = jnp.stack(
        [
            line(triple_modes, -1.0),
            line(triple_rows, -1.0),
            line(triple_cols, -1.0),
            line(triple_weights, 0.0),
            line(slot_of, -1.0),
        ]
        + [jnp.zeros((wide,), F32)] * 3
    )
    row_block = shape((own, width), F32)
    near_edge, far_edge = call(
        edge_kernel,
        (row_block, row_block),
        [pltpu.VMEM((2, own, width), F32), pltpu.SemaphoreType.DMA((2,))],
        2.0,
        [ANY],
        60,
    )(slot_field)
    halo_far = by_tile(near_edge)
    got_edge = by_core(far_edge)
    halo_near = by_tile(got_edge)

    main_table, send_table = call(
        functools.partial(table_kernel, terms, pair, hubs, slot_total),
        (shape((terms + 1, pair, room), BF16), shape((terms, 64, pair), BF16)),
        [
            pltpu.VMEM((pair + 64, wide), BF16),
            pltpu.VMEM((pair + 64, wide), BF16),
            pltpu.VMEM((room, wide), BF16),
        ],
        3.0,
        [VMEM, ANY],
        12,
    )(entries, got_edge)

    line_block = shape((half + 1, own, width), F32)
    keep, send = call(split_kernel, (line_block, line_block), (), 2.5, [VMEM, ANY])(
        slot_field, got_edge
    )
    got = by_core(send)

    def bents(count):
        return (shape((count, pair, width), BF16), shape((count, hubs, width), BF16))

    def outs(count):
        return (shape((count, own, width), F32),) * 2

    def bend(first, count, after, *halo):
        bent, buffer = call(
            functools.partial(first_kernel, first),
            bents(count),
            (),
            0.9 * count,
            [VMEM] * (4 + len(halo)) + [ANY],
        )(keep, got, *halo, stiffness, send_table, after)
        return bent, buffer, by_chip(buffer)

    def couple(bent, other, first, outer_row, inner_rows, after, weight=1.0):
        count = bent.shape[0]
        out = [shape((count, pair, width), F32)]
        if outer_row is not None:
            out.append(shape((1, pair, width), BF16))
        if inner_rows:
            out.append(shape((len(inner_rows), pair, width), BF16))
        return call(
            functools.partial(couple_kernel, first, outer_row, inner_rows),
            tuple(out),
            [pltpu.VMEM((room, width), BF16)],
            weight * count,
            [VMEM] * 4 + [ANY],
        )(bent, other, stiffness, main_table, after)

    bent_one, sent, cross_one = bend(1, 1, got)
    bent_in, sent, cross_in = bend(2, 2, sent)
    moment_one, edge_one = couple(bent_one, cross_one, 1, 1, (), sent)
    next_near = by_tile(edge_one)
    bent_out, sent, cross_out = bend(0, 1, edge_one, halo_near, halo_far)
    moment_in, edge_in = couple(bent_in, cross_in, 2, None, (3, 2), sent)
    inner = by_core(edge_in)
    moment_out, edge_zero = couple(bent_out, cross_out, 0, 0, (), edge_in)
    near = by_tile(edge_zero)

    held, keep_in, send_in, bent_in, buffer_in = call(
        second_inner_kernel, (shape((4, pair, width), F32),) + outs(3) + bents(2), (), 3.5
    )(moment_out, moment_one, moment_in, inner, stiffness, send_table)
    got_in = by_core(send_in)
    cross_in = by_chip(buffer_in)
    zero, keep_out, send_out, bent_out, buffer_out = call(
        second_edge_kernel,
        (shape((1, pair, width), F32),) + outs(1) + bents(1),
        (),
        0.01,
    )(moment_out, moment_one, near, next_near, held, stiffness, send_table)
    cross_out = by_chip(buffer_out)
    bent_one, buffer_one = call(second_next_kernel, bents(1), (), 0.01, [VMEM] * 4 + [ANY])(
        zero, held, stiffness, send_table, cross_in
    )
    cross_one = by_chip(buffer_one)
    got_out = by_core(send_out)
    moment_out, edge_zero = couple(bent_out, cross_out, 0, 0, (), buffer_one)
    near = by_tile(edge_zero)
    moment_in, inner = couple(bent_in, cross_in, 2, None, (3,), edge_zero)
    inner = by_core(inner)
    (moment_one,) = couple(bent_one, cross_one, 1, None, (), edge_zero)

    keep, send = call(last_kernel, outs(half), (), 2.5)(
        moment_out, moment_one, moment_in, inner
    )
    got = by_core(send)
    whole = shape(slot_field.shape, F32)
    writers = [pltpu.VMEM(slot_field.shape, F32), pltpu.SemaphoreType.DMA((own // 24,))]
    first_apply, token = call(
        merge_kernel, (whole, TOKEN), writers, 1.9, [VMEM] * 4 + [ANY], 6, (ANY, VMEM)
    )(keep_out, keep_in, got_out, got_in, keep)
    far_halo = by_core(jnp.where(token[0, 0] == 0, near, jnp.zeros_like(near)))
    second_apply = call(last_merge_kernel, whole, writers, 1.9, [VMEM] * 4, 6, ANY)(
        keep, got, near, far_halo
    )
    return first_apply, second_apply


def solution(mesh):
    return jax.shard_map(
        body,
        mesh=mesh,
        in_specs=(P("chaos", "tile", None), P(None, "tile", None), P(), P(), P(), P(), P()),
        out_specs=(P("chaos", "tile", None), P("chaos", "tile", None)),
        check_vma=False,
    )
```

```python
import functools
import jax
import jax.numpy as jnp
from jax import lax
from jax.experimental import pallas as pl
from jax.experimental.pallas import tpu as pltpu
from jax.sharding import PartitionSpec as P

F32, BF16 = jnp.float32, jnp.bfloat16
VMEM = pl.BlockSpec(memory_space=pltpu.VMEM)
TOKEN = jax.ShapeDtypeStruct((8, 128), jnp.int32)
ANY = pl.BlockSpec(memory_space=pl.ANY)
NT = (((1,), (1,)), ((), ()))
STEP = 16


def call(kernel, outs, scratch=(), us=1.0, specs=None, room=12, into=None):
    extra = {} if specs is None else {"in_specs": specs}
    if into is not None:
        extra["out_specs"] = into
    return pl.pallas_call(
        kernel,
        out_shape=outs,
        scratch_shapes=scratch,
        compiler_params=pltpu.CompilerParams(vmem_limit_bytes=room * 1024 * 1024),
        cost_estimate=pl.CostEstimate(
            flops=int(us * 1e10), bytes_accessed=10, transcendentals=0
        ),
        **extra,
    )


def shape(dims, kind):
    return jax.ShapeDtypeStruct(dims, kind)


def core_side():
    return lax.rem(lax.axis_index("chaos"), 2)


def table_kernel(
    terms, pair, hubs, slot_total, entries, unused, main_ref, send_ref, picks, codes, cols
):
    wide = entries.shape[1]
    modes = entries[0:1, :]
    rows = entries[1:2, :]
    colv = entries[2:3, :]
    weights = entries[3:4, :]
    slots = entries[4:5, :slot_total]
    chip = lax.axis_index("chaos") // 2
    base = (chip * pair).astype(F32)

    index_col = lax.broadcasted_iota(jnp.int32, (slot_total, wide), 0).astype(F32)
    row_hot = jnp.where(index_col == rows, 1.0, 0.0).astype(BF16)
    col_hot = jnp.where(index_col == colv, 1.0, 0.0).astype(BF16)
    ones = jnp.ones((8, wide), BF16)
    degree = lax.dot_general(ones, row_hot, NT, preferred_element_type=F32)
    zeroth = jnp.where(degree == float(terms), 1.0, 0.0)
    col_zeroth = lax.dot_general(
        zeroth.astype(BF16), col_hot, (((1,), (0,)), ((), ())), preferred_element_type=F32
    )
    beside = lax.dot_general(col_zeroth.astype(BF16), row_hot, NT, preferred_element_type=F32)
    even = jnp.where(degree > 5.0, jnp.where(beside > 0.5, zeroth, 1.0), 0.0)
    before = jnp.where(
        lax.broadcasted_iota(jnp.int32, (slot_total, slot_total), 0)
        < lax.broadcasted_iota(jnp.int32, (slot_total, slot_total), 1),
        1.0,
        0.0,
    ).astype(BF16)
    rank = lax.dot_general(
        even.astype(BF16), before, (((1,), (0,)), ((), ())), preferred_element_type=F32
    )
    rank = jnp.where(even > 0.5, rank, -1.0)[0:1, :]
    lane_index = lax.broadcasted_iota(jnp.int32, (hubs, slot_total), 1).astype(F32)
    hub_hit = lax.broadcasted_iota(jnp.int32, (hubs, slot_total), 0).astype(F32) == rank
    hub_index = jnp.sum(jnp.where(hub_hit, lane_index, 0.0), axis=1, keepdims=True)
    hub_slot = jnp.sum(jnp.where(hub_hit, slots, 0.0), axis=1, keepdims=True)
    hub_here = jnp.logical_and(hub_slot >= base, hub_slot < base + float(pair))
    hub_far = jnp.where(hub_here, -5.0, hub_index)
    hub_near = jnp.where(hub_here, hub_index, -5.0)

    place = lax.broadcasted_iota(jnp.int32, (pair, slot_total), 0).astype(F32) + base
    lanes = lax.broadcasted_iota(jnp.int32, (pair, slot_total), 1).astype(F32)
    own_index = jnp.sum(jnp.where(place == slots, lanes, 0.0), axis=1, keepdims=True)

    tail = cols.shape[0] - pair
    far_cols = jnp.concatenate([hub_far, jnp.full((tail - hubs, 1), -5.0, F32)], axis=0)
    far_rows = jnp.concatenate([hub_far, jnp.full((64 - hubs, 1), -5.0, F32)], axis=0)
    cols[0:pair, :] = jnp.where(own_index == colv, 1.0, 0.0).astype(BF16)
    cols[pair:, :] = jnp.where(far_cols == colv, 1.0, 0.0).astype(BF16)
    coded = modes + 1.0
    for index, start, stop in ((own_index, 0, pair), (far_rows, pair, pair + 64)):
        hit = index == rows
        picks[start:stop, :] = jnp.where(hit, weights, 0.0).astype(BF16)
        codes[start:stop, :] = jnp.where(hit, coded, 0.0).astype(BF16)
    weight = lax.dot_general(picks[...], cols[...], NT, preferred_element_type=F32)
    code = lax.dot_general(codes[...], cols[...], NT, preferred_element_type=F32)
    for mode in range(terms):
        table = jnp.where(code == float(mode + 1), weight, 0.0).astype(BF16)
        main_ref[mode] = table[:pair]
        if mode > 0:
            send_ref[mode] = table[pair:, :pair]
    hub_lane = lax.broadcasted_iota(jnp.int32, (pair, cols.shape[0]), 1).astype(F32) - float(pair)
    own_rank = jnp.sum(
        jnp.where(lanes == own_index, rank, 0.0), axis=1, keepdims=True
    )
    main_ref[terms] = jnp.where(
        jnp.logical_and(own_rank >= 0.0, hub_lane == own_rank), 1.0, 0.0
    ).astype(BF16)
    near_rank = lax.broadcasted_iota(jnp.int32, (64, slot_total), 0).astype(F32)
    slot_row = slots
    near_slot = jnp.sum(jnp.where(near_rank == rank, slot_row, 0.0), axis=1, keepdims=True)
    near_has = jnp.sum(jnp.where(near_rank == rank, 1.0, 0.0), axis=1, keepdims=True)
    near_slot = jnp.where(near_has > 0.5, near_slot - base, -5.0)
    send_ref[0] = jnp.where(
        lax.broadcasted_iota(jnp.int32, (64, pair), 1).astype(F32) == near_slot, 1.0, 0.0
    ).astype(BF16)


def edge_kernel(field, near, far, lines, arrived):
    rows = field.shape[1]
    copies = [
        pltpu.make_async_copy(field.at[:, row, :], lines.at[k], arrived.at[k])
        for k, row in enumerate((0, rows - 1))
    ]
    for copy in copies:
        copy.start()
    for copy in copies:
        copy.wait()
    first = core_side() == 0
    near[...] = jnp.where(first, lines[0], lines[1])
    far[...] = jnp.where(first, lines[1], lines[0])


def split_kernel(field, unused, keep, send):
    slots, rows, width = field.shape
    first = core_side() == 0
    for at in range(0, slots, 8):
        lines = jnp.swapaxes(field[at : at + 8], 0, 1)
        for i in range(keep.shape[0]):
            keep[i, at : at + 8, :] = jnp.where(first, lines[i], lines[rows - 1 - i])
            send[i, at : at + 8, :] = jnp.where(first, lines[rows - 1 - i], lines[i])


def five_point(above, center, below):
    width = center.shape[1]
    lane = lax.broadcasted_iota(jnp.int32, center.shape, 1)
    left = jnp.where(lane == 0, 0.0, pltpu.roll(center, 1, 1))
    right = jnp.where(lane == width - 1, 0.0, pltpu.roll(center, width - 1, 1))
    return above + below + left + right - 4.0 * center


def row_place(index, rows):
    return jnp.where(core_side() == 0, index, rows - 1 - index)


def fill_buffer(value_ref, stiff, send_table, buffer, row, place):
    hubs = buffer.shape[1]
    width = buffer.shape[2]
    terms = send_table.shape[0]
    for start in range(0, width, 256):
        cut = slice(start, start + 256)
        value = value_ref[row, :, cut]
        total = jnp.dot(send_table[0], value, preferred_element_type=F32)
        for mode in range(1, terms):
            part = jnp.dot(send_table[mode], value, preferred_element_type=F32)
            total = total + stiff[mode, pl.ds(place, 1), cut] * part
        buffer[row, :, cut] = total[:hubs].astype(BF16)


def first_kernel(first_row, keep, got, *rest):
    halos = rest[:2] if first_row == 0 else None
    stiff, send_table, unused, bent, buffer = rest[-5:]
    side = core_side()
    count, pair, width = bent.shape
    own = keep.shape[1]
    for group in range(2):

        def chunk(k, carry):
            at = pl.multiple_of(k * 8, 8)
            cut = pl.ds(at, 8)
            far = pl.ds(group * own + at, 8)
            lines = [
                jnp.where(side == group, halos[0][cut, :], halos[1][cut, :])
                if row < 0
                else jnp.where(side == group, keep[row, cut, :], got[row, cut, :])
                for row in range(first_row - 1, first_row + count + 1)
            ]
            for row in range(count):
                value = five_point(lines[row], lines[row + 1], lines[row + 2])
                bent[row, far, :] = value.astype(BF16)
            return carry

        lax.fori_loop(0, own // 8, chunk, 0, unroll=3)
    for row in range(count):
        fill_buffer(bent, stiff, send_table, buffer, row, row_place(first_row + row, stiff.shape[1]))


def couple_kernel(first, outer_row, inner_rows, bent, got, stiff, table, unused, moment, *rest):
    stacked = rest[-1]
    edges = list(rest[:-1])
    outer = edges.pop(0) if outer_row is not None else None
    inner = edges.pop(0) if inner_rows else None
    count, pair, width = bent.shape
    hubs = got.shape[1]
    terms = stiff.shape[0]
    room = stacked.shape[0]
    stacked[pair + hubs :, :] = jnp.zeros((room - pair - hubs, width), BF16)
    for row in range(count):
        place = row_place(first + row, stiff.shape[1])
        stacked[0:pair, :] = bent[row]
        stacked[pair : pair + hubs, :] = got[row]
        for start in range(0, width, 256):
            cut = slice(start, start + 256)
            value = stacked[:, cut]
            total = jnp.dot(table[terms], value, preferred_element_type=F32)
            for mode in range(terms):
                part = jnp.dot(table[mode], value, preferred_element_type=F32)
                total = total + stiff[mode, pl.ds(place, 1), cut] * part
            moment[row, :, cut] = total
            if first + row == outer_row:
                outer[0, :, cut] = total.astype(BF16)
            if first + row in inner_rows:
                inner[inner_rows.index(first + row), :, cut] = total.astype(BF16)


def share(held, keep, send, rows, own):
    side = core_side()
    near = pl.multiple_of(side * own, 8)
    far = pl.multiple_of((1 - side) * own, 8)
    for target, row in enumerate(rows):
        keep[target] = held[row, pl.ds(near, own), :]
        send[target] = held[row, pl.ds(far, own), :]


def second_inner_kernel(
    row_zero, row_one, others, inner, stiff, send_table, held, keep, send, bent, buffer
):
    count, pair, width = bent.shape

    def chunk(k, carry):
        cut = pl.ds(pl.multiple_of(k * STEP, STEP), STEP)
        lines = [row_zero[0, cut, :], row_one[0, cut, :]] + [others[row, cut, :] for row in range(2)]
        lines += [inner[row, cut, :].astype(F32) for row in range(2)]
        for row in range(4):
            held[row, cut, :] = five_point(lines[row], lines[row + 1], lines[row + 2])
        for row in range(2):
            value = five_point(
                held[row, cut, :], held[row + 1, cut, :], held[row + 2, cut, :]
            )
            bent[row, cut, :] = value.astype(BF16)
        return carry

    lax.fori_loop(0, pair // STEP, chunk, 0, unroll=3)
    share(held, keep, send, (0, 1, 2), pair // 2)
    for row in range(count):
        fill_buffer(bent, stiff, send_table, buffer, row, row_place(row + 2, stiff.shape[1]))


def second_edge_kernel(
    row_zero, others, near, next_near, held, stiff, send_table, zero, keep, send, bent, buffer
):
    pair = bent.shape[1]
    tile = lax.axis_index("tile")
    last = lax.axis_size("tile") - 1
    at_edge = jnp.where(core_side() == 0, tile == 0, tile == last)

    def chunk(k, carry):
        cut = pl.ds(pl.multiple_of(k * STEP, STEP), STEP)
        above = near[0, cut, :].astype(F32)
        beyond = next_near[0, cut, :].astype(F32)
        here = row_zero[0, cut, :]
        outside = jnp.where(at_edge, 0.0, five_point(beyond, above, here))
        value = five_point(above, here, others[0, cut, :])
        zero[0, cut, :] = value
        bent[0, cut, :] = five_point(outside, value, held[0, cut, :]).astype(BF16)
        return carry

    lax.fori_loop(0, pair // STEP, chunk, 0, unroll=3)
    fill_buffer(bent, stiff, send_table, buffer, 0, row_place(0, stiff.shape[1]))
    share(zero, keep, send, (0,), pair // 2)


def second_next_kernel(zero, held, stiff, send_table, unused, bent, buffer):
    pair = bent.shape[1]

    def chunk(k, carry):
        cut = pl.ds(pl.multiple_of(k * STEP, STEP), STEP)
        value = five_point(zero[0, cut, :], held[0, cut, :], held[1, cut, :])
        bent[0, cut, :] = value.astype(BF16)
        return carry

    lax.fori_loop(0, pair // STEP, chunk, 0, unroll=3)
    fill_buffer(bent, stiff, send_table, buffer, 0, row_place(1, stiff.shape[1]))


def last_kernel(zero, one, inners, inner, keep, send):
    side = core_side()
    count, own, width = keep.shape
    for target, group in ((send, 1 - side), (keep, side)):

        def chunk(k, carry):
            at = pl.multiple_of(k * 8, 8)
            cut = pl.ds(pl.multiple_of(group * own + at, 8), 8)
            lines = [jnp.zeros((8, width), F32), zero[0, cut, :], one[0, cut, :]]
            lines += [inners[row, cut, :] for row in range(2)]
            lines += [inner[0, cut, :].astype(F32)]
            for row in range(count):
                target[row, pl.ds(at, 8), :] = five_point(
                    lines[row], lines[row + 1], lines[row + 2]
                )
            return carry

        lax.fori_loop(0, own // 8, chunk, 0, unroll=3)


def write_tiles(near, far, out, lines, done):
    first = core_side() == 0
    half = out.shape[1] // 2
    step = 24
    copies = []
    for k, at in enumerate(range(0, out.shape[0], step)):
        for start in range(at, at + step, 8):
            ours = [near(i, slice(start, start + 8)) for i in range(half)]
            theirs = [far(i, slice(start, start + 8)) for i in range(half)]
            rows = [jnp.where(first, a, b) for a, b in zip(ours, theirs)]
            rows += [jnp.where(first, b, a) for a, b in zip(ours[::-1], theirs[::-1])]
            lines[start : start + 8] = jnp.swapaxes(jnp.stack(rows, axis=0), 0, 1)
        cut = pl.ds(at, step)
        copies.append(pltpu.make_async_copy(lines.at[cut], out.at[cut], done.at[k]))
        copies[-1].start()
    for copy in copies:
        copy.wait()


def merge_kernel(keep_zero, keep, got_zero, got, unused, out, token, lines, done):
    token[...] = jnp.zeros_like(token)

    def near(i, cut):
        return keep_zero[0, cut, :] if i == 0 else keep[i - 1, cut, :]

    def far(i, cut):
        return got_zero[0, cut, :] if i == 0 else got[i - 1, cut, :]

    write_tiles(near, far, out, lines, done)


def halves(halo, own):
    whole = halo[0].astype(F32)
    first = core_side() == 0
    lower, upper = whole[:own], whole[own:]
    return jnp.where(first, lower, upper), jnp.where(first, upper, lower)


def cut_kernel(halo, unused, part):
    part[...] = halves(halo, part.shape[0])[1].astype(BF16)


def last_merge_kernel(keep, got, halo, far_halo, out, lines, done):
    near_line = halves(halo, keep.shape[1])[0]
    far_line = far_halo[...].astype(F32)

    def near(i, cut):
        return keep[0, cut, :] + near_line[cut] if i == 0 else keep[i, cut, :]

    def far(i, cut):
        return got[0, cut, :] + far_line[cut] if i == 0 else got[i, cut, :]

    write_tiles(near, far, out, lines, done)


def body(slot_field, stiffness, triple_modes, triple_rows, triple_cols, triple_weights, slot_of):
    own, rows, width = slot_field.shape
    terms = stiffness.shape[0]
    pair = 2 * own
    half = rows // 2
    chaos = lax.axis_size("chaos")
    tiles = lax.axis_size("tile")
    slot_total = own * chaos
    modes = terms - 1
    hubs = 1 + modes * (modes + 1) // 2
    room = -(-(pair + hubs) // 16) * 16
    side = core_side()

    core_swap = [(i, i ^ 1) for i in range(chaos)]
    chip_swap = [(i, i ^ 2) for i in range(chaos)]
    tile_swap = []
    for high in range(0, chaos, 2):
        for tile in range(tiles - 1):
            one, two = (high + 1) * tiles + tile, high * tiles + tile + 1
            tile_swap += [(one, two), (two, one)]

    def by_core(value):
        return lax.ppermute(value, "chaos", core_swap)

    def by_chip(value):
        return lax.ppermute(value, "chaos", chip_swap)

    def by_tile(value):
        return lax.ppermute(value, ("chaos", "tile"), tile_swap)

    count = triple_modes.shape[0]
    wide = -(-count // 128) * 128

    def line(value, fill):
        value = value.astype(F32)
        return jnp.pad(value, (0, wide - value.shape[0]), constant_values=fill)

    entries = jnp.stack(
        [
            line(triple_modes, -1.0),
            line(triple_rows, -1.0),
            line(triple_cols, -1.0),
            line(triple_weights, 0.0),
            line(slot_of, -1.0),
        ]
        + [jnp.zeros((wide,), F32)] * 3
    )
    row_block = shape((own, width), F32)
    near_edge, far_edge = call(
        edge_kernel,
        (row_block, row_block),
        [pltpu.VMEM((2, own, width), F32), pltpu.SemaphoreType.DMA((2,))],
        2.0,
        [ANY],
        60,
    )(slot_field)
    halo_far = by_tile(near_edge)
    got_edge = by_core(far_edge)
    halo_near = by_tile(got_edge)

    main_table, send_table = call(
        functools.partial(table_kernel, terms, pair, hubs, slot_total),
        (shape((terms + 1, pair, room), BF16), shape((terms, 64, pair), BF16)),
        [
            pltpu.VMEM((pair + 64, wide), BF16),
            pltpu.VMEM((pair + 64, wide), BF16),
            pltpu.VMEM((room, wide), BF16),
        ],
        3.0,
        [VMEM, ANY],
        12,
    )(entries, got_edge)

    line_block = shape((half + 1, own, width), F32)
    keep, send = call(split_kernel, (line_block, line_block), (), 2.5, [VMEM, ANY])(
        slot_field, got_edge
    )
    got = by_core(send)

    def bents(count):
        return (shape((count, pair, width), BF16), shape((count, hubs, width), BF16))

    def outs(count):
        return (shape((count, own, width), F32),) * 2

    def bend(first, count, after, *halo):
        bent, buffer = call(
            functools.partial(first_kernel, first),
            bents(count),
            (),
            0.9 * count,
            [VMEM] * (4 + len(halo)) + [ANY],
        )(keep, got, *halo, stiffness, send_table, after)
        return bent, buffer, by_chip(buffer)

    def couple(bent, other, first, outer_row, inner_rows, after, weight=1.0):
        count = bent.shape[0]
        out = [shape((count, pair, width), F32)]
        if outer_row is not None:
            out.append(shape((1, pair, width), BF16))
        if inner_rows:
            out.append(shape((len(inner_rows), pair, width), BF16))
        return call(
            functools.partial(couple_kernel, first, outer_row, inner_rows),
            tuple(out),
            [pltpu.VMEM((room, width), BF16)],
            weight * count,
            [VMEM] * 4 + [ANY],
        )(bent, other, stiffness, main_table, after)

    bent_one, sent, cross_one = bend(1, 1, got)
    bent_in, sent, cross_in = bend(2, 2, sent)
    bent_out, sent, cross_out = bend(0, 1, sent, halo_near, halo_far)
    moment_one, edge_one = couple(bent_one, cross_one, 1, 1, (), sent)
    next_near = by_tile(edge_one)
    moment_in, edge_in = couple(bent_in, cross_in, 2, None, (3, 2), edge_one)
    inner = by_core(edge_in)
    moment_out, edge_zero = couple(bent_out, cross_out, 0, 0, (), edge_in)
    near = by_tile(edge_zero)

    held, keep_in, send_in, bent_in, buffer_in = call(
        second_inner_kernel, (shape((4, pair, width), F32),) + outs(3) + bents(2), (), 3.5
    )(moment_out, moment_one, moment_in, inner, stiffness, send_table)
    got_in = by_core(send_in)
    cross_in = by_chip(buffer_in)
    zero, keep_out, send_out, bent_out, buffer_out = call(
        second_edge_kernel,
        (shape((1, pair, width), F32),) + outs(1) + bents(1),
        (),
        0.01,
    )(moment_out, moment_one, near, next_near, held, stiffness, send_table)
    cross_out = by_chip(buffer_out)
    bent_one, buffer_one = call(second_next_kernel, bents(1), (), 0.01, [VMEM] * 4 + [ANY])(
        zero, held, stiffness, send_table, cross_in
    )
    cross_one = by_chip(buffer_one)
    got_out = by_core(send_out)
    moment_out, edge_zero = couple(bent_out, cross_out, 0, 0, (), buffer_one)
    near = by_tile(edge_zero)
    moment_in, inner = couple(bent_in, cross_in, 2, None, (3,), edge_zero)
    inner = by_core(inner)
    (moment_one,) = couple(bent_one, cross_one, 1, None, (), edge_zero)

    keep, send = call(last_kernel, outs(half), (), 2.5)(
        moment_out, moment_one, moment_in, inner
    )
    got = by_core(send)
    whole = shape(slot_field.shape, F32)
    writers = [pltpu.VMEM(slot_field.shape, F32), pltpu.SemaphoreType.DMA((own // 24,))]
    first_apply, token = call(
        merge_kernel, (whole, TOKEN), writers, 1.9, [VMEM] * 4 + [ANY], 6, (ANY, VMEM)
    )(keep_out, keep_in, got_out, got_in, keep)
    far_halo = by_core(
        call(cut_kernel, shape((own, width), BF16), (), 0.3, [VMEM, ANY])(near, token)
    )
    second_apply = call(last_merge_kernel, whole, writers, 1.9, [VMEM] * 4, 6, ANY)(
        keep, got, near, far_halo
    )
    return first_apply, second_apply


def solution(mesh):
    return jax.shard_map(
        body,
        mesh=mesh,
        in_specs=(P("chaos", "tile", None), P(None, "tile", None), P(), P(), P(), P(), P()),
        out_specs=(P("chaos", "tile", None), P("chaos", "tile", None)),
        check_vma=False,
    )
```

```python
import functools
import jax
import jax.numpy as jnp
from jax import lax
from jax.experimental import pallas as pl
from jax.experimental.pallas import tpu as pltpu
from jax.sharding import PartitionSpec as P

F32, BF16 = jnp.float32, jnp.bfloat16
VMEM = pl.BlockSpec(memory_space=pltpu.VMEM)
TOKEN = jax.ShapeDtypeStruct((8, 128), jnp.int32)
ANY = pl.BlockSpec(memory_space=pl.ANY)
NT = (((1,), (1,)), ((), ()))
STEP = 16
EARLY = 0.01


def call(kernel, outs, scratch=(), us=1.0, specs=None, room=12, into=None):
    extra = {} if specs is None else {"in_specs": specs}
    if into is not None:
        extra["out_specs"] = into
    return pl.pallas_call(
        kernel,
        out_shape=outs,
        scratch_shapes=scratch,
        compiler_params=pltpu.CompilerParams(vmem_limit_bytes=room * 1024 * 1024),
        cost_estimate=pl.CostEstimate(
            flops=int(us * 1e10), bytes_accessed=10, transcendentals=0
        ),
        **extra,
    )


def shape(dims, kind):
    return jax.ShapeDtypeStruct(dims, kind)


def core_side():
    return lax.rem(lax.axis_index("chaos"), 2)


def table_kernel(
    terms, pair, hubs, slot_total, entries, unused, main_ref, send_ref, picks, codes, cols
):
    wide = entries.shape[1]
    modes = entries[0:1, :]
    rows = entries[1:2, :]
    colv = entries[2:3, :]
    weights = entries[3:4, :]
    slots = entries[4:5, :slot_total]
    chip = lax.axis_index("chaos") // 2
    base = (chip * pair).astype(F32)

    index_col = lax.broadcasted_iota(jnp.int32, (slot_total, wide), 0).astype(F32)
    row_hot = jnp.where(index_col == rows, 1.0, 0.0).astype(BF16)
    col_hot = jnp.where(index_col == colv, 1.0, 0.0).astype(BF16)
    ones = jnp.ones((8, wide), BF16)
    degree = lax.dot_general(ones, row_hot, NT, preferred_element_type=F32)
    zeroth = jnp.where(degree == float(terms), 1.0, 0.0)
    col_zeroth = lax.dot_general(
        zeroth.astype(BF16), col_hot, (((1,), (0,)), ((), ())), preferred_element_type=F32
    )
    beside = lax.dot_general(col_zeroth.astype(BF16), row_hot, NT, preferred_element_type=F32)
    even = jnp.where(degree > 5.0, jnp.where(beside > 0.5, zeroth, 1.0), 0.0)
    before = jnp.where(
        lax.broadcasted_iota(jnp.int32, (slot_total, slot_total), 0)
        < lax.broadcasted_iota(jnp.int32, (slot_total, slot_total), 1),
        1.0,
        0.0,
    ).astype(BF16)
    rank = lax.dot_general(
        even.astype(BF16), before, (((1,), (0,)), ((), ())), preferred_element_type=F32
    )
    rank = jnp.where(even > 0.5, rank, -1.0)[0:1, :]
    lane_index = lax.broadcasted_iota(jnp.int32, (hubs, slot_total), 1).astype(F32)
    hub_hit = lax.broadcasted_iota(jnp.int32, (hubs, slot_total), 0).astype(F32) == rank
    hub_index = jnp.sum(jnp.where(hub_hit, lane_index, 0.0), axis=1, keepdims=True)
    hub_slot = jnp.sum(jnp.where(hub_hit, slots, 0.0), axis=1, keepdims=True)
    hub_here = jnp.logical_and(hub_slot >= base, hub_slot < base + float(pair))
    hub_far = jnp.where(hub_here, -5.0, hub_index)
    hub_near = jnp.where(hub_here, hub_index, -5.0)

    place = lax.broadcasted_iota(jnp.int32, (pair, slot_total), 0).astype(F32) + base
    lanes = lax.broadcasted_iota(jnp.int32, (pair, slot_total), 1).astype(F32)
    own_index = jnp.sum(jnp.where(place == slots, lanes, 0.0), axis=1, keepdims=True)

    tail = cols.shape[0] - pair
    far_cols = jnp.concatenate([hub_far, jnp.full((tail - hubs, 1), -5.0, F32)], axis=0)
    far_rows = jnp.concatenate([hub_far, jnp.full((64 - hubs, 1), -5.0, F32)], axis=0)
    cols[0:pair, :] = jnp.where(own_index == colv, 1.0, 0.0).astype(BF16)
    cols[pair:, :] = jnp.where(far_cols == colv, 1.0, 0.0).astype(BF16)
    coded = modes + 1.0
    for index, start, stop in ((own_index, 0, pair), (far_rows, pair, pair + 64)):
        hit = index == rows
        picks[start:stop, :] = jnp.where(hit, weights, 0.0).astype(BF16)
        codes[start:stop, :] = jnp.where(hit, coded, 0.0).astype(BF16)
    weight = lax.dot_general(picks[...], cols[...], NT, preferred_element_type=F32)
    code = lax.dot_general(codes[...], cols[...], NT, preferred_element_type=F32)
    for mode in range(terms):
        table = jnp.where(code == float(mode + 1), weight, 0.0).astype(BF16)
        main_ref[mode] = table[:pair]
        if mode > 0:
            send_ref[mode] = table[pair:, :pair]
    hub_lane = lax.broadcasted_iota(jnp.int32, (pair, cols.shape[0]), 1).astype(F32) - float(pair)
    own_rank = jnp.sum(
        jnp.where(lanes == own_index, rank, 0.0), axis=1, keepdims=True
    )
    main_ref[terms] = jnp.where(
        jnp.logical_and(own_rank >= 0.0, hub_lane == own_rank), 1.0, 0.0
    ).astype(BF16)
    near_rank = lax.broadcasted_iota(jnp.int32, (64, slot_total), 0).astype(F32)
    slot_row = slots
    near_slot = jnp.sum(jnp.where(near_rank == rank, slot_row, 0.0), axis=1, keepdims=True)
    near_has = jnp.sum(jnp.where(near_rank == rank, 1.0, 0.0), axis=1, keepdims=True)
    near_slot = jnp.where(near_has > 0.5, near_slot - base, -5.0)
    send_ref[0] = jnp.where(
        lax.broadcasted_iota(jnp.int32, (64, pair), 1).astype(F32) == near_slot, 1.0, 0.0
    ).astype(BF16)


def edge_kernel(field, near, far, lines, arrived):
    rows = field.shape[1]
    copies = [
        pltpu.make_async_copy(field.at[:, row, :], lines.at[k], arrived.at[k])
        for k, row in enumerate((0, rows - 1))
    ]
    for copy in copies:
        copy.start()
    for copy in copies:
        copy.wait()
    first = core_side() == 0
    near[...] = jnp.where(first, lines[0], lines[1])
    far[...] = jnp.where(first, lines[1], lines[0])


def split_kernel(field, unused, keep, send):
    slots, rows, width = field.shape
    first = core_side() == 0
    for at in range(0, slots, 8):
        lines = jnp.swapaxes(field[at : at + 8], 0, 1)
        for i in range(keep.shape[0]):
            keep[i, at : at + 8, :] = jnp.where(first, lines[i], lines[rows - 1 - i])
            send[i, at : at + 8, :] = jnp.where(first, lines[rows - 1 - i], lines[i])


def across(center):
    return five_point(0.0, center, 0.0)


def five_point(above, center, below):
    width = center.shape[1]
    lane = lax.broadcasted_iota(jnp.int32, center.shape, 1)
    left = jnp.where(lane == 0, 0.0, pltpu.roll(center, 1, 1))
    right = jnp.where(lane == width - 1, 0.0, pltpu.roll(center, width - 1, 1))
    return above + below + left + right - 4.0 * center


def row_place(index, rows):
    return jnp.where(core_side() == 0, index, rows - 1 - index)


def fill_buffer(value_ref, stiff, send_table, buffer, row, place):
    hubs = buffer.shape[1]
    width = buffer.shape[2]
    terms = send_table.shape[0]
    for start in range(0, width, 256):
        cut = slice(start, start + 256)
        value = value_ref[row, :, cut]
        total = jnp.dot(send_table[0], value, preferred_element_type=F32)
        for mode in range(1, terms):
            part = jnp.dot(send_table[mode], value, preferred_element_type=F32)
            total = total + stiff[mode, pl.ds(place, 1), cut] * part
        buffer[row, :, cut] = total[:hubs].astype(BF16)


def first_kernel(first_row, keep, got, stiff, send_table, unused, bent, buffer):
    side = core_side()
    count, pair, width = bent.shape
    own = keep.shape[1]
    for group in range(2):

        def chunk(k, carry):
            at = pl.multiple_of(k * 8, 8)
            cut = pl.ds(at, 8)
            far = pl.ds(group * own + at, 8)
            lines = [
                jnp.where(side == group, keep[row, cut, :], got[row, cut, :])
                for row in range(first_row - 1, first_row + count + 1)
            ]
            for row in range(count):
                value = five_point(lines[row], lines[row + 1], lines[row + 2])
                bent[row, far, :] = value.astype(BF16)
            return carry

        lax.fori_loop(0, own // 8, chunk, 0, unroll=3)
    for row in range(count):
        fill_buffer(bent, stiff, send_table, buffer, row, row_place(first_row + row, stiff.shape[1]))


def first_base_kernel(keep, got, unused, base):
    side = core_side()
    own = keep.shape[1]
    for group in range(2):

        def chunk(k, carry):
            at = pl.multiple_of(k * 8, 8)
            cut = pl.ds(at, 8)
            here, below = [
                jnp.where(side == group, keep[row, cut, :], got[row, cut, :]) for row in range(2)
            ]
            base[pl.ds(group * own + at, 8), :] = across(here) + below
            return carry

        lax.fori_loop(0, own // 8, chunk, 0, unroll=3)


def first_outer_kernel(base, halo_near, halo_far, stiff, send_table, unused, bent, buffer):
    first = core_side() == 0
    own = halo_near.shape[0]
    near, far = halo_near[...], halo_far[...]
    halo = jnp.concatenate([jnp.where(first, near, far), jnp.where(first, far, near)], axis=0)
    bent[0] = (base[...] + halo).astype(BF16)
    fill_buffer(bent, stiff, send_table, buffer, 0, row_place(0, stiff.shape[1]))


def pass_kernel(value, unused, out):
    out[...] = value[...]


def couple_kernel(first, outer_row, inner_rows, bent, got, stiff, table, unused, moment, *rest):
    stacked = rest[-1]
    edges = list(rest[:-1])
    outer = edges.pop(0) if outer_row is not None else None
    inner = edges.pop(0) if inner_rows else None
    count, pair, width = bent.shape
    hubs = got.shape[1]
    terms = stiff.shape[0]
    room = stacked.shape[0]
    stacked[pair + hubs :, :] = jnp.zeros((room - pair - hubs, width), BF16)
    for row in range(count):
        place = row_place(first + row, stiff.shape[1])
        stacked[0:pair, :] = bent[row]
        stacked[pair : pair + hubs, :] = got[row]
        for start in range(0, width, 256):
            cut = slice(start, start + 256)
            value = stacked[:, cut]
            total = jnp.dot(table[terms], value, preferred_element_type=F32)
            for mode in range(terms):
                part = jnp.dot(table[mode], value, preferred_element_type=F32)
                total = total + stiff[mode, pl.ds(place, 1), cut] * part
            moment[row, :, cut] = total
            if first + row == outer_row:
                outer[0, :, cut] = total.astype(BF16)
            if first + row in inner_rows:
                inner[inner_rows.index(first + row), :, cut] = total.astype(BF16)


def share(held, keep, send, rows, own):
    side = core_side()
    near = pl.multiple_of(side * own, 8)
    far = pl.multiple_of((1 - side) * own, 8)
    for target, row in enumerate(rows):
        keep[target] = held[row, pl.ds(near, own), :]
        send[target] = held[row, pl.ds(far, own), :]


def second_inner_kernel(
    row_zero, row_one, others, inner, stiff, send_table,
    held, base, ahead, keep, send, bent, buffer,
):
    count, pair, width = bent.shape
    tile = lax.axis_index("tile")
    last = lax.axis_size("tile") - 1
    at_edge = jnp.where(core_side() == 0, tile == 0, tile == last)

    def chunk(k, carry):
        cut = pl.ds(pl.multiple_of(k * STEP, STEP), STEP)
        lines = [row_zero[0, cut, :], row_one[0, cut, :]] + [others[row, cut, :] for row in range(2)]
        lines += [inner[row, cut, :].astype(F32) for row in range(2)]
        for row in range(4):
            held[row, cut, :] = five_point(lines[row], lines[row + 1], lines[row + 2])
        for row in range(2):
            value = five_point(
                held[row, cut, :], held[row + 1, cut, :], held[row + 2, cut, :]
            )
            bent[row, cut, :] = value.astype(BF16)
        partial = across(lines[0]) + lines[1]
        base[0, cut, :] = partial
        outside = jnp.where(at_edge, 0.0, lines[0])
        ahead[0, cut, :] = five_point(outside, partial, held[0, cut, :])
        return carry

    lax.fori_loop(0, pair // STEP, chunk, 0, unroll=3)
    for row in range(count):
        fill_buffer(bent, stiff, send_table, buffer, row, row_place(row + 2, stiff.shape[1]))
    share(held, keep, send, (0, 1, 2), pair // 2)


def second_edge_kernel(base, ahead, near, next_near, stiff, send_table, zero, bent, buffer):
    pair = bent.shape[1]

    def chunk(k, carry):
        cut = pl.ds(pl.multiple_of(k * STEP, STEP), STEP)
        above = near[0, cut, :].astype(F32)
        zero[0, cut, :] = base[0, cut, :] + above
        value = ahead[0, cut, :] + next_near[0, cut, :].astype(F32) + 2.0 * across(above)
        bent[0, cut, :] = value.astype(BF16)
        return carry

    lax.fori_loop(0, pair // STEP, chunk, 0, unroll=3)
    fill_buffer(bent, stiff, send_table, buffer, 0, row_place(0, stiff.shape[1]))


def second_next_kernel(zero, held, stiff, send_table, unused, keep, send, bent, buffer):
    pair = bent.shape[1]

    def chunk(k, carry):
        cut = pl.ds(pl.multiple_of(k * STEP, STEP), STEP)
        value = five_point(zero[0, cut, :], held[0, cut, :], held[1, cut, :])
        bent[0, cut, :] = value.astype(BF16)
        return carry

    lax.fori_loop(0, pair // STEP, chunk, 0, unroll=3)
    fill_buffer(bent, stiff, send_table, buffer, 0, row_place(1, stiff.shape[1]))
    share(zero, keep, send, (0,), pair // 2)


def last_kernel(zero, one, inners, inner, keep, send):
    side = core_side()
    count, own, width = keep.shape
    for target, group in ((send, 1 - side), (keep, side)):

        def chunk(k, carry):
            at = pl.multiple_of(k * 8, 8)
            cut = pl.ds(pl.multiple_of(group * own + at, 8), 8)
            lines = [jnp.zeros((8, width), F32), zero[0, cut, :], one[0, cut, :]]
            lines += [inners[row, cut, :] for row in range(2)]
            lines += [inner[0, cut, :].astype(F32)]
            for row in range(count):
                target[row, pl.ds(at, 8), :] = five_point(
                    lines[row], lines[row + 1], lines[row + 2]
                )
            return carry

        lax.fori_loop(0, own // 8, chunk, 0, unroll=3)


def write_tiles(near, far, out, lines, done):
    first = core_side() == 0
    half = out.shape[1] // 2
    step = 24
    copies = []
    for k, at in enumerate(range(0, out.shape[0], step)):
        for start in range(at, at + step, 8):
            ours = [near(i, slice(start, start + 8)) for i in range(half)]
            theirs = [far(i, slice(start, start + 8)) for i in range(half)]
            rows = [jnp.where(first, a, b) for a, b in zip(ours, theirs)]
            rows += [jnp.where(first, b, a) for a, b in zip(ours[::-1], theirs[::-1])]
            lines[start : start + 8] = jnp.swapaxes(jnp.stack(rows, axis=0), 0, 1)
        cut = pl.ds(at, step)
        copies.append(pltpu.make_async_copy(lines.at[cut], out.at[cut], done.at[k]))
        copies[-1].start()
    for copy in copies:
        copy.wait()


def merge_kernel(keep_zero, keep, got_zero, got, unused, out, token, lines, done):
    token[...] = jnp.zeros_like(token)

    def near(i, cut):
        return keep_zero[0, cut, :] if i == 0 else keep[i - 1, cut, :]

    def far(i, cut):
        return got_zero[0, cut, :] if i == 0 else got[i - 1, cut, :]

    write_tiles(near, far, out, lines, done)


def halves(halo, own):
    whole = halo[0].astype(F32)
    first = core_side() == 0
    lower, upper = whole[:own], whole[own:]
    return jnp.where(first, lower, upper), jnp.where(first, upper, lower)


def cut_kernel(halo, unused, part):
    part[...] = halves(halo, part.shape[0])[1].astype(BF16)


def last_merge_kernel(keep, got, halo, far_halo, out, lines, done):
    near_line = halves(halo, keep.shape[1])[0]
    far_line = far_halo[...].astype(F32)

    def near(i, cut):
        return keep[0, cut, :] + near_line[cut] if i == 0 else keep[i, cut, :]

    def far(i, cut):
        return got[0, cut, :] + far_line[cut] if i == 0 else got[i, cut, :]

    write_tiles(near, far, out, lines, done)


def body(slot_field, stiffness, triple_modes, triple_rows, triple_cols, triple_weights, slot_of):
    own, rows, width = slot_field.shape
    terms = stiffness.shape[0]
    pair = 2 * own
    half = rows // 2
    chaos = lax.axis_size("chaos")
    tiles = lax.axis_size("tile")
    slot_total = own * chaos
    modes = terms - 1
    hubs = 1 + modes * (modes + 1) // 2
    room = -(-(pair + hubs) // 16) * 16
    side = core_side()

    core_swap = [(i, i ^ 1) for i in range(chaos)]
    chip_swap = [(i, i ^ 2) for i in range(chaos)]
    tile_swap = []
    for high in range(0, chaos, 2):
        for tile in range(tiles - 1):
            one, two = (high + 1) * tiles + tile, high * tiles + tile + 1
            tile_swap += [(one, two), (two, one)]

    def by_core(value):
        return lax.ppermute(value, "chaos", core_swap)

    def by_chip(value):
        return lax.ppermute(value, "chaos", chip_swap)

    def by_tile(value):
        return lax.ppermute(value, ("chaos", "tile"), tile_swap)

    count = triple_modes.shape[0]
    wide = -(-count // 128) * 128

    def line(value, fill):
        value = value.astype(F32)
        return jnp.pad(value, (0, wide - value.shape[0]), constant_values=fill)

    entries = jnp.stack(
        [
            line(triple_modes, -1.0),
            line(triple_rows, -1.0),
            line(triple_cols, -1.0),
            line(triple_weights, 0.0),
            line(slot_of, -1.0),
        ]
        + [jnp.zeros((wide,), F32)] * 3
    )
    row_block = shape((own, width), F32)
    near_edge, far_edge = call(
        edge_kernel,
        (row_block, row_block),
        [pltpu.VMEM((2, own, width), F32), pltpu.SemaphoreType.DMA((2,))],
        2.0,
        [ANY],
        60,
    )(slot_field)
    halo_far = by_tile(near_edge)
    got_edge = by_core(far_edge)
    halo_near = by_tile(got_edge)

    main_table, send_table = call(
        functools.partial(table_kernel, terms, pair, hubs, slot_total),
        (shape((terms + 1, pair, room), BF16), shape((terms, 64, pair), BF16)),
        [
            pltpu.VMEM((pair + 64, wide), BF16),
            pltpu.VMEM((pair + 64, wide), BF16),
            pltpu.VMEM((room, wide), BF16),
        ],
        3.0,
        [VMEM, ANY],
        12,
    )(entries, got_edge)

    line_block = shape((half + 1, own, width), F32)
    keep, send = call(split_kernel, (line_block, line_block), (), 2.5, [VMEM, ANY])(
        slot_field, got_edge
    )
    got = by_core(send)

    def bents(count):
        return (shape((count, pair, width), BF16), shape((count, hubs, width), BF16))

    def outs(count):
        return (shape((count, own, width), F32),) * 2

    def bend(first, count, after):
        bent, buffer = call(
            functools.partial(first_kernel, first), bents(count), (), 0.9 * count, [VMEM] * 4 + [ANY]
        )(keep, got, stiffness, send_table, after)
        return bent, buffer, by_chip(buffer)

    def couple(bent, other, first, outer_row, inner_rows, after, weight=1.0):
        count = bent.shape[0]
        out = [shape((count, pair, width), F32)]
        if outer_row is not None:
            out.append(shape((1, pair, width), BF16))
        if inner_rows:
            out.append(shape((len(inner_rows), pair, width), BF16))
        return call(
            functools.partial(couple_kernel, first, outer_row, inner_rows),
            tuple(out),
            [pltpu.VMEM((room, width), BF16)],
            weight * count,
            [VMEM] * 4 + [ANY],
        )(bent, other, stiffness, main_table, after)

    bent_one, sent, cross_one = bend(1, 1, got)
    bent_in, sent, cross_in = bend(2, 2, sent)
    base = call(first_base_kernel, shape((pair, width), F32), (), 0.4, [VMEM] * 2 + [ANY])(
        keep, got, sent
    )
    moment_one, edge_one = couple(bent_one, cross_one, 1, 1, (), base)
    bent_out, sent = call(first_outer_kernel, bents(1), (), 0.9, [VMEM] * 5 + [ANY])(
        base, halo_near, halo_far, stiffness, send_table, edge_one
    )
    cross_out = by_chip(sent)
    edge_one = call(pass_kernel, shape(edge_one.shape, BF16), (), 0.1, [VMEM, ANY])(edge_one, sent)
    next_near = by_tile(edge_one)
    moment_in, edge_in = couple(bent_in, cross_in, 2, None, (3, 2), edge_one)
    inner = by_core(edge_in)
    moment_out, edge_zero = couple(bent_out, cross_out, 0, 0, (), edge_in)
    near = by_tile(edge_zero)

    row_shape = shape((1, pair, width), F32)
    held, base, ahead, keep_in, send_in, bent_in, buffer_in = call(
        second_inner_kernel,
        (shape((4, pair, width), F32), row_shape, row_shape) + outs(3) + bents(2),
        (),
        3.5,
    )(moment_out, moment_one, moment_in, inner, stiffness, send_table)
    got_in = by_core(send_in)
    cross_in = by_chip(buffer_in)
    zero, bent_out, buffer_out = call(second_edge_kernel, (row_shape,) + bents(1), (), EARLY)(
        base, ahead, near, next_near, stiffness, send_table
    )
    cross_out = by_chip(buffer_out)
    keep_out, send_out, bent_one, buffer_one = call(
        second_next_kernel, outs(1) + bents(1), (), EARLY, [VMEM] * 4 + [ANY]
    )(zero, held, stiffness, send_table, cross_in)
    cross_one = by_chip(buffer_one)
    got_out = by_core(send_out)
    moment_out, edge_zero = couple(bent_out, cross_out, 0, 0, (), buffer_one)
    near = by_tile(edge_zero)
    moment_in, inner = couple(bent_in, cross_in, 2, None, (3,), edge_zero)
    inner = by_core(inner)
    (moment_one,) = couple(bent_one, cross_one, 1, None, (), edge_zero)

    keep, send = call(last_kernel, outs(half), (), 2.5)(
        moment_out, moment_one, moment_in, inner
    )
    got = by_core(send)
    whole = shape(slot_field.shape, F32)
    writers = [pltpu.VMEM(slot_field.shape, F32), pltpu.SemaphoreType.DMA((own // 24,))]
    first_apply, token = call(
        merge_kernel, (whole, TOKEN), writers, 1.9, [VMEM] * 4 + [ANY], 6, (ANY, VMEM)
    )(keep_out, keep_in, got_out, got_in, keep)
    far_halo = by_core(
        call(cut_kernel, shape((own, width), BF16), (), 0.3, [VMEM, ANY])(near, token)
    )
    second_apply = call(last_merge_kernel, whole, writers, 1.9, [VMEM] * 4, 6, ANY)(
        keep, got, near, far_halo
    )
    return first_apply, second_apply


def solution(mesh):
    return jax.shard_map(
        body,
        mesh=mesh,
        in_specs=(P("chaos", "tile", None), P(None, "tile", None), P(), P(), P(), P(), P()),
        out_specs=(P("chaos", "tile", None), P("chaos", "tile", None)),
        check_vma=False,
    )
```

```python
import functools
import jax
import jax.numpy as jnp
from jax import lax
from jax.experimental import pallas as pl
from jax.experimental.pallas import tpu as pltpu
from jax.sharding import PartitionSpec as P

F32, BF16 = jnp.float32, jnp.bfloat16
VMEM = pl.BlockSpec(memory_space=pltpu.VMEM)
TOKEN = jax.ShapeDtypeStruct((8, 128), jnp.int32)
ANY = pl.BlockSpec(memory_space=pl.ANY)
NT = (((1,), (1,)), ((), ()))
STEP = 16
EARLY = 0.01


def call(kernel, outs, scratch=(), us=1.0, specs=None, room=12, into=None):
    extra = {} if specs is None else {"in_specs": specs}
    if into is not None:
        extra["out_specs"] = into
    return pl.pallas_call(
        kernel,
        out_shape=outs,
        scratch_shapes=scratch,
        compiler_params=pltpu.CompilerParams(vmem_limit_bytes=room * 1024 * 1024),
        cost_estimate=pl.CostEstimate(
            flops=int(us * 1e10), bytes_accessed=10, transcendentals=0
        ),
        **extra,
    )


def shape(dims, kind):
    return jax.ShapeDtypeStruct(dims, kind)


def core_side():
    return lax.rem(lax.axis_index("chaos"), 2)


def table_kernel(
    terms, pair, hubs, slot_total, entries, unused, main_ref, send_ref, picks, codes, cols
):
    wide = entries.shape[1]
    modes = entries[0:1, :]
    rows = entries[1:2, :]
    colv = entries[2:3, :]
    weights = entries[3:4, :]
    slots = entries[4:5, :slot_total]
    chip = lax.axis_index("chaos") // 2
    base = (chip * pair).astype(F32)

    index_col = lax.broadcasted_iota(jnp.int32, (slot_total, wide), 0).astype(F32)
    row_hot = jnp.where(index_col == rows, 1.0, 0.0).astype(BF16)
    col_hot = jnp.where(index_col == colv, 1.0, 0.0).astype(BF16)
    ones = jnp.ones((8, wide), BF16)
    degree = lax.dot_general(ones, row_hot, NT, preferred_element_type=F32)
    zeroth = jnp.where(degree == float(terms), 1.0, 0.0)
    col_zeroth = lax.dot_general(
        zeroth.astype(BF16), col_hot, (((1,), (0,)), ((), ())), preferred_element_type=F32
    )
    beside = lax.dot_general(col_zeroth.astype(BF16), row_hot, NT, preferred_element_type=F32)
    even = jnp.where(degree > 5.0, jnp.where(beside > 0.5, zeroth, 1.0), 0.0)
    before = jnp.where(
        lax.broadcasted_iota(jnp.int32, (slot_total, slot_total), 0)
        < lax.broadcasted_iota(jnp.int32, (slot_total, slot_total), 1),
        1.0,
        0.0,
    ).astype(BF16)
    rank = lax.dot_general(
        even.astype(BF16), before, (((1,), (0,)), ((), ())), preferred_element_type=F32
    )
    rank = jnp.where(even > 0.5, rank, -1.0)[0:1, :]
    lane_index = lax.broadcasted_iota(jnp.int32, (hubs, slot_total), 1).astype(F32)
    hub_hit = lax.broadcasted_iota(jnp.int32, (hubs, slot_total), 0).astype(F32) == rank
    hub_index = jnp.sum(jnp.where(hub_hit, lane_index, 0.0), axis=1, keepdims=True)
    hub_slot = jnp.sum(jnp.where(hub_hit, slots, 0.0), axis=1, keepdims=True)
    hub_here = jnp.logical_and(hub_slot >= base, hub_slot < base + float(pair))
    hub_far = jnp.where(hub_here, -5.0, hub_index)
    hub_near = jnp.where(hub_here, hub_index, -5.0)

    place = lax.broadcasted_iota(jnp.int32, (pair, slot_total), 0).astype(F32) + base
    lanes = lax.broadcasted_iota(jnp.int32, (pair, slot_total), 1).astype(F32)
    own_index = jnp.sum(jnp.where(place == slots, lanes, 0.0), axis=1, keepdims=True)

    tail = cols.shape[0] - pair
    far_cols = jnp.concatenate([hub_far, jnp.full((tail - hubs, 1), -5.0, F32)], axis=0)
    far_rows = jnp.concatenate([hub_far, jnp.full((64 - hubs, 1), -5.0, F32)], axis=0)
    cols[0:pair, :] = jnp.where(own_index == colv, 1.0, 0.0).astype(BF16)
    cols[pair:, :] = jnp.where(far_cols == colv, 1.0, 0.0).astype(BF16)
    coded = modes + 1.0
    for index, start, stop in ((own_index, 0, pair), (far_rows, pair, pair + 64)):
        hit = index == rows
        picks[start:stop, :] = jnp.where(hit, weights, 0.0).astype(BF16)
        codes[start:stop, :] = jnp.where(hit, coded, 0.0).astype(BF16)
    weight = lax.dot_general(picks[...], cols[...], NT, preferred_element_type=F32)
    code = lax.dot_general(codes[...], cols[...], NT, preferred_element_type=F32)
    for mode in range(terms):
        table = jnp.where(code == float(mode + 1), weight, 0.0).astype(BF16)
        main_ref[mode] = table[:pair]
        if mode > 0:
            send_ref[mode] = table[pair:, :pair]
    hub_lane = lax.broadcasted_iota(jnp.int32, (pair, cols.shape[0]), 1).astype(F32) - float(pair)
    own_rank = jnp.sum(
        jnp.where(lanes == own_index, rank, 0.0), axis=1, keepdims=True
    )
    main_ref[terms] = jnp.where(
        jnp.logical_and(own_rank >= 0.0, hub_lane == own_rank), 1.0, 0.0
    ).astype(BF16)
    near_rank = lax.broadcasted_iota(jnp.int32, (64, slot_total), 0).astype(F32)
    slot_row = slots
    near_slot = jnp.sum(jnp.where(near_rank == rank, slot_row, 0.0), axis=1, keepdims=True)
    near_has = jnp.sum(jnp.where(near_rank == rank, 1.0, 0.0), axis=1, keepdims=True)
    near_slot = jnp.where(near_has > 0.5, near_slot - base, -5.0)
    send_ref[0] = jnp.where(
        lax.broadcasted_iota(jnp.int32, (64, pair), 1).astype(F32) == near_slot, 1.0, 0.0
    ).astype(BF16)


def edge_kernel(field, near, far, lines, arrived):
    rows = field.shape[1]
    copies = [
        pltpu.make_async_copy(field.at[:, row, :], lines.at[k], arrived.at[k])
        for k, row in enumerate((0, rows - 1))
    ]
    for copy in copies:
        copy.start()
    for copy in copies:
        copy.wait()
    first = core_side() == 0
    near[...] = jnp.where(first, lines[0], lines[1])
    far[...] = jnp.where(first, lines[1], lines[0])


def split_kernel(field, unused, keep, send):
    slots, rows, width = field.shape
    first = core_side() == 0
    for at in range(0, slots, 8):
        lines = jnp.swapaxes(field[at : at + 8], 0, 1)
        for i in range(keep.shape[0]):
            keep[i, at : at + 8, :] = jnp.where(first, lines[i], lines[rows - 1 - i])
            send[i, at : at + 8, :] = jnp.where(first, lines[rows - 1 - i], lines[i])


def across(center):
    return five_point(0.0, center, 0.0)


def five_point(above, center, below):
    width = center.shape[1]
    lane = lax.broadcasted_iota(jnp.int32, center.shape, 1)
    left = jnp.where(lane == 0, 0.0, pltpu.roll(center, 1, 1))
    right = jnp.where(lane == width - 1, 0.0, pltpu.roll(center, width - 1, 1))
    return above + below + left + right - 4.0 * center


def row_place(index, rows):
    return jnp.where(core_side() == 0, index, rows - 1 - index)


def fill_buffer(value_ref, stiff, send_table, buffer, row, place):
    hubs = buffer.shape[1]
    width = buffer.shape[2]
    terms = send_table.shape[0]
    for start in range(0, width, 256):
        cut = slice(start, start + 256)
        value = value_ref[row, :, cut]
        total = jnp.dot(send_table[0], value, preferred_element_type=F32)
        for mode in range(1, terms):
            part = jnp.dot(send_table[mode], value, preferred_element_type=F32)
            total = total + stiff[mode, pl.ds(place, 1), cut] * part
        buffer[row, :, cut] = total[:hubs].astype(BF16)


def first_kernel(first_row, keep, got, stiff, send_table, unused, bent, buffer):
    side = core_side()
    count, pair, width = bent.shape
    own = keep.shape[1]
    for group in range(2):

        def chunk(k, carry):
            at = pl.multiple_of(k * 8, 8)
            cut = pl.ds(at, 8)
            far = pl.ds(group * own + at, 8)
            lines = [
                jnp.where(side == group, keep[row, cut, :], got[row, cut, :])
                for row in range(first_row - 1, first_row + count + 1)
            ]
            for row in range(count):
                value = five_point(lines[row], lines[row + 1], lines[row + 2])
                bent[row, far, :] = value.astype(BF16)
            return carry

        lax.fori_loop(0, own // 8, chunk, 0, unroll=3)
    for row in range(count):
        fill_buffer(bent, stiff, send_table, buffer, row, row_place(first_row + row, stiff.shape[1]))


def first_base_kernel(keep, got, unused, base):
    side = core_side()
    own = keep.shape[1]
    for group in range(2):

        def chunk(k, carry):
            at = pl.multiple_of(k * 8, 8)
            cut = pl.ds(at, 8)
            here, below = [
                jnp.where(side == group, keep[row, cut, :], got[row, cut, :]) for row in range(2)
            ]
            base[pl.ds(group * own + at, 8), :] = across(here) + below
            return carry

        lax.fori_loop(0, own // 8, chunk, 0, unroll=3)


def first_outer_kernel(base, halo_near, halo_far, stiff, send_table, unused, bent, buffer):
    first = core_side() == 0
    own = halo_near.shape[0]
    near, far = halo_near[...], halo_far[...]
    halo = jnp.concatenate([jnp.where(first, near, far), jnp.where(first, far, near)], axis=0)
    bent[0] = (base[...] + halo).astype(BF16)
    fill_buffer(bent, stiff, send_table, buffer, 0, row_place(0, stiff.shape[1]))


def pass_kernel(value, unused, out):
    out[...] = value[...]


def couple_kernel(first, outer_row, inner_rows, bent, got, stiff, table, unused, moment, *rest):
    stacked = rest[-1]
    edges = list(rest[:-1])
    outer = edges.pop(0) if outer_row is not None else None
    inner = edges.pop(0) if inner_rows else None
    count, pair, width = bent.shape
    hubs = got.shape[1]
    terms = stiff.shape[0]
    room = stacked.shape[0]
    stacked[pair + hubs :, :] = jnp.zeros((room - pair - hubs, width), BF16)
    for row in range(count):
        place = row_place(first + row, stiff.shape[1])
        stacked[0:pair, :] = bent[row]
        stacked[pair : pair + hubs, :] = got[row]
        for start in range(0, width, 256):
            cut = slice(start, start + 256)
            value = stacked[:, cut]
            total = jnp.dot(table[terms], value, preferred_element_type=F32)
            for mode in range(terms):
                part = jnp.dot(table[mode], value, preferred_element_type=F32)
                total = total + stiff[mode, pl.ds(place, 1), cut] * part
            moment[row, :, cut] = total
            if first + row == outer_row:
                outer[0, :, cut] = total.astype(BF16)
            if first + row in inner_rows:
                inner[inner_rows.index(first + row), :, cut] = total.astype(BF16)


def share(held, keep, send, rows, own):
    side = core_side()
    near = pl.multiple_of(side * own, 8)
    far = pl.multiple_of((1 - side) * own, 8)
    for target, row in enumerate(rows):
        keep[target] = held[row, pl.ds(near, own), :]
        send[target] = held[row, pl.ds(far, own), :]


def second_inner_kernel(row_zero, row_one, others, inner, stiff, send_table, held, bent, buffer):
    count, pair, width = bent.shape

    def chunk(k, carry):
        cut = pl.ds(pl.multiple_of(k * STEP, STEP), STEP)
        lines = [row_zero[0, cut, :], row_one[0, cut, :]] + [others[row, cut, :] for row in range(2)]
        lines += [inner[row, cut, :].astype(F32) for row in range(2)]
        for row in range(4):
            held[row, cut, :] = five_point(lines[row], lines[row + 1], lines[row + 2])
        for row in range(2):
            value = five_point(
                held[row, cut, :], held[row + 1, cut, :], held[row + 2, cut, :]
            )
            bent[row, cut, :] = value.astype(BF16)
        return carry

    lax.fori_loop(0, pair // STEP, chunk, 0, unroll=3)
    for row in range(count):
        fill_buffer(bent, stiff, send_table, buffer, row, row_place(row + 2, stiff.shape[1]))


def second_base_kernel(row_zero, row_one, held, base, ahead, keep, send):
    pair = row_zero.shape[1]
    tile = lax.axis_index("tile")
    last = lax.axis_size("tile") - 1
    at_edge = jnp.where(core_side() == 0, tile == 0, tile == last)

    def chunk(k, carry):
        cut = pl.ds(pl.multiple_of(k * STEP, STEP), STEP)
        here = row_zero[0, cut, :]
        partial = across(here) + row_one[0, cut, :]
        base[0, cut, :] = partial
        outside = jnp.where(at_edge, 0.0, here)
        ahead[0, cut, :] = five_point(outside, partial, held[0, cut, :])
        return carry

    lax.fori_loop(0, pair // STEP, chunk, 0, unroll=3)
    share(held, keep, send, (0, 1, 2), pair // 2)


def second_edge_kernel(base, ahead, near, next_near, stiff, send_table, zero, bent, buffer):
    pair = bent.shape[1]

    def chunk(k, carry):
        cut = pl.ds(pl.multiple_of(k * STEP, STEP), STEP)
        above = near[0, cut, :].astype(F32)
        zero[0, cut, :] = base[0, cut, :] + above
        value = ahead[0, cut, :] + next_near[0, cut, :].astype(F32) + 2.0 * across(above)
        bent[0, cut, :] = value.astype(BF16)
        return carry

    lax.fori_loop(0, pair // STEP, chunk, 0, unroll=3)
    fill_buffer(bent, stiff, send_table, buffer, 0, row_place(0, stiff.shape[1]))


def second_next_kernel(zero, held, stiff, send_table, unused, keep, send, bent, buffer):
    pair = bent.shape[1]

    def chunk(k, carry):
        cut = pl.ds(pl.multiple_of(k * STEP, STEP), STEP)
        value = five_point(zero[0, cut, :], held[0, cut, :], held[1, cut, :])
        bent[0, cut, :] = value.astype(BF16)
        return carry

    lax.fori_loop(0, pair // STEP, chunk, 0, unroll=3)
    fill_buffer(bent, stiff, send_table, buffer, 0, row_place(1, stiff.shape[1]))
    share(zero, keep, send, (0,), pair // 2)


def last_kernel(zero, one, inners, inner, keep, send):
    side = core_side()
    count, own, width = keep.shape
    for target, group in ((send, 1 - side), (keep, side)):

        def chunk(k, carry):
            at = pl.multiple_of(k * 8, 8)
            cut = pl.ds(pl.multiple_of(group * own + at, 8), 8)
            lines = [jnp.zeros((8, width), F32), zero[0, cut, :], one[0, cut, :]]
            lines += [inners[row, cut, :] for row in range(2)]
            lines += [inner[0, cut, :].astype(F32)]
            for row in range(count):
                target[row, pl.ds(at, 8), :] = five_point(
                    lines[row], lines[row + 1], lines[row + 2]
                )
            return carry

        lax.fori_loop(0, own // 8, chunk, 0, unroll=3)


def write_tiles(near, far, out, lines, done):
    first = core_side() == 0
    half = out.shape[1] // 2
    step = 24
    copies = []
    for k, at in enumerate(range(0, out.shape[0], step)):
        for start in range(at, at + step, 8):
            ours = [near(i, slice(start, start + 8)) for i in range(half)]
            theirs = [far(i, slice(start, start + 8)) for i in range(half)]
            rows = [jnp.where(first, a, b) for a, b in zip(ours, theirs)]
            rows += [jnp.where(first, b, a) for a, b in zip(ours[::-1], theirs[::-1])]
            lines[start : start + 8] = jnp.swapaxes(jnp.stack(rows, axis=0), 0, 1)
        cut = pl.ds(at, step)
        copies.append(pltpu.make_async_copy(lines.at[cut], out.at[cut], done.at[k]))
        copies[-1].start()
    for copy in copies:
        copy.wait()


def merge_kernel(keep_zero, keep, got_zero, got, unused, out, token, lines, done):
    token[...] = jnp.zeros_like(token)

    def near(i, cut):
        return keep_zero[0, cut, :] if i == 0 else keep[i - 1, cut, :]

    def far(i, cut):
        return got_zero[0, cut, :] if i == 0 else got[i - 1, cut, :]

    write_tiles(near, far, out, lines, done)


def halves(halo, own):
    whole = halo[0].astype(F32)
    first = core_side() == 0
    lower, upper = whole[:own], whole[own:]
    return jnp.where(first, lower, upper), jnp.where(first, upper, lower)


def cut_kernel(halo, unused, part):
    part[...] = halves(halo, part.shape[0])[1].astype(BF16)


def last_merge_kernel(keep, got, halo, far_halo, out, lines, done):
    near_line = halves(halo, keep.shape[1])[0]
    far_line = far_halo[...].astype(F32)

    def near(i, cut):
        return keep[0, cut, :] + near_line[cut] if i == 0 else keep[i, cut, :]

    def far(i, cut):
        return got[0, cut, :] + far_line[cut] if i == 0 else got[i, cut, :]

    write_tiles(near, far, out, lines, done)


def body(slot_field, stiffness, triple_modes, triple_rows, triple_cols, triple_weights, slot_of):
    own, rows, width = slot_field.shape
    terms = stiffness.shape[0]
    pair = 2 * own
    half = rows // 2
    chaos = lax.axis_size("chaos")
    tiles = lax.axis_size("tile")
    slot_total = own * chaos
    modes = terms - 1
    hubs = 1 + modes * (modes + 1) // 2
    room = -(-(pair + hubs) // 16) * 16
    side = core_side()

    core_swap = [(i, i ^ 1) for i in range(chaos)]
    chip_swap = [(i, i ^ 2) for i in range(chaos)]
    tile_swap = []
    for high in range(0, chaos, 2):
        for tile in range(tiles - 1):
            one, two = (high + 1) * tiles + tile, high * tiles + tile + 1
            tile_swap += [(one, two), (two, one)]

    def by_core(value):
        return lax.ppermute(value, "chaos", core_swap)

    def by_chip(value):
        return lax.ppermute(value, "chaos", chip_swap)

    def by_tile(value):
        return lax.ppermute(value, ("chaos", "tile"), tile_swap)

    count = triple_modes.shape[0]
    wide = -(-count // 128) * 128

    def line(value, fill):
        value = value.astype(F32)
        return jnp.pad(value, (0, wide - value.shape[0]), constant_values=fill)

    entries = jnp.stack(
        [
            line(triple_modes, -1.0),
            line(triple_rows, -1.0),
            line(triple_cols, -1.0),
            line(triple_weights, 0.0),
            line(slot_of, -1.0),
        ]
        + [jnp.zeros((wide,), F32)] * 3
    )
    row_block = shape((own, width), F32)
    near_edge, far_edge = call(
        edge_kernel,
        (row_block, row_block),
        [pltpu.VMEM((2, own, width), F32), pltpu.SemaphoreType.DMA((2,))],
        2.0,
        [ANY],
        60,
    )(slot_field)
    halo_far = by_tile(near_edge)
    got_edge = by_core(far_edge)
    halo_near = by_tile(got_edge)

    main_table, send_table = call(
        functools.partial(table_kernel, terms, pair, hubs, slot_total),
        (shape((terms + 1, pair, room), BF16), shape((terms, 64, pair), BF16)),
        [
            pltpu.VMEM((pair + 64, wide), BF16),
            pltpu.VMEM((pair + 64, wide), BF16),
            pltpu.VMEM((room, wide), BF16),
        ],
        3.0,
        [VMEM, ANY],
        12,
    )(entries, got_edge)

    line_block = shape((half + 1, own, width), F32)
    keep, send = call(split_kernel, (line_block, line_block), (), 2.5, [VMEM, ANY])(
        slot_field, got_edge
    )
    got = by_core(send)

    def bents(count):
        return (shape((count, pair, width), BF16), shape((count, hubs, width), BF16))

    def outs(count):
        return (shape((count, own, width), F32),) * 2

    def bend(first, count, after):
        bent, buffer = call(
            functools.partial(first_kernel, first), bents(count), (), 0.9 * count, [VMEM] * 4 + [ANY]
        )(keep, got, stiffness, send_table, after)
        return bent, buffer, by_chip(buffer)

    def couple(bent, other, first, outer_row, inner_rows, after, weight=1.0):
        count = bent.shape[0]
        out = [shape((count, pair, width), F32)]
        if outer_row is not None:
            out.append(shape((1, pair, width), BF16))
        if inner_rows:
            out.append(shape((len(inner_rows), pair, width), BF16))
        return call(
            functools.partial(couple_kernel, first, outer_row, inner_rows),
            tuple(out),
            [pltpu.VMEM((room, width), BF16)],
            weight * count,
            [VMEM] * 4 + [ANY],
        )(bent, other, stiffness, main_table, after)

    bent_one, sent, cross_one = bend(1, 1, got)
    bent_in, sent, cross_in = bend(2, 2, sent)
    base = call(first_base_kernel, shape((pair, width), F32), (), 0.4, [VMEM] * 2 + [ANY])(
        keep, got, sent
    )
    moment_one, edge_one = couple(bent_one, cross_one, 1, 1, (), base)
    bent_out, sent = call(first_outer_kernel, bents(1), (), 0.9, [VMEM] * 5 + [ANY])(
        base, halo_near, halo_far, stiffness, send_table, edge_one
    )
    cross_out = by_chip(sent)
    edge_one = call(pass_kernel, shape(edge_one.shape, BF16), (), 0.1, [VMEM, ANY])(edge_one, sent)
    next_near = by_tile(edge_one)
    moment_in, edge_in = couple(bent_in, cross_in, 2, None, (3, 2), edge_one)
    inner = by_core(edge_in)
    moment_out, edge_zero = couple(bent_out, cross_out, 0, 0, (), edge_in)
    near = by_tile(edge_zero)

    row_shape = shape((1, pair, width), F32)
    held, bent_in, buffer_in = call(
        second_inner_kernel, (shape((4, pair, width), F32),) + bents(2), (), 2.7
    )(moment_out, moment_one, moment_in, inner, stiffness, send_table)
    base, ahead, keep_in, send_in = call(
        second_base_kernel, (row_shape, row_shape) + outs(3), (), 3.0
    )(moment_out, moment_one, held)
    got_in = by_core(send_in)
    cross_in = by_chip(buffer_in)
    zero, bent_out, buffer_out = call(second_edge_kernel, (row_shape,) + bents(1), (), EARLY)(
        base, ahead, near, next_near, stiffness, send_table
    )
    cross_out = by_chip(buffer_out)
    keep_out, send_out, bent_one, buffer_one = call(
        second_next_kernel, outs(1) + bents(1), (), EARLY, [VMEM] * 4 + [ANY]
    )(zero, held, stiffness, send_table, cross_in)
    cross_one = by_chip(buffer_one)
    got_out = by_core(send_out)
    moment_out, edge_zero = couple(bent_out, cross_out, 0, 0, (), buffer_one)
    near = by_tile(edge_zero)
    moment_in, inner = couple(bent_in, cross_in, 2, None, (3,), edge_zero)
    inner = by_core(inner)
    (moment_one,) = couple(bent_one, cross_one, 1, None, (), edge_zero)

    keep, send = call(last_kernel, outs(half), (), 2.5)(
        moment_out, moment_one, moment_in, inner
    )
    got = by_core(send)
    whole = shape(slot_field.shape, F32)
    writers = [pltpu.VMEM(slot_field.shape, F32), pltpu.SemaphoreType.DMA((own // 24,))]
    first_apply, token = call(
        merge_kernel, (whole, TOKEN), writers, 1.9, [VMEM] * 4 + [ANY], 6, (ANY, VMEM)
    )(keep_out, keep_in, got_out, got_in, keep)
    far_halo = by_core(
        call(cut_kernel, shape((own, width), BF16), (), 0.3, [VMEM, ANY])(near, token)
    )
    second_apply = call(last_merge_kernel, whole, writers, 1.9, [VMEM] * 4, 6, ANY)(
        keep, got, near, far_halo
    )
    return first_apply, second_apply


def solution(mesh):
    return jax.shard_map(
        body,
        mesh=mesh,
        in_specs=(P("chaos", "tile", None), P(None, "tile", None), P(), P(), P(), P(), P()),
        out_specs=(P("chaos", "tile", None), P("chaos", "tile", None)),
        check_vma=False,
    )
```

```python
import functools
import jax
import jax.numpy as jnp
from jax import lax
from jax.experimental import pallas as pl
from jax.experimental.pallas import tpu as pltpu
from jax.sharding import PartitionSpec as P

F32, BF16 = jnp.float32, jnp.bfloat16
VMEM = pl.BlockSpec(memory_space=pltpu.VMEM)
TOKEN = jax.ShapeDtypeStruct((8, 128), jnp.int32)
ANY = pl.BlockSpec(memory_space=pl.ANY)
NT = (((1,), (1,)), ((), ()))
STEP = 16
CHUNK = 8
EARLY = 0.01


def call(kernel, outs, scratch=(), us=1.0, specs=None, room=12, into=None):
    extra = {} if specs is None else {"in_specs": specs}
    if into is not None:
        extra["out_specs"] = into
    return pl.pallas_call(
        kernel,
        out_shape=outs,
        scratch_shapes=scratch,
        compiler_params=pltpu.CompilerParams(vmem_limit_bytes=room * 1024 * 1024),
        cost_estimate=pl.CostEstimate(
            flops=int(us * 1e10), bytes_accessed=10, transcendentals=0
        ),
        **extra,
    )


def shape(dims, kind):
    return jax.ShapeDtypeStruct(dims, kind)


def core_side():
    return lax.rem(lax.axis_index("chaos"), 2)


def table_kernel(
    terms, pair, hubs, slot_total, entries, unused, main_ref, send_ref, picks, codes, cols
):
    wide = entries.shape[1]
    modes = entries[0:1, :]
    rows = entries[1:2, :]
    colv = entries[2:3, :]
    weights = entries[3:4, :]
    slots = entries[4:5, :slot_total]
    chip = lax.axis_index("chaos") // 2
    base = (chip * pair).astype(F32)

    index_col = lax.broadcasted_iota(jnp.int32, (slot_total, wide), 0).astype(F32)
    row_hot = jnp.where(index_col == rows, 1.0, 0.0).astype(BF16)
    col_hot = jnp.where(index_col == colv, 1.0, 0.0).astype(BF16)
    ones = jnp.ones((8, wide), BF16)
    degree = lax.dot_general(ones, row_hot, NT, preferred_element_type=F32)
    zeroth = jnp.where(degree == float(terms), 1.0, 0.0)
    col_zeroth = lax.dot_general(
        zeroth.astype(BF16), col_hot, (((1,), (0,)), ((), ())), preferred_element_type=F32
    )
    beside = lax.dot_general(col_zeroth.astype(BF16), row_hot, NT, preferred_element_type=F32)
    even = jnp.where(degree > 5.0, jnp.where(beside > 0.5, zeroth, 1.0), 0.0)
    before = jnp.where(
        lax.broadcasted_iota(jnp.int32, (slot_total, slot_total), 0)
        < lax.broadcasted_iota(jnp.int32, (slot_total, slot_total), 1),
        1.0,
        0.0,
    ).astype(BF16)
    rank = lax.dot_general(
        even.astype(BF16), before, (((1,), (0,)), ((), ())), preferred_element_type=F32
    )
    rank = jnp.where(even > 0.5, rank, -1.0)[0:1, :]
    lane_index = lax.broadcasted_iota(jnp.int32, (hubs, slot_total), 1).astype(F32)
    hub_hit = lax.broadcasted_iota(jnp.int32, (hubs, slot_total), 0).astype(F32) == rank
    hub_index = jnp.sum(jnp.where(hub_hit, lane_index, 0.0), axis=1, keepdims=True)
    hub_slot = jnp.sum(jnp.where(hub_hit, slots, 0.0), axis=1, keepdims=True)
    hub_here = jnp.logical_and(hub_slot >= base, hub_slot < base + float(pair))
    hub_far = jnp.where(hub_here, -5.0, hub_index)
    hub_near = jnp.where(hub_here, hub_index, -5.0)

    place = lax.broadcasted_iota(jnp.int32, (pair, slot_total), 0).astype(F32) + base
    lanes = lax.broadcasted_iota(jnp.int32, (pair, slot_total), 1).astype(F32)
    own_index = jnp.sum(jnp.where(place == slots, lanes, 0.0), axis=1, keepdims=True)

    tail = cols.shape[0] - pair
    far_cols = jnp.concatenate([hub_far, jnp.full((tail - hubs, 1), -5.0, F32)], axis=0)
    far_rows = jnp.concatenate([hub_far, jnp.full((64 - hubs, 1), -5.0, F32)], axis=0)
    cols[0:pair, :] = jnp.where(own_index == colv, 1.0, 0.0).astype(BF16)
    cols[pair:, :] = jnp.where(far_cols == colv, 1.0, 0.0).astype(BF16)
    coded = modes + 1.0
    for index, start, stop in ((own_index, 0, pair), (far_rows, pair, pair + 64)):
        hit = index == rows
        picks[start:stop, :] = jnp.where(hit, weights, 0.0).astype(BF16)
        codes[start:stop, :] = jnp.where(hit, coded, 0.0).astype(BF16)
    weight = lax.dot_general(picks[...], cols[...], NT, preferred_element_type=F32)
    code = lax.dot_general(codes[...], cols[...], NT, preferred_element_type=F32)
    for mode in range(terms):
        table = jnp.where(code == float(mode + 1), weight, 0.0).astype(BF16)
        main_ref[mode] = table[:pair]
        if mode > 0:
            send_ref[mode] = table[pair:, :pair]
    hub_lane = lax.broadcasted_iota(jnp.int32, (pair, cols.shape[0]), 1).astype(F32) - float(pair)
    own_rank = jnp.sum(
        jnp.where(lanes == own_index, rank, 0.0), axis=1, keepdims=True
    )
    main_ref[terms] = jnp.where(
        jnp.logical_and(own_rank >= 0.0, hub_lane == own_rank), 1.0, 0.0
    ).astype(BF16)
    near_rank = lax.broadcasted_iota(jnp.int32, (64, slot_total), 0).astype(F32)
    slot_row = slots
    near_slot = jnp.sum(jnp.where(near_rank == rank, slot_row, 0.0), axis=1, keepdims=True)
    near_has = jnp.sum(jnp.where(near_rank == rank, 1.0, 0.0), axis=1, keepdims=True)
    near_slot = jnp.where(near_has > 0.5, near_slot - base, -5.0)
    send_ref[0] = jnp.where(
        lax.broadcasted_iota(jnp.int32, (64, pair), 1).astype(F32) == near_slot, 1.0, 0.0
    ).astype(BF16)


def edge_kernel(field, near, far, lines, arrived):
    rows = field.shape[1]
    copies = [
        pltpu.make_async_copy(field.at[:, row, :], lines.at[k], arrived.at[k])
        for k, row in enumerate((0, rows - 1))
    ]
    for copy in copies:
        copy.start()
    for copy in copies:
        copy.wait()
    first = core_side() == 0
    near[...] = jnp.where(first, lines[0], lines[1])
    far[...] = jnp.where(first, lines[1], lines[0])


def split_kernel(field, unused, keep, send):
    slots, rows, width = field.shape
    first = core_side() == 0
    for at in range(0, slots, 8):
        lines = jnp.swapaxes(field[at : at + 8], 0, 1)
        for i in range(keep.shape[0]):
            keep[i, at : at + 8, :] = jnp.where(first, lines[i], lines[rows - 1 - i])
            send[i, at : at + 8, :] = jnp.where(first, lines[rows - 1 - i], lines[i])


def across(center):
    return five_point(0.0, center, 0.0)


def five_point(above, center, below):
    width = center.shape[1]
    lane = lax.broadcasted_iota(jnp.int32, center.shape, 1)
    left = jnp.where(lane == 0, 0.0, pltpu.roll(center, 1, 1))
    right = jnp.where(lane == width - 1, 0.0, pltpu.roll(center, width - 1, 1))
    return above + below + left + right - 4.0 * center


def row_place(index, rows):
    return jnp.where(core_side() == 0, index, rows - 1 - index)


def fill_buffer(value_ref, stiff, send_table, buffer, row, place):
    hubs = buffer.shape[1]
    width = buffer.shape[2]
    terms = send_table.shape[0]
    for start in range(0, width, 256):
        cut = slice(start, start + 256)
        value = value_ref[row, :, cut]
        total = jnp.dot(send_table[0], value, preferred_element_type=F32)
        for mode in range(1, terms):
            part = jnp.dot(send_table[mode], value, preferred_element_type=F32)
            total = total + stiff[mode, pl.ds(place, 1), cut] * part
        buffer[row, :, cut] = total[:hubs].astype(BF16)


def first_kernel(first_row, keep, got, stiff, send_table, unused, bent, buffer):
    side = core_side()
    count, pair, width = bent.shape
    own = keep.shape[1]
    for group in range(2):

        def chunk(k, carry):
            at = pl.multiple_of(k * 8, 8)
            cut = pl.ds(at, 8)
            far = pl.ds(group * own + at, 8)
            lines = [
                jnp.where(side == group, keep[row, cut, :], got[row, cut, :])
                for row in range(first_row - 1, first_row + count + 1)
            ]
            for row in range(count):
                value = five_point(lines[row], lines[row + 1], lines[row + 2])
                bent[row, far, :] = value.astype(BF16)
            return carry

        lax.fori_loop(0, own // 8, chunk, 0, unroll=3)
    for row in range(count):
        fill_buffer(bent, stiff, send_table, buffer, row, row_place(first_row + row, stiff.shape[1]))


def first_base_kernel(keep, got, unused, base):
    side = core_side()
    own = keep.shape[1]
    for group in range(2):

        def chunk(k, carry):
            at = pl.multiple_of(k * 8, 8)
            cut = pl.ds(at, 8)
            here, below = [
                jnp.where(side == group, keep[row, cut, :], got[row, cut, :]) for row in range(2)
            ]
            base[pl.ds(group * own + at, 8), :] = across(here) + below
            return carry

        lax.fori_loop(0, own // 8, chunk, 0, unroll=3)


def first_outer_kernel(base, halo_near, halo_far, stiff, send_table, unused, bent, buffer):
    first = core_side() == 0
    own = halo_near.shape[0]
    near, far = halo_near[...], halo_far[...]
    halo = jnp.concatenate([jnp.where(first, near, far), jnp.where(first, far, near)], axis=0)
    bent[0] = (base[...] + halo).astype(BF16)
    fill_buffer(bent, stiff, send_table, buffer, 0, row_place(0, stiff.shape[1]))


def pass_kernel(value, unused, out):
    out[...] = value[...]


def couple_kernel(first, outer_row, inner_rows, bent, got, stiff, table, unused, moment, *rest):
    stacked = rest[-1]
    edges = list(rest[:-1])
    outer = edges.pop(0) if outer_row is not None else None
    inner = edges.pop(0) if inner_rows else None
    count, pair, width = bent.shape
    hubs = got.shape[1]
    terms = stiff.shape[0]
    room = stacked.shape[0]
    stacked[pair + hubs :, :] = jnp.zeros((room - pair - hubs, width), BF16)
    for row in range(count):
        place = row_place(first + row, stiff.shape[1])
        stacked[0:pair, :] = bent[row]
        stacked[pair : pair + hubs, :] = got[row]
        for start in range(0, width, 256):
            cut = slice(start, start + 256)
            value = stacked[:, cut]
            total = jnp.dot(table[terms], value, preferred_element_type=F32)
            for mode in range(terms):
                part = jnp.dot(table[mode], value, preferred_element_type=F32)
                total = total + stiff[mode, pl.ds(place, 1), cut] * part
            moment[row, :, cut] = total
            if first + row == outer_row:
                outer[0, :, cut] = total.astype(BF16)
            if first + row in inner_rows:
                inner[inner_rows.index(first + row), :, cut] = total.astype(BF16)


def share(held, keep, send, rows, own):
    side = core_side()
    near = pl.multiple_of(side * own, 8)
    far = pl.multiple_of((1 - side) * own, 8)
    for target, row in enumerate(rows):
        keep[target] = held[row, pl.ds(near, own), :]
        send[target] = held[row, pl.ds(far, own), :]


def second_inner_kernel(row_zero, row_one, others, inner, stiff, send_table, held, bent, buffer):
    count, pair, width = bent.shape

    def chunk(k, carry):
        cut = pl.ds(pl.multiple_of(k * STEP, STEP), STEP)
        lines = [row_zero[0, cut, :], row_one[0, cut, :]] + [others[row, cut, :] for row in range(2)]
        lines += [inner[row, cut, :].astype(F32) for row in range(2)]
        for row in range(4):
            held[row, cut, :] = five_point(lines[row], lines[row + 1], lines[row + 2])
        for row in range(2):
            value = five_point(
                held[row, cut, :], held[row + 1, cut, :], held[row + 2, cut, :]
            )
            bent[row, cut, :] = value.astype(BF16)
        return carry

    lax.fori_loop(0, pair // STEP, chunk, 0, unroll=3)
    for row in range(count):
        fill_buffer(bent, stiff, send_table, buffer, row, row_place(row + 2, stiff.shape[1]))


def second_base_kernel(row_zero, row_one, held, base, ahead, keep, send):
    pair = row_zero.shape[1]
    tile = lax.axis_index("tile")
    last = lax.axis_size("tile") - 1
    at_edge = jnp.where(core_side() == 0, tile == 0, tile == last)

    def chunk(k, carry):
        cut = pl.ds(pl.multiple_of(k * STEP, STEP), STEP)
        here = row_zero[0, cut, :]
        partial = across(here) + row_one[0, cut, :]
        base[0, cut, :] = partial
        outside = jnp.where(at_edge, 0.0, here)
        ahead[0, cut, :] = five_point(outside, partial, held[0, cut, :])
        return carry

    lax.fori_loop(0, pair // STEP, chunk, 0, unroll=3)
    share(held, keep, send, (0, 1, 2), pair // 2)


def second_edge_kernel(base, ahead, near, next_near, stiff, send_table, zero, bent, buffer):
    pair = bent.shape[1]

    def chunk(k, carry):
        cut = pl.ds(pl.multiple_of(k * STEP, STEP), STEP)
        above = near[0, cut, :].astype(F32)
        zero[0, cut, :] = base[0, cut, :] + above
        value = ahead[0, cut, :] + next_near[0, cut, :].astype(F32) + 2.0 * across(above)
        bent[0, cut, :] = value.astype(BF16)
        return carry

    lax.fori_loop(0, pair // STEP, chunk, 0, unroll=3)
    fill_buffer(bent, stiff, send_table, buffer, 0, row_place(0, stiff.shape[1]))


def second_next_kernel(zero, held, stiff, send_table, unused, keep, send, bent, buffer):
    pair = bent.shape[1]

    def chunk(k, carry):
        cut = pl.ds(pl.multiple_of(k * STEP, STEP), STEP)
        value = five_point(zero[0, cut, :], held[0, cut, :], held[1, cut, :])
        bent[0, cut, :] = value.astype(BF16)
        return carry

    lax.fori_loop(0, pair // STEP, chunk, 0, unroll=3)
    fill_buffer(bent, stiff, send_table, buffer, 0, row_place(1, stiff.shape[1]))
    share(zero, keep, send, (0,), pair // 2)


def last_kernel(zero, one, inners, inner, keep, send):
    side = core_side()
    count, own, width = keep.shape
    for target, group in ((send, 1 - side), (keep, side)):

        def chunk(k, carry):
            at = pl.multiple_of(k * 8, 8)
            cut = pl.ds(pl.multiple_of(group * own + at, 8), 8)
            lines = [jnp.zeros((8, width), F32), zero[0, cut, :], one[0, cut, :]]
            lines += [inners[row, cut, :] for row in range(2)]
            lines += [inner[0, cut, :].astype(F32)]
            for row in range(count):
                target[row, pl.ds(at, 8), :] = five_point(
                    lines[row], lines[row + 1], lines[row + 2]
                )
            return carry

        lax.fori_loop(0, own // 8, chunk, 0, unroll=3)


def write_tiles(near, far, out, lines, done):
    first = core_side() == 0
    half = out.shape[1] // 2
    copies = []
    for k, at in enumerate(range(0, out.shape[0], CHUNK)):
        for start in range(at, at + CHUNK, 8):
            ours = [near(i, slice(start, start + 8)) for i in range(half)]
            theirs = [far(i, slice(start, start + 8)) for i in range(half)]
            rows = [jnp.where(first, a, b) for a, b in zip(ours, theirs)]
            rows += [jnp.where(first, b, a) for a, b in zip(ours[::-1], theirs[::-1])]
            lines[start : start + 8] = jnp.swapaxes(jnp.stack(rows, axis=0), 0, 1)
        cut = pl.ds(at, CHUNK)
        copies.append(pltpu.make_async_copy(lines.at[cut], out.at[cut], done.at[k]))
        copies[-1].start()
    for copy in copies:
        copy.wait()


def merge_kernel(keep_zero, keep, got_zero, got, unused, out, token, lines, done):
    token[...] = jnp.zeros_like(token)

    def near(i, cut):
        return keep_zero[0, cut, :] if i == 0 else keep[i - 1, cut, :]

    def far(i, cut):
        return got_zero[0, cut, :] if i == 0 else got[i - 1, cut, :]

    write_tiles(near, far, out, lines, done)


def halves(halo, own):
    whole = halo[0].astype(F32)
    first = core_side() == 0
    lower, upper = whole[:own], whole[own:]
    return jnp.where(first, lower, upper), jnp.where(first, upper, lower)


def cut_kernel(halo, unused, part):
    part[...] = halves(halo, part.shape[0])[1].astype(BF16)


def last_merge_kernel(keep, got, halo, far_halo, out, lines, done):
    near_line = halves(halo, keep.shape[1])[0]
    far_line = far_halo[...].astype(F32)

    def near(i, cut):
        return keep[0, cut, :] + near_line[cut] if i == 0 else keep[i, cut, :]

    def far(i, cut):
        return got[0, cut, :] + far_line[cut] if i == 0 else got[i, cut, :]

    write_tiles(near, far, out, lines, done)


def body(slot_field, stiffness, triple_modes, triple_rows, triple_cols, triple_weights, slot_of):
    own, rows, width = slot_field.shape
    terms = stiffness.shape[0]
    pair = 2 * own
    half = rows // 2
    chaos = lax.axis_size("chaos")
    tiles = lax.axis_size("tile")
    slot_total = own * chaos
    modes = terms - 1
    hubs = 1 + modes * (modes + 1) // 2
    room = -(-(pair + hubs) // 16) * 16
    side = core_side()

    core_swap = [(i, i ^ 1) for i in range(chaos)]
    chip_swap = [(i, i ^ 2) for i in range(chaos)]
    tile_swap = []
    for high in range(0, chaos, 2):
        for tile in range(tiles - 1):
            one, two = (high + 1) * tiles + tile, high * tiles + tile + 1
            tile_swap += [(one, two), (two, one)]

    def by_core(value):
        return lax.ppermute(value, "chaos", core_swap)

    def by_chip(value):
        return lax.ppermute(value, "chaos", chip_swap)

    def by_tile(value):
        return lax.ppermute(value, ("chaos", "tile"), tile_swap)

    count = triple_modes.shape[0]
    wide = -(-count // 128) * 128

    def line(value, fill):
        value = value.astype(F32)
        return jnp.pad(value, (0, wide - value.shape[0]), constant_values=fill)

    entries = jnp.stack(
        [
            line(triple_modes, -1.0),
            line(triple_rows, -1.0),
            line(triple_cols, -1.0),
            line(triple_weights, 0.0),
            line(slot_of, -1.0),
        ]
        + [jnp.zeros((wide,), F32)] * 3
    )
    row_block = shape((own, width), F32)
    near_edge, far_edge = call(
        edge_kernel,
        (row_block, row_block),
        [pltpu.VMEM((2, own, width), F32), pltpu.SemaphoreType.DMA((2,))],
        2.0,
        [ANY],
        60,
    )(slot_field)
    halo_far = by_tile(near_edge)
    got_edge = by_core(far_edge)
    halo_near = by_tile(got_edge)

    main_table, send_table = call(
        functools.partial(table_kernel, terms, pair, hubs, slot_total),
        (shape((terms + 1, pair, room), BF16), shape((terms, 64, pair), BF16)),
        [
            pltpu.VMEM((pair + 64, wide), BF16),
            pltpu.VMEM((pair + 64, wide), BF16),
            pltpu.VMEM((room, wide), BF16),
        ],
        3.0,
        [VMEM, ANY],
        12,
    )(entries, got_edge)

    line_block = shape((half + 1, own, width), F32)
    keep, send = call(split_kernel, (line_block, line_block), (), 2.5, [VMEM, ANY])(
        slot_field, got_edge
    )
    got = by_core(send)

    def bents(count):
        return (shape((count, pair, width), BF16), shape((count, hubs, width), BF16))

    def outs(count):
        return (shape((count, own, width), F32),) * 2

    def bend(first, count, after):
        bent, buffer = call(
            functools.partial(first_kernel, first), bents(count), (), 0.9 * count, [VMEM] * 4 + [ANY]
        )(keep, got, stiffness, send_table, after)
        return bent, buffer, by_chip(buffer)

    def couple(bent, other, first, outer_row, inner_rows, after, weight=1.0):
        count = bent.shape[0]
        out = [shape((count, pair, width), F32)]
        if outer_row is not None:
            out.append(shape((1, pair, width), BF16))
        if inner_rows:
            out.append(shape((len(inner_rows), pair, width), BF16))
        return call(
            functools.partial(couple_kernel, first, outer_row, inner_rows),
            tuple(out),
            [pltpu.VMEM((room, width), BF16)],
            weight * count,
            [VMEM] * 4 + [ANY],
        )(bent, other, stiffness, main_table, after)

    bent_one, sent, cross_one = bend(1, 1, got)
    bent_in, sent, cross_in = bend(2, 2, sent)
    base = call(first_base_kernel, shape((pair, width), F32), (), 0.4, [VMEM] * 2 + [ANY])(
        keep, got, sent
    )
    moment_one, edge_one = couple(bent_one, cross_one, 1, 1, (), base)
    bent_out, sent = call(first_outer_kernel, bents(1), (), 0.9, [VMEM] * 5 + [ANY])(
        base, halo_near, halo_far, stiffness, send_table, edge_one
    )
    cross_out = by_chip(sent)
    edge_one = call(pass_kernel, shape(edge_one.shape, BF16), (), 0.1, [VMEM, ANY])(edge_one, sent)
    next_near = by_tile(edge_one)
    moment_in, edge_in = couple(bent_in, cross_in, 2, None, (3, 2), edge_one)
    inner = by_core(edge_in)
    moment_out, edge_zero = couple(bent_out, cross_out, 0, 0, (), edge_in)
    near = by_tile(edge_zero)

    row_shape = shape((1, pair, width), F32)
    held, bent_in, buffer_in = call(
        second_inner_kernel, (shape((4, pair, width), F32),) + bents(2), (), 2.7
    )(moment_out, moment_one, moment_in, inner, stiffness, send_table)
    base, ahead, keep_in, send_in = call(
        second_base_kernel, (row_shape, row_shape) + outs(3), (), 3.0
    )(moment_out, moment_one, held)
    got_in = by_core(send_in)
    cross_in = by_chip(buffer_in)
    zero, bent_out, buffer_out = call(second_edge_kernel, (row_shape,) + bents(1), (), EARLY)(
        base, ahead, near, next_near, stiffness, send_table
    )
    cross_out = by_chip(buffer_out)
    keep_out, send_out, bent_one, buffer_one = call(
        second_next_kernel, outs(1) + bents(1), (), EARLY, [VMEM] * 4 + [ANY]
    )(zero, held, stiffness, send_table, buffer_out)
    cross_one = by_chip(buffer_one)
    got_out = by_core(send_out)
    moment_out, edge_zero = couple(bent_out, cross_out, 0, 0, (), buffer_one)
    near = by_tile(edge_zero)
    moment_in, inner = couple(bent_in, cross_in, 2, None, (3,), edge_zero)
    inner = by_core(inner)
    (moment_one,) = couple(bent_one, cross_one, 1, None, (), edge_zero)

    keep, send = call(last_kernel, outs(half), (), 2.5)(
        moment_out, moment_one, moment_in, inner
    )
    got = by_core(send)
    whole = shape(slot_field.shape, F32)
    writers = [pltpu.VMEM(slot_field.shape, F32), pltpu.SemaphoreType.DMA((own // CHUNK,))]
    first_apply, token = call(
        merge_kernel, (whole, TOKEN), writers, 1.9, [VMEM] * 4 + [ANY], 6, (ANY, VMEM)
    )(keep_out, keep_in, got_out, got_in, keep)
    far_halo = by_core(
        call(cut_kernel, shape((own, width), BF16), (), 0.3, [VMEM, ANY])(near, token)
    )
    second_apply = call(last_merge_kernel, whole, writers, 1.9, [VMEM] * 4, 6, ANY)(
        keep, got, near, far_halo
    )
    return first_apply, second_apply


def solution(mesh):
    return jax.shard_map(
        body,
        mesh=mesh,
        in_specs=(P("chaos", "tile", None), P(None, "tile", None), P(), P(), P(), P(), P()),
        out_specs=(P("chaos", "tile", None), P("chaos", "tile", None)),
        check_vma=False,
    )
```

```python
import functools
import jax
import jax.numpy as jnp
from jax import lax
from jax.experimental import pallas as pl
from jax.experimental.pallas import tpu as pltpu
from jax.sharding import PartitionSpec as P

F32, BF16 = jnp.float32, jnp.bfloat16
VMEM = pl.BlockSpec(memory_space=pltpu.VMEM)
TOKEN = jax.ShapeDtypeStruct((8, 128), jnp.int32)
ANY = pl.BlockSpec(memory_space=pl.ANY)
NT = (((1,), (1,)), ((), ()))
STEP = 16
CHUNK = 8
PIECES = 3
EARLY = 0.01


def call(kernel, outs, scratch=(), us=1.0, specs=None, room=12, into=None):
    extra = {} if specs is None else {"in_specs": specs}
    if into is not None:
        extra["out_specs"] = into
    return pl.pallas_call(
        kernel,
        out_shape=outs,
        scratch_shapes=scratch,
        compiler_params=pltpu.CompilerParams(vmem_limit_bytes=room * 1024 * 1024),
        cost_estimate=pl.CostEstimate(
            flops=int(us * 1e10), bytes_accessed=10, transcendentals=0
        ),
        **extra,
    )


def shape(dims, kind):
    return jax.ShapeDtypeStruct(dims, kind)


def core_side():
    return lax.rem(lax.axis_index("chaos"), 2)


def table_kernel(
    terms, pair, hubs, slot_total, entries, unused, main_ref, send_ref, picks, codes, cols
):
    wide = entries.shape[1]
    modes = entries[0:1, :]
    rows = entries[1:2, :]
    colv = entries[2:3, :]
    weights = entries[3:4, :]
    slots = entries[4:5, :slot_total]
    chip = lax.axis_index("chaos") // 2
    base = (chip * pair).astype(F32)

    index_col = lax.broadcasted_iota(jnp.int32, (slot_total, wide), 0).astype(F32)
    row_hot = jnp.where(index_col == rows, 1.0, 0.0).astype(BF16)
    col_hot = jnp.where(index_col == colv, 1.0, 0.0).astype(BF16)
    ones = jnp.ones((8, wide), BF16)
    degree = lax.dot_general(ones, row_hot, NT, preferred_element_type=F32)
    zeroth = jnp.where(degree == float(terms), 1.0, 0.0)
    col_zeroth = lax.dot_general(
        zeroth.astype(BF16), col_hot, (((1,), (0,)), ((), ())), preferred_element_type=F32
    )
    beside = lax.dot_general(col_zeroth.astype(BF16), row_hot, NT, preferred_element_type=F32)
    even = jnp.where(degree > 5.0, jnp.where(beside > 0.5, zeroth, 1.0), 0.0)
    before = jnp.where(
        lax.broadcasted_iota(jnp.int32, (slot_total, slot_total), 0)
        < lax.broadcasted_iota(jnp.int32, (slot_total, slot_total), 1),
        1.0,
        0.0,
    ).astype(BF16)
    rank = lax.dot_general(
        even.astype(BF16), before, (((1,), (0,)), ((), ())), preferred_element_type=F32
    )
    rank = jnp.where(even > 0.5, rank, -1.0)[0:1, :]
    lane_index = lax.broadcasted_iota(jnp.int32, (hubs, slot_total), 1).astype(F32)
    hub_hit = lax.broadcasted_iota(jnp.int32, (hubs, slot_total), 0).astype(F32) == rank
    hub_index = jnp.sum(jnp.where(hub_hit, lane_index, 0.0), axis=1, keepdims=True)
    hub_slot = jnp.sum(jnp.where(hub_hit, slots, 0.0), axis=1, keepdims=True)
    hub_here = jnp.logical_and(hub_slot >= base, hub_slot < base + float(pair))
    hub_far = jnp.where(hub_here, -5.0, hub_index)
    hub_near = jnp.where(hub_here, hub_index, -5.0)

    place = lax.broadcasted_iota(jnp.int32, (pair, slot_total), 0).astype(F32) + base
    lanes = lax.broadcasted_iota(jnp.int32, (pair, slot_total), 1).astype(F32)
    own_index = jnp.sum(jnp.where(place == slots, lanes, 0.0), axis=1, keepdims=True)

    tail = cols.shape[0] - pair
    far_cols = jnp.concatenate([hub_far, jnp.full((tail - hubs, 1), -5.0, F32)], axis=0)
    far_rows = jnp.concatenate([hub_far, jnp.full((64 - hubs, 1), -5.0, F32)], axis=0)
    cols[0:pair, :] = jnp.where(own_index == colv, 1.0, 0.0).astype(BF16)
    cols[pair:, :] = jnp.where(far_cols == colv, 1.0, 0.0).astype(BF16)
    coded = modes + 1.0
    for index, start, stop in ((own_index, 0, pair), (far_rows, pair, pair + 64)):
        hit = index == rows
        picks[start:stop, :] = jnp.where(hit, weights, 0.0).astype(BF16)
        codes[start:stop, :] = jnp.where(hit, coded, 0.0).astype(BF16)
    weight = lax.dot_general(picks[...], cols[...], NT, preferred_element_type=F32)
    code = lax.dot_general(codes[...], cols[...], NT, preferred_element_type=F32)
    for mode in range(terms):
        table = jnp.where(code == float(mode + 1), weight, 0.0).astype(BF16)
        main_ref[mode] = table[:pair]
        if mode > 0:
            send_ref[mode] = table[pair:, :pair]
    hub_lane = lax.broadcasted_iota(jnp.int32, (pair, cols.shape[0]), 1).astype(F32) - float(pair)
    own_rank = jnp.sum(
        jnp.where(lanes == own_index, rank, 0.0), axis=1, keepdims=True
    )
    main_ref[terms] = jnp.where(
        jnp.logical_and(own_rank >= 0.0, hub_lane == own_rank), 1.0, 0.0
    ).astype(BF16)
    near_rank = lax.broadcasted_iota(jnp.int32, (64, slot_total), 0).astype(F32)
    slot_row = slots
    near_slot = jnp.sum(jnp.where(near_rank == rank, slot_row, 0.0), axis=1, keepdims=True)
    near_has = jnp.sum(jnp.where(near_rank == rank, 1.0, 0.0), axis=1, keepdims=True)
    near_slot = jnp.where(near_has > 0.5, near_slot - base, -5.0)
    send_ref[0] = jnp.where(
        lax.broadcasted_iota(jnp.int32, (64, pair), 1).astype(F32) == near_slot, 1.0, 0.0
    ).astype(BF16)


def edge_kernel(field, near, far, lines, arrived):
    rows = field.shape[1]
    step = field.shape[0] // PIECES
    copies = []
    for k, row in enumerate((0, rows - 1)):
        for piece in range(PIECES):
            cut = pl.ds(piece * step, step)
            copies.append(
                pltpu.make_async_copy(
                    field.at[cut, row, :], lines.at[k, cut, :], arrived.at[k * PIECES + piece]
                )
            )
    for copy in copies:
        copy.start()
    for copy in copies:
        copy.wait()
    first = core_side() == 0
    near[...] = jnp.where(first, lines[0], lines[1])
    far[...] = jnp.where(first, lines[1], lines[0])


def split_kernel(field, unused, keep, send):
    slots, rows, width = field.shape
    first = core_side() == 0
    for at in range(0, slots, 8):
        lines = jnp.swapaxes(field[at : at + 8], 0, 1)
        for i in range(keep.shape[0]):
            keep[i, at : at + 8, :] = jnp.where(first, lines[i], lines[rows - 1 - i])
            send[i, at : at + 8, :] = jnp.where(first, lines[rows - 1 - i], lines[i])


def across(center):
    return five_point(0.0, center, 0.0)


def five_point(above, center, below):
    width = center.shape[1]
    lane = lax.broadcasted_iota(jnp.int32, center.shape, 1)
    left = jnp.where(lane == 0, 0.0, pltpu.roll(center, 1, 1))
    right = jnp.where(lane == width - 1, 0.0, pltpu.roll(center, width - 1, 1))
    return above + below + left + right - 4.0 * center


def row_place(index, rows):
    return jnp.where(core_side() == 0, index, rows - 1 - index)


def fill_buffer(value_ref, stiff, send_table, buffer, row, place):
    hubs = buffer.shape[1]
    width = buffer.shape[2]
    terms = send_table.shape[0]
    for start in range(0, width, 256):
        cut = slice(start, start + 256)
        value = value_ref[row, :, cut]
        total = jnp.dot(send_table[0], value, preferred_element_type=F32)
        for mode in range(1, terms):
            part = jnp.dot(send_table[mode], value, preferred_element_type=F32)
            total = total + stiff[mode, pl.ds(place, 1), cut] * part
        buffer[row, :, cut] = total[:hubs].astype(BF16)


def first_kernel(first_row, keep, got, stiff, send_table, unused, bent, buffer):
    side = core_side()
    count, pair, width = bent.shape
    own = keep.shape[1]
    for group in range(2):

        def chunk(k, carry):
            at = pl.multiple_of(k * 8, 8)
            cut = pl.ds(at, 8)
            far = pl.ds(group * own + at, 8)
            lines = [
                jnp.where(side == group, keep[row, cut, :], got[row, cut, :])
                for row in range(first_row - 1, first_row + count + 1)
            ]
            for row in range(count):
                value = five_point(lines[row], lines[row + 1], lines[row + 2])
                bent[row, far, :] = value.astype(BF16)
            return carry

        lax.fori_loop(0, own // 8, chunk, 0, unroll=3)
    for row in range(count):
        fill_buffer(bent, stiff, send_table, buffer, row, row_place(first_row + row, stiff.shape[1]))


def first_base_kernel(keep, got, unused, base):
    side = core_side()
    own = keep.shape[1]
    for group in range(2):

        def chunk(k, carry):
            at = pl.multiple_of(k * 8, 8)
            cut = pl.ds(at, 8)
            here, below = [
                jnp.where(side == group, keep[row, cut, :], got[row, cut, :]) for row in range(2)
            ]
            base[pl.ds(group * own + at, 8), :] = across(here) + below
            return carry

        lax.fori_loop(0, own // 8, chunk, 0, unroll=3)


def first_outer_kernel(base, halo_near, halo_far, stiff, send_table, unused, bent, buffer):
    first = core_side() == 0
    own = halo_near.shape[0]
    near, far = halo_near[...], halo_far[...]
    halo = jnp.concatenate([jnp.where(first, near, far), jnp.where(first, far, near)], axis=0)
    bent[0] = (base[...] + halo).astype(BF16)
    fill_buffer(bent, stiff, send_table, buffer, 0, row_place(0, stiff.shape[1]))


def pass_kernel(value, unused, out):
    out[...] = value[...]


def couple_kernel(first, outer_row, inner_rows, bent, got, stiff, table, unused, moment, *rest):
    stacked = rest[-1]
    edges = list(rest[:-1])
    outer = edges.pop(0) if outer_row is not None else None
    inner = edges.pop(0) if inner_rows else None
    count, pair, width = bent.shape
    hubs = got.shape[1]
    terms = stiff.shape[0]
    room = stacked.shape[0]
    stacked[pair + hubs :, :] = jnp.zeros((room - pair - hubs, width), BF16)
    for row in range(count):
        place = row_place(first + row, stiff.shape[1])
        stacked[0:pair, :] = bent[row]
        stacked[pair : pair + hubs, :] = got[row]
        for start in range(0, width, 256):
            cut = slice(start, start + 256)
            value = stacked[:, cut]
            total = jnp.dot(table[terms], value, preferred_element_type=F32)
            for mode in range(terms):
                part = jnp.dot(table[mode], value, preferred_element_type=F32)
                total = total + stiff[mode, pl.ds(place, 1), cut] * part
            moment[row, :, cut] = total
            if first + row == outer_row:
                outer[0, :, cut] = total.astype(BF16)
            if first + row in inner_rows:
                inner[inner_rows.index(first + row), :, cut] = total.astype(BF16)


def share(held, keep, send, rows, own):
    side = core_side()
    near = pl.multiple_of(side * own, 8)
    far = pl.multiple_of((1 - side) * own, 8)
    for target, row in enumerate(rows):
        keep[target] = held[row, pl.ds(near, own), :]
        send[target] = held[row, pl.ds(far, own), :]


def second_inner_kernel(row_zero, row_one, others, inner, stiff, send_table, held, bent, buffer):
    count, pair, width = bent.shape

    def chunk(k, carry):
        cut = pl.ds(pl.multiple_of(k * STEP, STEP), STEP)
        lines = [row_zero[0, cut, :], row_one[0, cut, :]] + [others[row, cut, :] for row in range(2)]
        lines += [inner[row, cut, :].astype(F32) for row in range(2)]
        for row in range(4):
            held[row, cut, :] = five_point(lines[row], lines[row + 1], lines[row + 2])
        for row in range(2):
            value = five_point(
                held[row, cut, :], held[row + 1, cut, :], held[row + 2, cut, :]
            )
            bent[row, cut, :] = value.astype(BF16)
        return carry

    lax.fori_loop(0, pair // STEP, chunk, 0, unroll=3)
    for row in range(count):
        fill_buffer(bent, stiff, send_table, buffer, row, row_place(row + 2, stiff.shape[1]))


def second_base_kernel(row_zero, row_one, held, base, ahead, keep, send):
    pair = row_zero.shape[1]
    tile = lax.axis_index("tile")
    last = lax.axis_size("tile") - 1
    at_edge = jnp.where(core_side() == 0, tile == 0, tile == last)

    def chunk(k, carry):
        cut = pl.ds(pl.multiple_of(k * STEP, STEP), STEP)
        here = row_zero[0, cut, :]
        partial = across(here) + row_one[0, cut, :]
        base[0, cut, :] = partial
        outside = jnp.where(at_edge, 0.0, here)
        ahead[0, cut, :] = five_point(outside, partial, held[0, cut, :])
        return carry

    lax.fori_loop(0, pair // STEP, chunk, 0, unroll=3)
    share(held, keep, send, (0, 1, 2), pair // 2)


def second_edge_kernel(base, ahead, near, next_near, stiff, send_table, zero, bent, buffer):
    pair = bent.shape[1]

    def chunk(k, carry):
        cut = pl.ds(pl.multiple_of(k * STEP, STEP), STEP)
        above = near[0, cut, :].astype(F32)
        zero[0, cut, :] = base[0, cut, :] + above
        value = ahead[0, cut, :] + next_near[0, cut, :].astype(F32) + 2.0 * across(above)
        bent[0, cut, :] = value.astype(BF16)
        return carry

    lax.fori_loop(0, pair // STEP, chunk, 0, unroll=9)
    fill_buffer(bent, stiff, send_table, buffer, 0, row_place(0, stiff.shape[1]))


def second_next_kernel(zero, held, stiff, send_table, unused, keep, send, bent, buffer):
    pair = bent.shape[1]

    def chunk(k, carry):
        cut = pl.ds(pl.multiple_of(k * STEP, STEP), STEP)
        value = five_point(zero[0, cut, :], held[0, cut, :], held[1, cut, :])
        bent[0, cut, :] = value.astype(BF16)
        return carry

    lax.fori_loop(0, pair // STEP, chunk, 0, unroll=3)
    fill_buffer(bent, stiff, send_table, buffer, 0, row_place(1, stiff.shape[1]))
    share(zero, keep, send, (0,), pair // 2)


def last_kernel(zero, one, inners, inner, keep, send):
    side = core_side()
    count, own, width = keep.shape
    for target, group in ((send, 1 - side), (keep, side)):

        def chunk(k, carry):
            at = pl.multiple_of(k * 8, 8)
            cut = pl.ds(pl.multiple_of(group * own + at, 8), 8)
            lines = [jnp.zeros((8, width), F32), zero[0, cut, :], one[0, cut, :]]
            lines += [inners[row, cut, :] for row in range(2)]
            lines += [inner[0, cut, :].astype(F32)]
            for row in range(count):
                target[row, pl.ds(at, 8), :] = five_point(
                    lines[row], lines[row + 1], lines[row + 2]
                )
            return carry

        lax.fori_loop(0, own // 8, chunk, 0, unroll=3)


def write_tiles(near, far, out, lines, done):
    first = core_side() == 0
    half = out.shape[1] // 2
    copies = []
    for k, at in enumerate(range(0, out.shape[0], CHUNK)):
        for start in range(at, at + CHUNK, 8):
            ours = [near(i, slice(start, start + 8)) for i in range(half)]
            theirs = [far(i, slice(start, start + 8)) for i in range(half)]
            rows = [jnp.where(first, a, b) for a, b in zip(ours, theirs)]
            rows += [jnp.where(first, b, a) for a, b in zip(ours[::-1], theirs[::-1])]
            lines[start : start + 8] = jnp.swapaxes(jnp.stack(rows, axis=0), 0, 1)
        cut = pl.ds(at, CHUNK)
        copies.append(pltpu.make_async_copy(lines.at[cut], out.at[cut], done.at[k]))
        copies[-1].start()
    for copy in copies:
        copy.wait()


def merge_kernel(keep_zero, keep, got_zero, got, unused, out, token, lines, done):
    token[...] = jnp.zeros_like(token)

    def near(i, cut):
        return keep_zero[0, cut, :] if i == 0 else keep[i - 1, cut, :]

    def far(i, cut):
        return got_zero[0, cut, :] if i == 0 else got[i - 1, cut, :]

    write_tiles(near, far, out, lines, done)


def halves(halo, own):
    whole = halo[0].astype(F32)
    first = core_side() == 0
    lower, upper = whole[:own], whole[own:]
    return jnp.where(first, lower, upper), jnp.where(first, upper, lower)


def cut_kernel(halo, unused, part):
    part[...] = halves(halo, part.shape[0])[1].astype(BF16)


def last_merge_kernel(keep, got, halo, far_halo, out, lines, done):
    near_line = halves(halo, keep.shape[1])[0]
    far_line = far_halo[...].astype(F32)

    def near(i, cut):
        return keep[0, cut, :] + near_line[cut] if i == 0 else keep[i, cut, :]

    def far(i, cut):
        return got[0, cut, :] + far_line[cut] if i == 0 else got[i, cut, :]

    write_tiles(near, far, out, lines, done)


def body(slot_field, stiffness, triple_modes, triple_rows, triple_cols, triple_weights, slot_of):
    own, rows, width = slot_field.shape
    terms = stiffness.shape[0]
    pair = 2 * own
    half = rows // 2
    chaos = lax.axis_size("chaos")
    tiles = lax.axis_size("tile")
    slot_total = own * chaos
    modes = terms - 1
    hubs = 1 + modes * (modes + 1) // 2
    room = -(-(pair + hubs) // 16) * 16
    side = core_side()

    core_swap = [(i, i ^ 1) for i in range(chaos)]
    chip_swap = [(i, i ^ 2) for i in range(chaos)]
    tile_swap = []
    for high in range(0, chaos, 2):
        for tile in range(tiles - 1):
            one, two = (high + 1) * tiles + tile, high * tiles + tile + 1
            tile_swap += [(one, two), (two, one)]

    def by_core(value):
        return lax.ppermute(value, "chaos", core_swap)

    def by_chip(value):
        return lax.ppermute(value, "chaos", chip_swap)

    def by_tile(value):
        return lax.ppermute(value, ("chaos", "tile"), tile_swap)

    count = triple_modes.shape[0]
    wide = -(-count // 128) * 128

    def line(value, fill):
        value = value.astype(F32)
        return jnp.pad(value, (0, wide - value.shape[0]), constant_values=fill)

    entries = jnp.stack(
        [
            line(triple_modes, -1.0),
            line(triple_rows, -1.0),
            line(triple_cols, -1.0),
            line(triple_weights, 0.0),
            line(slot_of, -1.0),
        ]
        + [jnp.zeros((wide,), F32)] * 3
    )
    row_block = shape((own, width), F32)
    near_edge, far_edge = call(
        edge_kernel,
        (row_block, row_block),
        [pltpu.VMEM((2, own, width), F32), pltpu.SemaphoreType.DMA((2 * PIECES,))],
        2.0,
        [ANY],
        60,
    )(slot_field)
    halo_far = by_tile(near_edge)
    got_edge = by_core(far_edge)
    halo_near = by_tile(got_edge)

    main_table, send_table = call(
        functools.partial(table_kernel, terms, pair, hubs, slot_total),
        (shape((terms + 1, pair, room), BF16), shape((terms, 64, pair), BF16)),
        [
            pltpu.VMEM((pair + 64, wide), BF16),
            pltpu.VMEM((pair + 64, wide), BF16),
            pltpu.VMEM((room, wide), BF16),
        ],
        3.0,
        [VMEM, ANY],
        12,
    )(entries, got_edge)

    line_block = shape((half + 1, own, width), F32)
    keep, send = call(split_kernel, (line_block, line_block), (), 2.5, [VMEM, ANY])(
        slot_field, got_edge
    )
    got = by_core(send)

    def bents(count):
        return (shape((count, pair, width), BF16), shape((count, hubs, width), BF16))

    def outs(count):
        return (shape((count, own, width), F32),) * 2

    def bend(first, count, after):
        bent, buffer = call(
            functools.partial(first_kernel, first), bents(count), (), 0.9 * count, [VMEM] * 4 + [ANY]
        )(keep, got, stiffness, send_table, after)
        return bent, buffer, by_chip(buffer)

    def couple(bent, other, first, outer_row, inner_rows, after, weight=1.0):
        count = bent.shape[0]
        out = [shape((count, pair, width), F32)]
        if outer_row is not None:
            out.append(shape((1, pair, width), BF16))
        if inner_rows:
            out.append(shape((len(inner_rows), pair, width), BF16))
        return call(
            functools.partial(couple_kernel, first, outer_row, inner_rows),
            tuple(out),
            [pltpu.VMEM((room, width), BF16)],
            weight * count,
            [VMEM] * 4 + [ANY],
        )(bent, other, stiffness, main_table, after)

    bent_one, sent, cross_one = bend(1, 1, got)
    bent_in, sent, cross_in = bend(2, 2, sent)
    base = call(first_base_kernel, shape((pair, width), F32), (), 0.4, [VMEM] * 2 + [ANY])(
        keep, got, sent
    )
    moment_one, edge_one = couple(bent_one, cross_one, 1, 1, (), base)
    bent_out, sent = call(first_outer_kernel, bents(1), (), 0.9, [VMEM] * 5 + [ANY])(
        base, halo_near, halo_far, stiffness, send_table, edge_one
    )
    cross_out = by_chip(sent)
    edge_one = call(pass_kernel, shape(edge_one.shape, BF16), (), 0.1, [VMEM, ANY])(edge_one, sent)
    next_near = by_tile(edge_one)
    moment_in, edge_in = couple(bent_in, cross_in, 2, None, (3, 2), edge_one)
    inner = by_core(edge_in)
    moment_out, edge_zero = couple(bent_out, cross_out, 0, 0, (), edge_in)
    near = by_tile(edge_zero)

    row_shape = shape((1, pair, width), F32)
    held, bent_in, buffer_in = call(
        second_inner_kernel, (shape((4, pair, width), F32),) + bents(2), (), 2.7
    )(moment_out, moment_one, moment_in, inner, stiffness, send_table)
    base, ahead, keep_in, send_in = call(
        second_base_kernel, (row_shape, row_shape) + outs(3), (), 3.0
    )(moment_out, moment_one, held)
    got_in = by_core(send_in)
    cross_in = by_chip(buffer_in)
    zero, bent_out, buffer_out = call(second_edge_kernel, (row_shape,) + bents(1), (), EARLY)(
        base, ahead, near, next_near, stiffness, send_table
    )
    cross_out = by_chip(buffer_out)
    keep_out, send_out, bent_one, buffer_one = call(
        second_next_kernel, outs(1) + bents(1), (), EARLY, [VMEM] * 4 + [ANY]
    )(zero, held, stiffness, send_table, cross_in)
    cross_one = by_chip(buffer_one)
    got_out = by_core(send_out)
    moment_out, edge_zero = couple(bent_out, cross_out, 0, 0, (), buffer_one)
    near = by_tile(edge_zero)
    moment_in, inner = couple(bent_in, cross_in, 2, None, (3,), edge_zero)
    inner = by_core(inner)
    (moment_one,) = couple(bent_one, cross_one, 1, None, (), edge_zero)

    keep, send = call(last_kernel, outs(half), (), 2.5)(
        moment_out, moment_one, moment_in, inner
    )
    got = by_core(send)
    whole = shape(slot_field.shape, F32)
    writers = [pltpu.VMEM(slot_field.shape, F32), pltpu.SemaphoreType.DMA((own // CHUNK,))]
    first_apply, token = call(
        merge_kernel, (whole, TOKEN), writers, 1.9, [VMEM] * 4 + [ANY], 6, (ANY, VMEM)
    )(keep_out, keep_in, got_out, got_in, keep)
    far_halo = by_core(
        call(cut_kernel, shape((own, width), BF16), (), 0.3, [VMEM, ANY])(near, token)
    )
    second_apply = call(last_merge_kernel, whole, writers, 1.9, [VMEM] * 4, 6, ANY)(
        keep, got, near, far_halo
    )
    return first_apply, second_apply


def solution(mesh):
    return jax.shard_map(
        body,
        mesh=mesh,
        in_specs=(P("chaos", "tile", None), P(None, "tile", None), P(), P(), P(), P(), P()),
        out_specs=(P("chaos", "tile", None), P("chaos", "tile", None)),
        check_vma=False,
    )
```

```python
import functools
import jax
import jax.numpy as jnp
from jax import lax
from jax.experimental import pallas as pl
from jax.experimental.pallas import tpu as pltpu
from jax.sharding import PartitionSpec as P

F32, BF16 = jnp.float32, jnp.bfloat16
VMEM = pl.BlockSpec(memory_space=pltpu.VMEM)
TOKEN = jax.ShapeDtypeStruct((8, 128), jnp.int32)
ANY = pl.BlockSpec(memory_space=pl.ANY)
NT = (((1,), (1,)), ((), ()))
STEP = 16
CHUNK = 8
PIECES = 1
EARLY = 0.01


def call(kernel, outs, scratch=(), us=1.0, specs=None, room=12, into=None):
    extra = {} if specs is None else {"in_specs": specs}
    if into is not None:
        extra["out_specs"] = into
    return pl.pallas_call(
        kernel,
        out_shape=outs,
        scratch_shapes=scratch,
        compiler_params=pltpu.CompilerParams(vmem_limit_bytes=room * 1024 * 1024),
        cost_estimate=pl.CostEstimate(
            flops=int(us * 1e10), bytes_accessed=10, transcendentals=0
        ),
        **extra,
    )


def shape(dims, kind):
    return jax.ShapeDtypeStruct(dims, kind)


def core_side():
    return lax.rem(lax.axis_index("chaos"), 2)


def table_kernel(
    terms, pair, hubs, slot_total, entries, unused, main_ref, send_ref, picks, codes, cols
):
    wide = entries.shape[1]
    modes = entries[0:1, :]
    rows = entries[1:2, :]
    colv = entries[2:3, :]
    weights = entries[3:4, :]
    slots = entries[4:5, :slot_total]
    chip = lax.axis_index("chaos") // 2
    base = (chip * pair).astype(F32)

    index_col = lax.broadcasted_iota(jnp.int32, (slot_total, wide), 0).astype(F32)
    row_hot = jnp.where(index_col == rows, 1.0, 0.0).astype(BF16)
    col_hot = jnp.where(index_col == colv, 1.0, 0.0).astype(BF16)
    ones = jnp.ones((8, wide), BF16)
    degree = lax.dot_general(ones, row_hot, NT, preferred_element_type=F32)
    zeroth = jnp.where(degree == float(terms), 1.0, 0.0)
    col_zeroth = lax.dot_general(
        zeroth.astype(BF16), col_hot, (((1,), (0,)), ((), ())), preferred_element_type=F32
    )
    beside = lax.dot_general(col_zeroth.astype(BF16), row_hot, NT, preferred_element_type=F32)
    even = jnp.where(degree > 5.0, jnp.where(beside > 0.5, zeroth, 1.0), 0.0)
    before = jnp.where(
        lax.broadcasted_iota(jnp.int32, (slot_total, slot_total), 0)
        < lax.broadcasted_iota(jnp.int32, (slot_total, slot_total), 1),
        1.0,
        0.0,
    ).astype(BF16)
    rank = lax.dot_general(
        even.astype(BF16), before, (((1,), (0,)), ((), ())), preferred_element_type=F32
    )
    rank = jnp.where(even > 0.5, rank, -1.0)[0:1, :]
    lane_index = lax.broadcasted_iota(jnp.int32, (hubs, slot_total), 1).astype(F32)
    hub_hit = lax.broadcasted_iota(jnp.int32, (hubs, slot_total), 0).astype(F32) == rank
    hub_index = jnp.sum(jnp.where(hub_hit, lane_index, 0.0), axis=1, keepdims=True)
    hub_slot = jnp.sum(jnp.where(hub_hit, slots, 0.0), axis=1, keepdims=True)
    hub_here = jnp.logical_and(hub_slot >= base, hub_slot < base + float(pair))
    hub_far = jnp.where(hub_here, -5.0, hub_index)
    hub_near = jnp.where(hub_here, hub_index, -5.0)

    place = lax.broadcasted_iota(jnp.int32, (pair, slot_total), 0).astype(F32) + base
    lanes = lax.broadcasted_iota(jnp.int32, (pair, slot_total), 1).astype(F32)
    own_index = jnp.sum(jnp.where(place == slots, lanes, 0.0), axis=1, keepdims=True)

    tail = cols.shape[0] - pair
    far_cols = jnp.concatenate([hub_far, jnp.full((tail - hubs, 1), -5.0, F32)], axis=0)
    far_rows = jnp.concatenate([hub_far, jnp.full((64 - hubs, 1), -5.0, F32)], axis=0)
    cols[0:pair, :] = jnp.where(own_index == colv, 1.0, 0.0).astype(BF16)
    cols[pair:, :] = jnp.where(far_cols == colv, 1.0, 0.0).astype(BF16)
    coded = modes + 1.0
    for index, start, stop in ((own_index, 0, pair), (far_rows, pair, pair + 64)):
        hit = index == rows
        picks[start:stop, :] = jnp.where(hit, weights, 0.0).astype(BF16)
        codes[start:stop, :] = jnp.where(hit, coded, 0.0).astype(BF16)
    weight = lax.dot_general(picks[...], cols[...], NT, preferred_element_type=F32)
    code = lax.dot_general(codes[...], cols[...], NT, preferred_element_type=F32)
    for mode in range(terms):
        table = jnp.where(code == float(mode + 1), weight, 0.0).astype(BF16)
        main_ref[mode] = table[:pair]
        if mode > 0:
            send_ref[mode] = table[pair:, :pair]
    hub_lane = lax.broadcasted_iota(jnp.int32, (pair, cols.shape[0]), 1).astype(F32) - float(pair)
    own_rank = jnp.sum(
        jnp.where(lanes == own_index, rank, 0.0), axis=1, keepdims=True
    )
    main_ref[terms] = jnp.where(
        jnp.logical_and(own_rank >= 0.0, hub_lane == own_rank), 1.0, 0.0
    ).astype(BF16)
    near_rank = lax.broadcasted_iota(jnp.int32, (64, slot_total), 0).astype(F32)
    slot_row = slots
    near_slot = jnp.sum(jnp.where(near_rank == rank, slot_row, 0.0), axis=1, keepdims=True)
    near_has = jnp.sum(jnp.where(near_rank == rank, 1.0, 0.0), axis=1, keepdims=True)
    near_slot = jnp.where(near_has > 0.5, near_slot - base, -5.0)
    send_ref[0] = jnp.where(
        lax.broadcasted_iota(jnp.int32, (64, pair), 1).astype(F32) == near_slot, 1.0, 0.0
    ).astype(BF16)


def edge_kernel(field, near, far, lines, arrived):
    rows = field.shape[1]
    step = field.shape[0] // PIECES
    copies = []
    for k, row in enumerate((0, rows - 1)):
        for piece in range(PIECES):
            cut = pl.ds(piece * step, step)
            copies.append(
                pltpu.make_async_copy(
                    field.at[cut, row, :], lines.at[k, cut, :], arrived.at[k * PIECES + piece]
                )
            )
    for copy in copies:
        copy.start()
    for copy in copies:
        copy.wait()
    first = core_side() == 0
    near[...] = jnp.where(first, lines[0], lines[1])
    far[...] = jnp.where(first, lines[1], lines[0])


def split_kernel(field, unused, keep, send):
    slots, rows, width = field.shape
    first = core_side() == 0
    for at in range(0, slots, 8):
        lines = jnp.swapaxes(field[at : at + 8], 0, 1)
        for i in range(keep.shape[0]):
            keep[i, at : at + 8, :] = jnp.where(first, lines[i], lines[rows - 1 - i])
            send[i, at : at + 8, :] = jnp.where(first, lines[rows - 1 - i], lines[i])


def across(center):
    return five_point(0.0, center, 0.0)


def five_point(above, center, below):
    width = center.shape[1]
    lane = lax.broadcasted_iota(jnp.int32, center.shape, 1)
    left = jnp.where(lane == 0, 0.0, pltpu.roll(center, 1, 1))
    right = jnp.where(lane == width - 1, 0.0, pltpu.roll(center, width - 1, 1))
    return above + below + left + right - 4.0 * center


def row_place(index, rows):
    return jnp.where(core_side() == 0, index, rows - 1 - index)


def fill_buffer(value_ref, stiff, send_table, buffer, row, place):
    hubs = buffer.shape[1]
    width = buffer.shape[2]
    terms = send_table.shape[0]
    for start in range(0, width, 256):
        cut = slice(start, start + 256)
        value = value_ref[row, :, cut]
        total = jnp.dot(send_table[0], value, preferred_element_type=F32)
        for mode in range(1, terms):
            part = jnp.dot(send_table[mode], value, preferred_element_type=F32)
            total = total + stiff[mode, pl.ds(place, 1), cut] * part
        buffer[row, :, cut] = total[:hubs].astype(BF16)


def first_kernel(first_row, keep, got, stiff, send_table, unused, bent, buffer):
    side = core_side()
    count, pair, width = bent.shape
    own = keep.shape[1]
    for group in range(2):

        def chunk(k, carry):
            at = pl.multiple_of(k * 8, 8)
            cut = pl.ds(at, 8)
            far = pl.ds(group * own + at, 8)
            lines = [
                jnp.where(side == group, keep[row, cut, :], got[row, cut, :])
                for row in range(first_row - 1, first_row + count + 1)
            ]
            for row in range(count):
                value = five_point(lines[row], lines[row + 1], lines[row + 2])
                bent[row, far, :] = value.astype(BF16)
            return carry

        lax.fori_loop(0, own // 8, chunk, 0, unroll=9)
    for row in range(count):
        fill_buffer(bent, stiff, send_table, buffer, row, row_place(first_row + row, stiff.shape[1]))


def first_base_kernel(keep, got, unused, base):
    side = core_side()
    own = keep.shape[1]
    for group in range(2):

        def chunk(k, carry):
            at = pl.multiple_of(k * 8, 8)
            cut = pl.ds(at, 8)
            here, below = [
                jnp.where(side == group, keep[row, cut, :], got[row, cut, :]) for row in range(2)
            ]
            base[pl.ds(group * own + at, 8), :] = across(here) + below
            return carry

        lax.fori_loop(0, own // 8, chunk, 0, unroll=9)


def first_outer_kernel(base, halo_near, halo_far, stiff, send_table, unused, bent, buffer):
    first = core_side() == 0
    own = halo_near.shape[0]
    near, far = halo_near[...], halo_far[...]
    halo = jnp.concatenate([jnp.where(first, near, far), jnp.where(first, far, near)], axis=0)
    bent[0] = (base[...] + halo).astype(BF16)
    fill_buffer(bent, stiff, send_table, buffer, 0, row_place(0, stiff.shape[1]))


def pass_kernel(value, unused, out):
    out[...] = value[...]


def couple_kernel(first, outer_row, inner_rows, bent, got, stiff, table, unused, moment, *rest):
    stacked = rest[-1]
    edges = list(rest[:-1])
    outer = edges.pop(0) if outer_row is not None else None
    inner = edges.pop(0) if inner_rows else None
    count, pair, width = bent.shape
    hubs = got.shape[1]
    terms = stiff.shape[0]
    room = stacked.shape[0]
    stacked[pair + hubs :, :] = jnp.zeros((room - pair - hubs, width), BF16)
    for row in range(count):
        place = row_place(first + row, stiff.shape[1])
        stacked[0:pair, :] = bent[row]
        stacked[pair : pair + hubs, :] = got[row]
        for start in range(0, width, 256):
            cut = slice(start, start + 256)
            value = stacked[:, cut]
            total = jnp.dot(table[terms], value, preferred_element_type=F32)
            for mode in range(terms):
                part = jnp.dot(table[mode], value, preferred_element_type=F32)
                total = total + stiff[mode, pl.ds(place, 1), cut] * part
            moment[row, :, cut] = total
            if first + row == outer_row:
                outer[0, :, cut] = total.astype(BF16)
            if first + row in inner_rows:
                inner[inner_rows.index(first + row), :, cut] = total.astype(BF16)


def share(held, keep, send, rows, own):
    side = core_side()
    near = pl.multiple_of(side * own, 8)
    far = pl.multiple_of((1 - side) * own, 8)
    for target, row in enumerate(rows):
        keep[target] = held[row, pl.ds(near, own), :]
        send[target] = held[row, pl.ds(far, own), :]


def second_inner_kernel(row_zero, row_one, others, inner, stiff, send_table, held, bent, buffer):
    count, pair, width = bent.shape

    def chunk(k, carry):
        cut = pl.ds(pl.multiple_of(k * STEP, STEP), STEP)
        lines = [row_zero[0, cut, :], row_one[0, cut, :]] + [others[row, cut, :] for row in range(2)]
        lines += [inner[row, cut, :].astype(F32) for row in range(2)]
        for row in range(4):
            held[row, cut, :] = five_point(lines[row], lines[row + 1], lines[row + 2])
        for row in range(2):
            value = five_point(
                held[row, cut, :], held[row + 1, cut, :], held[row + 2, cut, :]
            )
            bent[row, cut, :] = value.astype(BF16)
        return carry

    lax.fori_loop(0, pair // STEP, chunk, 0, unroll=9)
    for row in range(count):
        fill_buffer(bent, stiff, send_table, buffer, row, row_place(row + 2, stiff.shape[1]))


def second_base_kernel(row_zero, row_one, held, base, ahead, keep, send):
    pair = row_zero.shape[1]
    tile = lax.axis_index("tile")
    last = lax.axis_size("tile") - 1
    at_edge = jnp.where(core_side() == 0, tile == 0, tile == last)

    def chunk(k, carry):
        cut = pl.ds(pl.multiple_of(k * STEP, STEP), STEP)
        here = row_zero[0, cut, :]
        partial = across(here) + row_one[0, cut, :]
        base[0, cut, :] = partial
        outside = jnp.where(at_edge, 0.0, here)
        ahead[0, cut, :] = five_point(outside, partial, held[0, cut, :])
        return carry

    lax.fori_loop(0, pair // STEP, chunk, 0, unroll=9)
    share(held, keep, send, (0, 1, 2), pair // 2)


def second_edge_kernel(base, ahead, near, next_near, stiff, send_table, zero, bent, buffer):
    pair = bent.shape[1]

    def chunk(k, carry):
        cut = pl.ds(pl.multiple_of(k * STEP, STEP), STEP)
        above = near[0, cut, :].astype(F32)
        zero[0, cut, :] = base[0, cut, :] + above
        value = ahead[0, cut, :] + next_near[0, cut, :].astype(F32) + 2.0 * across(above)
        bent[0, cut, :] = value.astype(BF16)
        return carry

    lax.fori_loop(0, pair // STEP, chunk, 0, unroll=9)
    fill_buffer(bent, stiff, send_table, buffer, 0, row_place(0, stiff.shape[1]))


def second_next_kernel(zero, held, stiff, send_table, unused, keep, send, bent, buffer):
    pair = bent.shape[1]

    def chunk(k, carry):
        cut = pl.ds(pl.multiple_of(k * STEP, STEP), STEP)
        value = five_point(zero[0, cut, :], held[0, cut, :], held[1, cut, :])
        bent[0, cut, :] = value.astype(BF16)
        return carry

    lax.fori_loop(0, pair // STEP, chunk, 0, unroll=9)
    fill_buffer(bent, stiff, send_table, buffer, 0, row_place(1, stiff.shape[1]))
    share(zero, keep, send, (0,), pair // 2)


def last_kernel(zero, one, inners, inner, keep, send):
    side = core_side()
    count, own, width = keep.shape
    for target, group in ((send, 1 - side), (keep, side)):

        def chunk(k, carry):
            at = pl.multiple_of(k * 8, 8)
            cut = pl.ds(pl.multiple_of(group * own + at, 8), 8)
            lines = [jnp.zeros((8, width), F32), zero[0, cut, :], one[0, cut, :]]
            lines += [inners[row, cut, :] for row in range(2)]
            lines += [inner[0, cut, :].astype(F32)]
            for row in range(count):
                target[row, pl.ds(at, 8), :] = five_point(
                    lines[row], lines[row + 1], lines[row + 2]
                )
            return carry

        lax.fori_loop(0, own // 8, chunk, 0, unroll=9)


def write_tiles(near, far, out, lines, done):
    first = core_side() == 0
    half = out.shape[1] // 2
    copies = []
    for k, at in enumerate(range(0, out.shape[0], CHUNK)):
        for start in range(at, at + CHUNK, 8):
            ours = [near(i, slice(start, start + 8)) for i in range(half)]
            theirs = [far(i, slice(start, start + 8)) for i in range(half)]
            rows = [jnp.where(first, a, b) for a, b in zip(ours, theirs)]
            rows += [jnp.where(first, b, a) for a, b in zip(ours[::-1], theirs[::-1])]
            lines[start : start + 8] = jnp.swapaxes(jnp.stack(rows, axis=0), 0, 1)
        cut = pl.ds(at, CHUNK)
        copies.append(pltpu.make_async_copy(lines.at[cut], out.at[cut], done.at[k]))
        copies[-1].start()
    for copy in copies:
        copy.wait()


def merge_kernel(keep_zero, keep, got_zero, got, unused, out, token, lines, done):
    token[...] = jnp.zeros_like(token)

    def near(i, cut):
        return keep_zero[0, cut, :] if i == 0 else keep[i - 1, cut, :]

    def far(i, cut):
        return got_zero[0, cut, :] if i == 0 else got[i - 1, cut, :]

    write_tiles(near, far, out, lines, done)


def halves(halo, own):
    whole = halo[0].astype(F32)
    first = core_side() == 0
    lower, upper = whole[:own], whole[own:]
    return jnp.where(first, lower, upper), jnp.where(first, upper, lower)


def cut_kernel(halo, unused, part):
    part[...] = halves(halo, part.shape[0])[1].astype(BF16)


def last_merge_kernel(keep, got, halo, far_halo, out, lines, done):
    near_line = halves(halo, keep.shape[1])[0]
    far_line = far_halo[...].astype(F32)

    def near(i, cut):
        return keep[0, cut, :] + near_line[cut] if i == 0 else keep[i, cut, :]

    def far(i, cut):
        return got[0, cut, :] + far_line[cut] if i == 0 else got[i, cut, :]

    write_tiles(near, far, out, lines, done)


def body(slot_field, stiffness, triple_modes, triple_rows, triple_cols, triple_weights, slot_of):
    own, rows, width = slot_field.shape
    terms = stiffness.shape[0]
    pair = 2 * own
    half = rows // 2
    chaos = lax.axis_size("chaos")
    tiles = lax.axis_size("tile")
    slot_total = own * chaos
    modes = terms - 1
    hubs = 1 + modes * (modes + 1) // 2
    room = -(-(pair + hubs) // 16) * 16
    side = core_side()

    core_swap = [(i, i ^ 1) for i in range(chaos)]
    chip_swap = [(i, i ^ 2) for i in range(chaos)]
    tile_swap = []
    for high in range(0, chaos, 2):
        for tile in range(tiles - 1):
            one, two = (high + 1) * tiles + tile, high * tiles + tile + 1
            tile_swap += [(one, two), (two, one)]

    def by_core(value):
        return lax.ppermute(value, "chaos", core_swap)

    def by_chip(value):
        return lax.ppermute(value, "chaos", chip_swap)

    def by_tile(value):
        return lax.ppermute(value, ("chaos", "tile"), tile_swap)

    count = triple_modes.shape[0]
    wide = -(-count // 128) * 128

    def line(value, fill):
        value = value.astype(F32)
        return jnp.pad(value, (0, wide - value.shape[0]), constant_values=fill)

    entries = jnp.stack(
        [
            line(triple_modes, -1.0),
            line(triple_rows, -1.0),
            line(triple_cols, -1.0),
            line(triple_weights, 0.0),
            line(slot_of, -1.0),
        ]
        + [jnp.zeros((wide,), F32)] * 3
    )
    row_block = shape((own, width), F32)
    near_edge, far_edge = call(
        edge_kernel,
        (row_block, row_block),
        [pltpu.VMEM((2, own, width), F32), pltpu.SemaphoreType.DMA((2 * PIECES,))],
        2.0,
        [ANY],
        60,
    )(slot_field)
    halo_far = by_tile(near_edge)
    got_edge = by_core(far_edge)
    halo_near = by_tile(got_edge)

    main_table, send_table = call(
        functools.partial(table_kernel, terms, pair, hubs, slot_total),
        (shape((terms + 1, pair, room), BF16), shape((terms, 64, pair), BF16)),
        [
            pltpu.VMEM((pair + 64, wide), BF16),
            pltpu.VMEM((pair + 64, wide), BF16),
            pltpu.VMEM((room, wide), BF16),
        ],
        3.0,
        [VMEM, ANY],
        12,
    )(entries, got_edge)

    line_block = shape((half + 1, own, width), F32)
    keep, send = call(split_kernel, (line_block, line_block), (), 2.5, [VMEM, ANY])(
        slot_field, got_edge
    )
    got = by_core(send)

    def bents(count):
        return (shape((count, pair, width), BF16), shape((count, hubs, width), BF16))

    def outs(count):
        return (shape((count, own, width), F32),) * 2

    def bend(first, count, after):
        bent, buffer = call(
            functools.partial(first_kernel, first), bents(count), (), 0.9 * count, [VMEM] * 4 + [ANY]
        )(keep, got, stiffness, send_table, after)
        return bent, buffer, by_chip(buffer)

    def couple(bent, other, first, outer_row, inner_rows, after, weight=1.0):
        count = bent.shape[0]
        out = [shape((count, pair, width), F32)]
        if outer_row is not None:
            out.append(shape((1, pair, width), BF16))
        if inner_rows:
            out.append(shape((len(inner_rows), pair, width), BF16))
        return call(
            functools.partial(couple_kernel, first, outer_row, inner_rows),
            tuple(out),
            [pltpu.VMEM((room, width), BF16)],
            weight * count,
            [VMEM] * 4 + [ANY],
        )(bent, other, stiffness, main_table, after)

    bent_one, sent, cross_one = bend(1, 1, got)
    bent_in, sent, cross_in = bend(2, 2, sent)
    base = call(first_base_kernel, shape((pair, width), F32), (), 0.4, [VMEM] * 2 + [ANY])(
        keep, got, sent
    )
    moment_one, edge_one = couple(bent_one, cross_one, 1, 1, (), base)
    bent_out, sent = call(first_outer_kernel, bents(1), (), 0.9, [VMEM] * 5 + [ANY])(
        base, halo_near, halo_far, stiffness, send_table, edge_one
    )
    cross_out = by_chip(sent)
    edge_one = call(pass_kernel, shape(edge_one.shape, BF16), (), 0.1, [VMEM, ANY])(edge_one, sent)
    next_near = by_tile(edge_one)
    moment_in, edge_in = couple(bent_in, cross_in, 2, None, (3, 2), edge_one)
    inner = by_core(edge_in)
    moment_out, edge_zero = couple(bent_out, cross_out, 0, 0, (), edge_in)
    near = by_tile(edge_zero)

    row_shape = shape((1, pair, width), F32)
    held, bent_in, buffer_in = call(
        second_inner_kernel, (shape((4, pair, width), F32),) + bents(2), (), 2.7
    )(moment_out, moment_one, moment_in, inner, stiffness, send_table)
    base, ahead, keep_in, send_in = call(
        second_base_kernel, (row_shape, row_shape) + outs(3), (), 3.0
    )(moment_out, moment_one, held)
    got_in = by_core(send_in)
    cross_in = by_chip(buffer_in)
    zero, bent_out, buffer_out = call(second_edge_kernel, (row_shape,) + bents(1), (), EARLY)(
        base, ahead, near, next_near, stiffness, send_table
    )
    cross_out = by_chip(buffer_out)
    keep_out, send_out, bent_one, buffer_one = call(
        second_next_kernel, outs(1) + bents(1), (), EARLY, [VMEM] * 4 + [ANY]
    )(zero, held, stiffness, send_table, cross_in)
    cross_one = by_chip(buffer_one)
    got_out = by_core(send_out)
    moment_out, edge_zero = couple(bent_out, cross_out, 0, 0, (), buffer_one)
    near = by_tile(edge_zero)
    moment_in, inner = couple(bent_in, cross_in, 2, None, (3,), edge_zero)
    inner = by_core(inner)
    (moment_one,) = couple(bent_one, cross_one, 1, None, (), edge_zero)

    keep, send = call(last_kernel, outs(half), (), 2.5)(
        moment_out, moment_one, moment_in, inner
    )
    got = by_core(send)
    whole = shape(slot_field.shape, F32)
    writers = [pltpu.VMEM(slot_field.shape, F32), pltpu.SemaphoreType.DMA((own // CHUNK,))]
    first_apply, token = call(
        merge_kernel, (whole, TOKEN), writers, 1.9, [VMEM] * 4 + [ANY], 6, (ANY, VMEM)
    )(keep_out, keep_in, got_out, got_in, keep)
    far_halo = by_core(
        call(cut_kernel, shape((own, width), BF16), (), 0.3, [VMEM, ANY])(near, token)
    )
    second_apply = call(last_merge_kernel, whole, writers, 1.9, [VMEM] * 4, 6, ANY)(
        keep, got, near, far_halo
    )
    return first_apply, second_apply


def solution(mesh):
    return jax.shard_map(
        body,
        mesh=mesh,
        in_specs=(P("chaos", "tile", None), P(None, "tile", None), P(), P(), P(), P(), P()),
        out_specs=(P("chaos", "tile", None), P("chaos", "tile", None)),
        check_vma=False,
    )
```

```python
import functools
import jax
import jax.numpy as jnp
from jax import lax
from jax.experimental import pallas as pl
from jax.experimental.pallas import tpu as pltpu
from jax.sharding import PartitionSpec as P

F32, BF16 = jnp.float32, jnp.bfloat16
VMEM = pl.BlockSpec(memory_space=pltpu.VMEM)
TOKEN = jax.ShapeDtypeStruct((8, 128), jnp.int32)
ANY = pl.BlockSpec(memory_space=pl.ANY)
NT = (((1,), (1,)), ((), ()))
STEP = 16
CHUNK = 8
PIECES = 1
EARLY = 0.01


def call(kernel, outs, scratch=(), us=1.0, specs=None, room=12, into=None):
    extra = {} if specs is None else {"in_specs": specs}
    if into is not None:
        extra["out_specs"] = into
    return pl.pallas_call(
        kernel,
        out_shape=outs,
        scratch_shapes=scratch,
        compiler_params=pltpu.CompilerParams(vmem_limit_bytes=room * 1024 * 1024),
        cost_estimate=pl.CostEstimate(
            flops=int(us * 1e10), bytes_accessed=10, transcendentals=0
        ),
        **extra,
    )


def shape(dims, kind):
    return jax.ShapeDtypeStruct(dims, kind)


def core_side():
    return lax.rem(lax.axis_index("chaos"), 2)


def table_kernel(
    terms, pair, hubs, slot_total, entries, unused, main_ref, send_ref, picks, codes, cols
):
    wide = entries.shape[1]
    modes = entries[0:1, :]
    rows = entries[1:2, :]
    colv = entries[2:3, :]
    weights = entries[3:4, :]
    slots = entries[4:5, :slot_total]
    chip = lax.axis_index("chaos") // 2
    base = (chip * pair).astype(F32)

    index_col = lax.broadcasted_iota(jnp.int32, (slot_total, wide), 0).astype(F32)
    row_hot = jnp.where(index_col == rows, 1.0, 0.0).astype(BF16)
    col_hot = jnp.where(index_col == colv, 1.0, 0.0).astype(BF16)
    ones = jnp.ones((8, wide), BF16)
    degree = lax.dot_general(ones, row_hot, NT, preferred_element_type=F32)
    zeroth = jnp.where(degree == float(terms), 1.0, 0.0)
    col_zeroth = lax.dot_general(
        zeroth.astype(BF16), col_hot, (((1,), (0,)), ((), ())), preferred_element_type=F32
    )
    beside = lax.dot_general(col_zeroth.astype(BF16), row_hot, NT, preferred_element_type=F32)
    even = jnp.where(degree > 5.0, jnp.where(beside > 0.5, zeroth, 1.0), 0.0)
    before = jnp.where(
        lax.broadcasted_iota(jnp.int32, (slot_total, slot_total), 0)
        < lax.broadcasted_iota(jnp.int32, (slot_total, slot_total), 1),
        1.0,
        0.0,
    ).astype(BF16)
    rank = lax.dot_general(
        even.astype(BF16), before, (((1,), (0,)), ((), ())), preferred_element_type=F32
    )
    rank = jnp.where(even > 0.5, rank, -1.0)[0:1, :]
    lane_index = lax.broadcasted_iota(jnp.int32, (hubs, slot_total), 1).astype(F32)
    hub_hit = lax.broadcasted_iota(jnp.int32, (hubs, slot_total), 0).astype(F32) == rank
    hub_index = jnp.sum(jnp.where(hub_hit, lane_index, 0.0), axis=1, keepdims=True)
    hub_slot = jnp.sum(jnp.where(hub_hit, slots, 0.0), axis=1, keepdims=True)
    hub_here = jnp.logical_and(hub_slot >= base, hub_slot < base + float(pair))
    hub_far = jnp.where(hub_here, -5.0, hub_index)
    hub_near = jnp.where(hub_here, hub_index, -5.0)

    place = lax.broadcasted_iota(jnp.int32, (pair, slot_total), 0).astype(F32) + base
    lanes = lax.broadcasted_iota(jnp.int32, (pair, slot_total), 1).astype(F32)
    own_index = jnp.sum(jnp.where(place == slots, lanes, 0.0), axis=1, keepdims=True)

    tail = cols.shape[0] - pair
    far_cols = jnp.concatenate([hub_far, jnp.full((tail - hubs, 1), -5.0, F32)], axis=0)
    far_rows = jnp.concatenate([hub_far, jnp.full((64 - hubs, 1), -5.0, F32)], axis=0)
    cols[0:pair, :] = jnp.where(own_index == colv, 1.0, 0.0).astype(BF16)
    cols[pair:, :] = jnp.where(far_cols == colv, 1.0, 0.0).astype(BF16)
    coded = modes + 1.0
    for index, start, stop in ((own_index, 0, pair), (far_rows, pair, pair + 64)):
        hit = index == rows
        picks[start:stop, :] = jnp.where(hit, weights, 0.0).astype(BF16)
        codes[start:stop, :] = jnp.where(hit, coded, 0.0).astype(BF16)
    weight = lax.dot_general(picks[...], cols[...], NT, preferred_element_type=F32)
    code = lax.dot_general(codes[...], cols[...], NT, preferred_element_type=F32)
    for mode in range(terms):
        table = jnp.where(code == float(mode + 1), weight, 0.0).astype(BF16)
        main_ref[mode] = table[:pair]
        if mode > 0:
            send_ref[mode] = table[pair:, :pair]
    hub_lane = lax.broadcasted_iota(jnp.int32, (pair, cols.shape[0]), 1).astype(F32) - float(pair)
    own_rank = jnp.sum(
        jnp.where(lanes == own_index, rank, 0.0), axis=1, keepdims=True
    )
    main_ref[terms] = jnp.where(
        jnp.logical_and(own_rank >= 0.0, hub_lane == own_rank), 1.0, 0.0
    ).astype(BF16)
    near_rank = lax.broadcasted_iota(jnp.int32, (64, slot_total), 0).astype(F32)
    slot_row = slots
    near_slot = jnp.sum(jnp.where(near_rank == rank, slot_row, 0.0), axis=1, keepdims=True)
    near_has = jnp.sum(jnp.where(near_rank == rank, 1.0, 0.0), axis=1, keepdims=True)
    near_slot = jnp.where(near_has > 0.5, near_slot - base, -5.0)
    send_ref[0] = jnp.where(
        lax.broadcasted_iota(jnp.int32, (64, pair), 1).astype(F32) == near_slot, 1.0, 0.0
    ).astype(BF16)


def edge_kernel(field, near, far, lines, arrived):
    rows = field.shape[1]
    step = field.shape[0] // PIECES
    copies = []
    for k, row in enumerate((0, rows - 1)):
        for piece in range(PIECES):
            cut = pl.ds(piece * step, step)
            copies.append(
                pltpu.make_async_copy(
                    field.at[cut, row, :], lines.at[k, cut, :], arrived.at[k * PIECES + piece]
                )
            )
    for copy in copies:
        copy.start()
    for copy in copies:
        copy.wait()
    first = core_side() == 0
    near[...] = jnp.where(first, lines[0], lines[1])
    far[...] = jnp.where(first, lines[1], lines[0])


def split_kernel(field, unused, keep, send):
    slots, rows, width = field.shape
    first = core_side() == 0
    for at in range(0, slots, 8):
        lines = jnp.swapaxes(field[at : at + 8], 0, 1)
        for i in range(keep.shape[0]):
            keep[i, at : at + 8, :] = jnp.where(first, lines[i], lines[rows - 1 - i])
            send[i, at : at + 8, :] = jnp.where(first, lines[rows - 1 - i], lines[i])


def across(center):
    return five_point(0.0, center, 0.0)


def five_point(above, center, below):
    width = center.shape[1]
    lane = lax.broadcasted_iota(jnp.int32, center.shape, 1)
    left = jnp.where(lane == 0, 0.0, pltpu.roll(center, 1, 1))
    right = jnp.where(lane == width - 1, 0.0, pltpu.roll(center, width - 1, 1))
    return above + below + left + right - 4.0 * center


def row_place(index, rows):
    return jnp.where(core_side() == 0, index, rows - 1 - index)


def fill_buffer(value_ref, stiff, send_table, buffer, row, place):
    hubs = buffer.shape[1]
    width = buffer.shape[2]
    terms, deep, pair = send_table.shape
    lines = send_table[...].reshape(terms * deep, pair)
    for start in range(0, width, 256):
        cut = slice(start, start + 256)
        value = value_ref[row, :, cut]
        parts = jnp.dot(lines, value, preferred_element_type=F32)
        total = parts[:deep]
        for mode in range(1, terms):
            part = parts[mode * deep : (mode + 1) * deep]
            total = total + stiff[mode, pl.ds(place, 1), cut] * part
        buffer[row, :, cut] = total[:hubs].astype(BF16)


def first_kernel(first_row, keep, got, stiff, send_table, unused, bent, buffer):
    side = core_side()
    count, pair, width = bent.shape
    own = keep.shape[1]
    for group in range(2):

        def chunk(k, carry):
            at = pl.multiple_of(k * 8, 8)
            cut = pl.ds(at, 8)
            far = pl.ds(group * own + at, 8)
            lines = [
                jnp.where(side == group, keep[row, cut, :], got[row, cut, :])
                for row in range(first_row - 1, first_row + count + 1)
            ]
            for row in range(count):
                value = five_point(lines[row], lines[row + 1], lines[row + 2])
                bent[row, far, :] = value.astype(BF16)
            return carry

        lax.fori_loop(0, own // 8, chunk, 0, unroll=9)
    for row in range(count):
        fill_buffer(bent, stiff, send_table, buffer, row, row_place(first_row + row, stiff.shape[1]))


def first_base_kernel(keep, got, unused, base):
    side = core_side()
    own = keep.shape[1]
    for group in range(2):

        def chunk(k, carry):
            at = pl.multiple_of(k * 8, 8)
            cut = pl.ds(at, 8)
            here, below = [
                jnp.where(side == group, keep[row, cut, :], got[row, cut, :]) for row in range(2)
            ]
            base[pl.ds(group * own + at, 8), :] = across(here) + below
            return carry

        lax.fori_loop(0, own // 8, chunk, 0, unroll=9)


def first_outer_kernel(base, halo_near, halo_far, stiff, send_table, unused, bent, buffer):
    first = core_side() == 0
    own = halo_near.shape[0]
    near, far = halo_near[...], halo_far[...]
    halo = jnp.concatenate([jnp.where(first, near, far), jnp.where(first, far, near)], axis=0)
    bent[0] = (base[...] + halo).astype(BF16)
    fill_buffer(bent, stiff, send_table, buffer, 0, row_place(0, stiff.shape[1]))


def pass_kernel(value, unused, out):
    out[...] = value[...]


def couple_kernel(first, outer_row, inner_rows, bent, got, stiff, table, unused, moment, *rest):
    stacked = rest[-1]
    edges = list(rest[:-1])
    outer = edges.pop(0) if outer_row is not None else None
    inner = edges.pop(0) if inner_rows else None
    count, pair, width = bent.shape
    hubs = got.shape[1]
    terms = stiff.shape[0]
    room = stacked.shape[0]
    stacked[pair + hubs :, :] = jnp.zeros((room - pair - hubs, width), BF16)
    for row in range(count):
        place = row_place(first + row, stiff.shape[1])
        stacked[0:pair, :] = bent[row]
        stacked[pair : pair + hubs, :] = got[row]
        for start in range(0, width, 256):
            cut = slice(start, start + 256)
            value = stacked[:, cut]
            total = jnp.dot(table[terms], value, preferred_element_type=F32)
            for mode in range(terms):
                part = jnp.dot(table[mode], value, preferred_element_type=F32)
                total = total + stiff[mode, pl.ds(place, 1), cut] * part
            moment[row, :, cut] = total
            if first + row == outer_row:
                outer[0, :, cut] = total.astype(BF16)
            if first + row in inner_rows:
                inner[inner_rows.index(first + row), :, cut] = total.astype(BF16)


def share(held, keep, send, rows, own):
    side = core_side()
    near = pl.multiple_of(side * own, 8)
    far = pl.multiple_of((1 - side) * own, 8)
    for target, row in enumerate(rows):
        keep[target] = held[row, pl.ds(near, own), :]
        send[target] = held[row, pl.ds(far, own), :]


def second_inner_kernel(row_zero, row_one, others, inner, stiff, send_table, held, bent, buffer):
    count, pair, width = bent.shape

    def chunk(k, carry):
        cut = pl.ds(pl.multiple_of(k * STEP, STEP), STEP)
        lines = [row_zero[0, cut, :], row_one[0, cut, :]] + [others[row, cut, :] for row in range(2)]
        lines += [inner[row, cut, :].astype(F32) for row in range(2)]
        for row in range(4):
            held[row, cut, :] = five_point(lines[row], lines[row + 1], lines[row + 2])
        for row in range(2):
            value = five_point(
                held[row, cut, :], held[row + 1, cut, :], held[row + 2, cut, :]
            )
            bent[row, cut, :] = value.astype(BF16)
        return carry

    lax.fori_loop(0, pair // STEP, chunk, 0, unroll=9)
    for row in range(count):
        fill_buffer(bent, stiff, send_table, buffer, row, row_place(row + 2, stiff.shape[1]))


def second_base_kernel(row_zero, row_one, held, base, ahead, keep, send):
    pair = row_zero.shape[1]
    tile = lax.axis_index("tile")
    last = lax.axis_size("tile") - 1
    at_edge = jnp.where(core_side() == 0, tile == 0, tile == last)

    def chunk(k, carry):
        cut = pl.ds(pl.multiple_of(k * STEP, STEP), STEP)
        here = row_zero[0, cut, :]
        partial = across(here) + row_one[0, cut, :]
        base[0, cut, :] = partial
        outside = jnp.where(at_edge, 0.0, here)
        ahead[0, cut, :] = five_point(outside, partial, held[0, cut, :])
        return carry

    lax.fori_loop(0, pair // STEP, chunk, 0, unroll=9)
    share(held, keep, send, (0, 1, 2), pair // 2)


def second_edge_kernel(base, ahead, near, next_near, stiff, send_table, zero, bent, buffer):
    pair = bent.shape[1]

    def chunk(k, carry):
        cut = pl.ds(pl.multiple_of(k * STEP, STEP), STEP)
        above = near[0, cut, :].astype(F32)
        zero[0, cut, :] = base[0, cut, :] + above
        value = ahead[0, cut, :] + next_near[0, cut, :].astype(F32) + 2.0 * across(above)
        bent[0, cut, :] = value.astype(BF16)
        return carry

    lax.fori_loop(0, pair // STEP, chunk, 0, unroll=9)
    fill_buffer(bent, stiff, send_table, buffer, 0, row_place(0, stiff.shape[1]))


def second_next_kernel(zero, held, stiff, send_table, unused, keep, send, bent, buffer):
    pair = bent.shape[1]

    def chunk(k, carry):
        cut = pl.ds(pl.multiple_of(k * STEP, STEP), STEP)
        value = five_point(zero[0, cut, :], held[0, cut, :], held[1, cut, :])
        bent[0, cut, :] = value.astype(BF16)
        return carry

    lax.fori_loop(0, pair // STEP, chunk, 0, unroll=9)
    fill_buffer(bent, stiff, send_table, buffer, 0, row_place(1, stiff.shape[1]))
    share(zero, keep, send, (0,), pair // 2)


def last_kernel(zero, one, inners, inner, keep, send):
    side = core_side()
    count, own, width = keep.shape
    for target, group in ((send, 1 - side), (keep, side)):

        def chunk(k, carry):
            at = pl.multiple_of(k * 8, 8)
            cut = pl.ds(pl.multiple_of(group * own + at, 8), 8)
            lines = [jnp.zeros((8, width), F32), zero[0, cut, :], one[0, cut, :]]
            lines += [inners[row, cut, :] for row in range(2)]
            lines += [inner[0, cut, :].astype(F32)]
            for row in range(count):
                target[row, pl.ds(at, 8), :] = five_point(
                    lines[row], lines[row + 1], lines[row + 2]
                )
            return carry

        lax.fori_loop(0, own // 8, chunk, 0, unroll=9)


def write_tiles(near, far, out, lines, done):
    first = core_side() == 0
    half = out.shape[1] // 2
    copies = []
    for k, at in enumerate(range(0, out.shape[0], CHUNK)):
        for start in range(at, at + CHUNK, 8):
            ours = [near(i, slice(start, start + 8)) for i in range(half)]
            theirs = [far(i, slice(start, start + 8)) for i in range(half)]
            rows = [jnp.where(first, a, b) for a, b in zip(ours, theirs)]
            rows += [jnp.where(first, b, a) for a, b in zip(ours[::-1], theirs[::-1])]
            lines[start : start + 8] = jnp.swapaxes(jnp.stack(rows, axis=0), 0, 1)
        cut = pl.ds(at, CHUNK)
        copies.append(pltpu.make_async_copy(lines.at[cut], out.at[cut], done.at[k]))
        copies[-1].start()
    for copy in copies:
        copy.wait()


def merge_kernel(keep_zero, keep, got_zero, got, unused, out, token, lines, done):
    token[...] = jnp.zeros_like(token)

    def near(i, cut):
        return keep_zero[0, cut, :] if i == 0 else keep[i - 1, cut, :]

    def far(i, cut):
        return got_zero[0, cut, :] if i == 0 else got[i - 1, cut, :]

    write_tiles(near, far, out, lines, done)


def halves(halo, own):
    whole = halo[0].astype(F32)
    first = core_side() == 0
    lower, upper = whole[:own], whole[own:]
    return jnp.where(first, lower, upper), jnp.where(first, upper, lower)


def cut_kernel(halo, unused, part):
    part[...] = halves(halo, part.shape[0])[1].astype(BF16)


def last_merge_kernel(keep, got, halo, far_halo, out, lines, done):
    near_line = halves(halo, keep.shape[1])[0]
    far_line = far_halo[...].astype(F32)

    def near(i, cut):
        return keep[0, cut, :] + near_line[cut] if i == 0 else keep[i, cut, :]

    def far(i, cut):
        return got[0, cut, :] + far_line[cut] if i == 0 else got[i, cut, :]

    write_tiles(near, far, out, lines, done)


def body(slot_field, stiffness, triple_modes, triple_rows, triple_cols, triple_weights, slot_of):
    own, rows, width = slot_field.shape
    terms = stiffness.shape[0]
    pair = 2 * own
    half = rows // 2
    chaos = lax.axis_size("chaos")
    tiles = lax.axis_size("tile")
    slot_total = own * chaos
    modes = terms - 1
    hubs = 1 + modes * (modes + 1) // 2
    room = -(-(pair + hubs) // 16) * 16
    side = core_side()

    core_swap = [(i, i ^ 1) for i in range(chaos)]
    chip_swap = [(i, i ^ 2) for i in range(chaos)]
    tile_swap = []
    for high in range(0, chaos, 2):
        for tile in range(tiles - 1):
            one, two = (high + 1) * tiles + tile, high * tiles + tile + 1
            tile_swap += [(one, two), (two, one)]

    def by_core(value):
        return lax.ppermute(value, "chaos", core_swap)

    def by_chip(value):
        return lax.ppermute(value, "chaos", chip_swap)

    def by_tile(value):
        return lax.ppermute(value, ("chaos", "tile"), tile_swap)

    count = triple_modes.shape[0]
    wide = -(-count // 128) * 128

    def line(value, fill):
        value = value.astype(F32)
        return jnp.pad(value, (0, wide - value.shape[0]), constant_values=fill)

    entries = jnp.stack(
        [
            line(triple_modes, -1.0),
            line(triple_rows, -1.0),
            line(triple_cols, -1.0),
            line(triple_weights, 0.0),
            line(slot_of, -1.0),
        ]
        + [jnp.zeros((wide,), F32)] * 3
    )
    row_block = shape((own, width), F32)
    near_edge, far_edge = call(
        edge_kernel,
        (row_block, row_block),
        [pltpu.VMEM((2, own, width), F32), pltpu.SemaphoreType.DMA((2 * PIECES,))],
        2.0,
        [ANY],
        60,
    )(slot_field)
    halo_far = by_tile(near_edge)
    got_edge = by_core(far_edge)
    halo_near = by_tile(got_edge)

    main_table, send_table = call(
        functools.partial(table_kernel, terms, pair, hubs, slot_total),
        (shape((terms + 1, pair, room), BF16), shape((terms, 64, pair), BF16)),
        [
            pltpu.VMEM((pair + 64, wide), BF16),
            pltpu.VMEM((pair + 64, wide), BF16),
            pltpu.VMEM((room, wide), BF16),
        ],
        3.0,
        [VMEM, ANY],
        12,
    )(entries, got_edge)

    line_block = shape((half + 1, own, width), F32)
    keep, send = call(split_kernel, (line_block, line_block), (), 2.5, [VMEM, ANY])(
        slot_field, got_edge
    )
    got = by_core(send)

    def bents(count):
        return (shape((count, pair, width), BF16), shape((count, hubs, width), BF16))

    def outs(count):
        return (shape((count, own, width), F32),) * 2

    def bend(first, count, after):
        bent, buffer = call(
            functools.partial(first_kernel, first), bents(count), (), 0.9 * count, [VMEM] * 4 + [ANY]
        )(keep, got, stiffness, send_table, after)
        return bent, buffer, by_chip(buffer)

    def couple(bent, other, first, outer_row, inner_rows, after, weight=1.0):
        count = bent.shape[0]
        out = [shape((count, pair, width), F32)]
        if outer_row is not None:
            out.append(shape((1, pair, width), BF16))
        if inner_rows:
            out.append(shape((len(inner_rows), pair, width), BF16))
        return call(
            functools.partial(couple_kernel, first, outer_row, inner_rows),
            tuple(out),
            [pltpu.VMEM((room, width), BF16)],
            weight * count,
            [VMEM] * 4 + [ANY],
        )(bent, other, stiffness, main_table, after)

    bent_one, sent, cross_one = bend(1, 1, got)
    bent_in, sent, cross_in = bend(2, 2, sent)
    base = call(first_base_kernel, shape((pair, width), F32), (), 0.4, [VMEM] * 2 + [ANY])(
        keep, got, sent
    )
    moment_one, edge_one = couple(bent_one, cross_one, 1, 1, (), base)
    bent_out, sent = call(first_outer_kernel, bents(1), (), 0.9, [VMEM] * 5 + [ANY])(
        base, halo_near, halo_far, stiffness, send_table, edge_one
    )
    cross_out = by_chip(sent)
    edge_one = call(pass_kernel, shape(edge_one.shape, BF16), (), 0.1, [VMEM, ANY])(edge_one, sent)
    next_near = by_tile(edge_one)
    moment_in, edge_in = couple(bent_in, cross_in, 2, None, (3, 2), edge_one)
    inner = by_core(edge_in)
    moment_out, edge_zero = couple(bent_out, cross_out, 0, 0, (), edge_in)
    near = by_tile(edge_zero)

    row_shape = shape((1, pair, width), F32)
    held, bent_in, buffer_in = call(
        second_inner_kernel, (shape((4, pair, width), F32),) + bents(2), (), 2.7
    )(moment_out, moment_one, moment_in, inner, stiffness, send_table)
    base, ahead, keep_in, send_in = call(
        second_base_kernel, (row_shape, row_shape) + outs(3), (), 3.0
    )(moment_out, moment_one, held)
    got_in = by_core(send_in)
    cross_in = by_chip(buffer_in)
    zero, bent_out, buffer_out = call(second_edge_kernel, (row_shape,) + bents(1), (), EARLY)(
        base, ahead, near, next_near, stiffness, send_table
    )
    cross_out = by_chip(buffer_out)
    keep_out, send_out, bent_one, buffer_one = call(
        second_next_kernel, outs(1) + bents(1), (), EARLY, [VMEM] * 4 + [ANY]
    )(zero, held, stiffness, send_table, cross_in)
    cross_one = by_chip(buffer_one)
    got_out = by_core(send_out)
    moment_out, edge_zero = couple(bent_out, cross_out, 0, 0, (), buffer_one)
    near = by_tile(edge_zero)
    moment_in, inner = couple(bent_in, cross_in, 2, None, (3,), edge_zero)
    inner = by_core(inner)
    (moment_one,) = couple(bent_one, cross_one, 1, None, (), edge_zero)

    keep, send = call(last_kernel, outs(half), (), 2.5)(
        moment_out, moment_one, moment_in, inner
    )
    got = by_core(send)
    whole = shape(slot_field.shape, F32)
    writers = [pltpu.VMEM(slot_field.shape, F32), pltpu.SemaphoreType.DMA((own // CHUNK,))]
    first_apply, token = call(
        merge_kernel, (whole, TOKEN), writers, 1.9, [VMEM] * 4 + [ANY], 6, (ANY, VMEM)
    )(keep_out, keep_in, got_out, got_in, keep)
    far_halo = by_core(
        call(cut_kernel, shape((own, width), BF16), (), 0.3, [VMEM, ANY])(near, token)
    )
    second_apply = call(last_merge_kernel, whole, writers, 1.9, [VMEM] * 4, 6, ANY)(
        keep, got, near, far_halo
    )
    return first_apply, second_apply


def solution(mesh):
    return jax.shard_map(
        body,
        mesh=mesh,
        in_specs=(P("chaos", "tile", None), P(None, "tile", None), P(), P(), P(), P(), P()),
        out_specs=(P("chaos", "tile", None), P("chaos", "tile", None)),
        check_vma=False,
    )
```

```python
import functools
import jax
import jax.numpy as jnp
from jax import lax
from jax.experimental import pallas as pl
from jax.experimental.pallas import tpu as pltpu
from jax.sharding import PartitionSpec as P

F32, BF16 = jnp.float32, jnp.bfloat16
VMEM = pl.BlockSpec(memory_space=pltpu.VMEM)
TOKEN = jax.ShapeDtypeStruct((8, 128), jnp.int32)
ANY = pl.BlockSpec(memory_space=pl.ANY)
NT = (((1,), (1,)), ((), ()))
STEP = 16
CHUNK = 8
PIECES = 1
EARLY = 0.01


def call(kernel, outs, scratch=(), us=1.0, specs=None, room=12, into=None):
    extra = {} if specs is None else {"in_specs": specs}
    if into is not None:
        extra["out_specs"] = into
    return pl.pallas_call(
        kernel,
        out_shape=outs,
        scratch_shapes=scratch,
        compiler_params=pltpu.CompilerParams(vmem_limit_bytes=room * 1024 * 1024),
        cost_estimate=pl.CostEstimate(
            flops=int(us * 1e10), bytes_accessed=10, transcendentals=0
        ),
        **extra,
    )


def shape(dims, kind):
    return jax.ShapeDtypeStruct(dims, kind)


def core_side():
    return lax.rem(lax.axis_index("chaos"), 2)


def table_kernel(
    terms, pair, hubs, slot_total, entries, unused, main_ref, send_ref, picks, codes, cols
):
    wide = entries.shape[1]
    modes = entries[0:1, :]
    rows = entries[1:2, :]
    colv = entries[2:3, :]
    weights = entries[3:4, :]
    slots = entries[4:5, :slot_total]
    chip = lax.axis_index("chaos") // 2
    base = (chip * pair).astype(F32)

    index_col = lax.broadcasted_iota(jnp.int32, (slot_total, wide), 0).astype(F32)
    row_hot = jnp.where(index_col == rows, 1.0, 0.0).astype(BF16)
    col_hot = jnp.where(index_col == colv, 1.0, 0.0).astype(BF16)
    ones = jnp.ones((8, wide), BF16)
    degree = lax.dot_general(ones, row_hot, NT, preferred_element_type=F32)
    zeroth = jnp.where(degree == float(terms), 1.0, 0.0)
    col_zeroth = lax.dot_general(
        zeroth.astype(BF16), col_hot, (((1,), (0,)), ((), ())), preferred_element_type=F32
    )
    beside = lax.dot_general(col_zeroth.astype(BF16), row_hot, NT, preferred_element_type=F32)
    even = jnp.where(degree > 5.0, jnp.where(beside > 0.5, zeroth, 1.0), 0.0)
    before = jnp.where(
        lax.broadcasted_iota(jnp.int32, (slot_total, slot_total), 0)
        < lax.broadcasted_iota(jnp.int32, (slot_total, slot_total), 1),
        1.0,
        0.0,
    ).astype(BF16)
    rank = lax.dot_general(
        even.astype(BF16), before, (((1,), (0,)), ((), ())), preferred_element_type=F32
    )
    rank = jnp.where(even > 0.5, rank, -1.0)[0:1, :]
    lane_index = lax.broadcasted_iota(jnp.int32, (hubs, slot_total), 1).astype(F32)
    hub_hit = lax.broadcasted_iota(jnp.int32, (hubs, slot_total), 0).astype(F32) == rank
    hub_index = jnp.sum(jnp.where(hub_hit, lane_index, 0.0), axis=1, keepdims=True)
    hub_slot = jnp.sum(jnp.where(hub_hit, slots, 0.0), axis=1, keepdims=True)
    hub_here = jnp.logical_and(hub_slot >= base, hub_slot < base + float(pair))
    hub_far = jnp.where(hub_here, -5.0, hub_index)
    hub_near = jnp.where(hub_here, hub_index, -5.0)

    place = lax.broadcasted_iota(jnp.int32, (pair, slot_total), 0).astype(F32) + base
    lanes = lax.broadcasted_iota(jnp.int32, (pair, slot_total), 1).astype(F32)
    own_index = jnp.sum(jnp.where(place == slots, lanes, 0.0), axis=1, keepdims=True)

    tail = cols.shape[0] - pair
    far_cols = jnp.concatenate([hub_far, jnp.full((tail - hubs, 1), -5.0, F32)], axis=0)
    far_rows = jnp.concatenate([hub_far, jnp.full((64 - hubs, 1), -5.0, F32)], axis=0)
    cols[0:pair, :] = jnp.where(own_index == colv, 1.0, 0.0).astype(BF16)
    cols[pair:, :] = jnp.where(far_cols == colv, 1.0, 0.0).astype(BF16)
    coded = modes + 1.0
    for index, start, stop in ((own_index, 0, pair), (far_rows, pair, pair + 64)):
        hit = index == rows
        picks[start:stop, :] = jnp.where(hit, weights, 0.0).astype(BF16)
        codes[start:stop, :] = jnp.where(hit, coded, 0.0).astype(BF16)
    weight = lax.dot_general(picks[...], cols[...], NT, preferred_element_type=F32)
    code = lax.dot_general(codes[...], cols[...], NT, preferred_element_type=F32)
    for mode in range(terms):
        table = jnp.where(code == float(mode + 1), weight, 0.0).astype(BF16)
        main_ref[mode] = table[:pair]
        if mode > 0:
            send_ref[mode] = table[pair:, :pair]
    hub_lane = lax.broadcasted_iota(jnp.int32, (pair, cols.shape[0]), 1).astype(F32) - float(pair)
    own_rank = jnp.sum(
        jnp.where(lanes == own_index, rank, 0.0), axis=1, keepdims=True
    )
    main_ref[terms] = jnp.where(
        jnp.logical_and(own_rank >= 0.0, hub_lane == own_rank), 1.0, 0.0
    ).astype(BF16)
    near_rank = lax.broadcasted_iota(jnp.int32, (64, slot_total), 0).astype(F32)
    slot_row = slots
    near_slot = jnp.sum(jnp.where(near_rank == rank, slot_row, 0.0), axis=1, keepdims=True)
    near_has = jnp.sum(jnp.where(near_rank == rank, 1.0, 0.0), axis=1, keepdims=True)
    near_slot = jnp.where(near_has > 0.5, near_slot - base, -5.0)
    send_ref[0] = jnp.where(
        lax.broadcasted_iota(jnp.int32, (64, pair), 1).astype(F32) == near_slot, 1.0, 0.0
    ).astype(BF16)


def edge_kernel(field, near, far, lines, arrived):
    rows = field.shape[1]
    step = field.shape[0] // PIECES
    copies = []
    for k, row in enumerate((0, rows - 1)):
        for piece in range(PIECES):
            cut = pl.ds(piece * step, step)
            copies.append(
                pltpu.make_async_copy(
                    field.at[cut, row, :], lines.at[k, cut, :], arrived.at[k * PIECES + piece]
                )
            )
    for copy in copies:
        copy.start()
    for copy in copies:
        copy.wait()
    first = core_side() == 0
    near[...] = jnp.where(first, lines[0], lines[1])
    far[...] = jnp.where(first, lines[1], lines[0])


def split_kernel(field, unused, keep, send):
    slots, rows, width = field.shape
    first = core_side() == 0
    for at in range(0, slots, 8):
        lines = jnp.swapaxes(field[at : at + 8], 0, 1)
        for i in range(keep.shape[0]):
            keep[i, at : at + 8, :] = jnp.where(first, lines[i], lines[rows - 1 - i])
            send[i, at : at + 8, :] = jnp.where(first, lines[rows - 1 - i], lines[i])


def across(center):
    return five_point(0.0, center, 0.0)


def five_point(above, center, below):
    width = center.shape[1]
    lane = lax.broadcasted_iota(jnp.int32, center.shape, 1)
    left = jnp.where(lane == 0, 0.0, pltpu.roll(center, 1, 1))
    right = jnp.where(lane == width - 1, 0.0, pltpu.roll(center, width - 1, 1))
    return above + below + left + right - 4.0 * center


def row_place(index, rows):
    return jnp.where(core_side() == 0, index, rows - 1 - index)


def fill_buffer(value_ref, stiff, send_table, buffer, row, place):
    hubs = buffer.shape[1]
    width = buffer.shape[2]
    terms, deep, pair = send_table.shape
    lines = send_table[...].reshape(terms * deep, pair)
    for start in range(0, width, 256):
        cut = slice(start, start + 256)
        value = value_ref[row, :, cut]
        parts = jnp.dot(lines, value, preferred_element_type=F32)
        total = parts[:deep]
        for mode in range(1, terms):
            part = parts[mode * deep : (mode + 1) * deep]
            total = total + stiff[mode, pl.ds(place, 1), cut] * part
        buffer[row, :, cut] = total[:hubs].astype(BF16)


def first_kernel(first_row, keep, got, stiff, send_table, unused, bent, buffer):
    side = core_side()
    count, pair, width = bent.shape
    own = keep.shape[1]
    for group in range(2):

        def chunk(k, carry):
            at = pl.multiple_of(k * 8, 8)
            cut = pl.ds(at, 8)
            far = pl.ds(group * own + at, 8)
            lines = [
                jnp.where(side == group, keep[row, cut, :], got[row, cut, :])
                for row in range(first_row - 1, first_row + count + 1)
            ]
            for row in range(count):
                value = five_point(lines[row], lines[row + 1], lines[row + 2])
                bent[row, far, :] = value.astype(BF16)
            return carry

        lax.fori_loop(0, own // 8, chunk, 0, unroll=9)
    for row in range(count):
        fill_buffer(bent, stiff, send_table, buffer, row, row_place(first_row + row, stiff.shape[1]))


def first_base_kernel(keep, got, unused, base):
    side = core_side()
    own = keep.shape[1]
    for group in range(2):

        def chunk(k, carry):
            at = pl.multiple_of(k * 8, 8)
            cut = pl.ds(at, 8)
            here, below = [
                jnp.where(side == group, keep[row, cut, :], got[row, cut, :]) for row in range(2)
            ]
            base[pl.ds(group * own + at, 8), :] = across(here) + below
            return carry

        lax.fori_loop(0, own // 8, chunk, 0, unroll=9)


def first_outer_kernel(base, halo_near, halo_far, stiff, send_table, unused, bent, buffer):
    first = core_side() == 0
    own = halo_near.shape[0]
    near, far = halo_near[...], halo_far[...]
    halo = jnp.concatenate([jnp.where(first, near, far), jnp.where(first, far, near)], axis=0)
    bent[0] = (base[...] + halo).astype(BF16)
    fill_buffer(bent, stiff, send_table, buffer, 0, row_place(0, stiff.shape[1]))


def pass_kernel(value, unused, out):
    out[...] = value[...]


def couple_kernel(first, outer_row, inner_rows, bent, got, stiff, table, unused, moment, *rest):
    stacked = rest[-1]
    edges = list(rest[:-1])
    outer = edges.pop(0) if outer_row is not None else None
    inner = edges.pop(0) if inner_rows else None
    count, pair, width = bent.shape
    hubs = got.shape[1]
    terms = stiff.shape[0]
    room = stacked.shape[0]
    stacked[pair + hubs :, :] = jnp.zeros((room - pair - hubs, width), BF16)
    for row in range(count):
        place = row_place(first + row, stiff.shape[1])
        stacked[0:pair, :] = bent[row]
        stacked[pair : pair + hubs, :] = got[row]
        for start in range(0, width, 256):
            cut = slice(start, start + 256)
            value = stacked[:, cut]
            total = jnp.dot(table[terms], value, preferred_element_type=F32)
            for mode in range(terms):
                part = jnp.dot(table[mode], value, preferred_element_type=F32)
                total = total + stiff[mode, pl.ds(place, 1), cut] * part
            moment[row, :, cut] = total
            if first + row == outer_row:
                outer[0, :, cut] = total.astype(BF16)
            if first + row in inner_rows:
                inner[inner_rows.index(first + row), :, cut] = total.astype(BF16)


def share(held, keep, send, rows, own):
    side = core_side()
    near = pl.multiple_of(side * own, 8)
    far = pl.multiple_of((1 - side) * own, 8)
    for target, row in enumerate(rows):
        keep[target] = held[row, pl.ds(near, own), :]
        send[target] = held[row, pl.ds(far, own), :]


def second_inner_kernel(row_zero, row_one, others, inner, stiff, send_table, held, bent, buffer):
    count, pair, width = bent.shape

    def chunk(k, carry):
        cut = pl.ds(pl.multiple_of(k * STEP, STEP), STEP)
        lines = [row_zero[0, cut, :], row_one[0, cut, :]] + [others[row, cut, :] for row in range(2)]
        lines += [inner[row, cut, :].astype(F32) for row in range(2)]
        for row in range(4):
            held[row, cut, :] = five_point(lines[row], lines[row + 1], lines[row + 2])
        for row in range(2):
            value = five_point(
                held[row, cut, :], held[row + 1, cut, :], held[row + 2, cut, :]
            )
            bent[row, cut, :] = value.astype(BF16)
        return carry

    lax.fori_loop(0, pair // STEP, chunk, 0, unroll=9)
    for row in range(count):
        fill_buffer(bent, stiff, send_table, buffer, row, row_place(row + 2, stiff.shape[1]))


def second_base_kernel(row_zero, row_one, held, base, ahead, keep, send):
    pair = row_zero.shape[1]
    tile = lax.axis_index("tile")
    last = lax.axis_size("tile") - 1
    at_edge = jnp.where(core_side() == 0, tile == 0, tile == last)

    def chunk(k, carry):
        cut = pl.ds(pl.multiple_of(k * STEP, STEP), STEP)
        here = row_zero[0, cut, :]
        partial = across(here) + row_one[0, cut, :]
        base[0, cut, :] = partial
        outside = jnp.where(at_edge, 0.0, here)
        ahead[0, cut, :] = five_point(outside, partial, held[0, cut, :])
        return carry

    lax.fori_loop(0, pair // STEP, chunk, 0, unroll=9)
    share(held, keep, send, (0, 1, 2), pair // 2)


def second_edge_kernel(base, ahead, near, next_near, stiff, send_table, zero, bent, buffer):
    pair = bent.shape[1]

    def chunk(k, carry):
        cut = pl.ds(pl.multiple_of(k * STEP, STEP), STEP)
        above = near[0, cut, :].astype(F32)
        zero[0, cut, :] = base[0, cut, :] + above
        value = ahead[0, cut, :] + next_near[0, cut, :].astype(F32) + 2.0 * across(above)
        bent[0, cut, :] = value.astype(BF16)
        return carry

    lax.fori_loop(0, pair // STEP, chunk, 0, unroll=9)
    fill_buffer(bent, stiff, send_table, buffer, 0, row_place(0, stiff.shape[1]))


def second_next_kernel(zero, held, stiff, send_table, unused, keep, send, bent, buffer):
    pair = bent.shape[1]

    def chunk(k, carry):
        cut = pl.ds(pl.multiple_of(k * STEP, STEP), STEP)
        value = five_point(zero[0, cut, :], held[0, cut, :], held[1, cut, :])
        bent[0, cut, :] = value.astype(BF16)
        return carry

    lax.fori_loop(0, pair // STEP, chunk, 0, unroll=9)
    fill_buffer(bent, stiff, send_table, buffer, 0, row_place(1, stiff.shape[1]))
    share(zero, keep, send, (0,), pair // 2)


def last_kernel(zero, one, inners, inner, keep, send):
    side = core_side()
    count, own, width = keep.shape
    for target, group in ((send, 1 - side), (keep, side)):

        def chunk(k, carry):
            at = pl.multiple_of(k * 8, 8)
            cut = pl.ds(pl.multiple_of(group * own + at, 8), 8)
            lines = [jnp.zeros((8, width), F32), zero[0, cut, :], one[0, cut, :]]
            lines += [inners[row, cut, :] for row in range(2)]
            lines += [inner[0, cut, :].astype(F32)]
            for row in range(count):
                target[row, pl.ds(at, 8), :] = five_point(
                    lines[row], lines[row + 1], lines[row + 2]
                )
            return carry

        lax.fori_loop(0, own // 8, chunk, 0, unroll=9)


def write_tiles(near, far, out, lines, done):
    first = core_side() == 0
    half = out.shape[1] // 2
    copies = []
    for k, at in enumerate(range(0, out.shape[0], CHUNK)):
        for start in range(at, at + CHUNK, 8):
            ours = [near(i, slice(start, start + 8)) for i in range(half)]
            theirs = [far(i, slice(start, start + 8)) for i in range(half)]
            rows = [jnp.where(first, a, b) for a, b in zip(ours, theirs)]
            rows += [jnp.where(first, b, a) for a, b in zip(ours[::-1], theirs[::-1])]
            lines[start : start + 8] = jnp.swapaxes(jnp.stack(rows, axis=0), 0, 1)
        cut = pl.ds(at, CHUNK)
        copies.append(pltpu.make_async_copy(lines.at[cut], out.at[cut], done.at[k]))
        copies[-1].start()
    for copy in copies:
        copy.wait()


def merge_kernel(keep_zero, keep, got_zero, got, unused, out, token, lines, done):
    token[...] = jnp.zeros_like(token)

    def near(i, cut):
        return keep_zero[0, cut, :] if i == 0 else keep[i - 1, cut, :]

    def far(i, cut):
        return got_zero[0, cut, :] if i == 0 else got[i - 1, cut, :]

    write_tiles(near, far, out, lines, done)


def halves(halo, own):
    whole = halo[0].astype(F32)
    first = core_side() == 0
    lower, upper = whole[:own], whole[own:]
    return jnp.where(first, lower, upper), jnp.where(first, upper, lower)


def cut_kernel(halo, keep, unused, part, line):
    near, far = halves(halo, part.shape[0])
    part[...] = far.astype(BF16)
    line[...] = keep[0] + near


def last_merge_kernel(keep, got, line, far_halo, out, lines, done):
    far_line = far_halo[...].astype(F32)

    def near(i, cut):
        return line[cut, :] if i == 0 else keep[i, cut, :]

    def far(i, cut):
        return got[0, cut, :] + far_line[cut] if i == 0 else got[i, cut, :]

    write_tiles(near, far, out, lines, done)


def body(slot_field, stiffness, triple_modes, triple_rows, triple_cols, triple_weights, slot_of):
    own, rows, width = slot_field.shape
    terms = stiffness.shape[0]
    pair = 2 * own
    half = rows // 2
    chaos = lax.axis_size("chaos")
    tiles = lax.axis_size("tile")
    slot_total = own * chaos
    modes = terms - 1
    hubs = 1 + modes * (modes + 1) // 2
    room = -(-(pair + hubs) // 16) * 16
    side = core_side()

    core_swap = [(i, i ^ 1) for i in range(chaos)]
    chip_swap = [(i, i ^ 2) for i in range(chaos)]
    tile_swap = []
    for high in range(0, chaos, 2):
        for tile in range(tiles - 1):
            one, two = (high + 1) * tiles + tile, high * tiles + tile + 1
            tile_swap += [(one, two), (two, one)]

    def by_core(value):
        return lax.ppermute(value, "chaos", core_swap)

    def by_chip(value):
        return lax.ppermute(value, "chaos", chip_swap)

    def by_tile(value):
        return lax.ppermute(value, ("chaos", "tile"), tile_swap)

    count = triple_modes.shape[0]
    wide = -(-count // 128) * 128

    def line(value, fill):
        value = value.astype(F32)
        return jnp.pad(value, (0, wide - value.shape[0]), constant_values=fill)

    entries = jnp.stack(
        [
            line(triple_modes, -1.0),
            line(triple_rows, -1.0),
            line(triple_cols, -1.0),
            line(triple_weights, 0.0),
            line(slot_of, -1.0),
        ]
        + [jnp.zeros((wide,), F32)] * 3
    )
    row_block = shape((own, width), F32)
    near_edge, far_edge = call(
        edge_kernel,
        (row_block, row_block),
        [pltpu.VMEM((2, own, width), F32), pltpu.SemaphoreType.DMA((2 * PIECES,))],
        2.0,
        [ANY],
        60,
    )(slot_field)
    halo_far = by_tile(near_edge)
    got_edge = by_core(far_edge)
    halo_near = by_tile(got_edge)

    main_table, send_table = call(
        functools.partial(table_kernel, terms, pair, hubs, slot_total),
        (shape((terms + 1, pair, room), BF16), shape((terms, 64, pair), BF16)),
        [
            pltpu.VMEM((pair + 64, wide), BF16),
            pltpu.VMEM((pair + 64, wide), BF16),
            pltpu.VMEM((room, wide), BF16),
        ],
        3.0,
        [VMEM, ANY],
        12,
    )(entries, got_edge)

    line_block = shape((half + 1, own, width), F32)
    keep, send = call(split_kernel, (line_block, line_block), (), 2.5, [VMEM, ANY])(
        slot_field, got_edge
    )
    got = by_core(send)

    def bents(count):
        return (shape((count, pair, width), BF16), shape((count, hubs, width), BF16))

    def outs(count):
        return (shape((count, own, width), F32),) * 2

    def bend(first, count, after):
        bent, buffer = call(
            functools.partial(first_kernel, first), bents(count), (), 0.9 * count, [VMEM] * 4 + [ANY]
        )(keep, got, stiffness, send_table, after)
        return bent, buffer, by_chip(buffer)

    def couple(bent, other, first, outer_row, inner_rows, after, weight=1.0):
        count = bent.shape[0]
        out = [shape((count, pair, width), F32)]
        if outer_row is not None:
            out.append(shape((1, pair, width), BF16))
        if inner_rows:
            out.append(shape((len(inner_rows), pair, width), BF16))
        return call(
            functools.partial(couple_kernel, first, outer_row, inner_rows),
            tuple(out),
            [pltpu.VMEM((room, width), BF16)],
            weight * count,
            [VMEM] * 4 + [ANY],
        )(bent, other, stiffness, main_table, after)

    bent_one, sent, cross_one = bend(1, 1, got)
    bent_in, sent, cross_in = bend(2, 2, sent)
    base = call(first_base_kernel, shape((pair, width), F32), (), 0.4, [VMEM] * 2 + [ANY])(
        keep, got, sent
    )
    moment_one, edge_one = couple(bent_one, cross_one, 1, 1, (), base)
    bent_out, sent = call(first_outer_kernel, bents(1), (), 0.9, [VMEM] * 5 + [ANY])(
        base, halo_near, halo_far, stiffness, send_table, edge_one
    )
    cross_out = by_chip(sent)
    edge_one = call(pass_kernel, shape(edge_one.shape, BF16), (), 0.1, [VMEM, ANY])(edge_one, sent)
    next_near = by_tile(edge_one)
    moment_in, edge_in = couple(bent_in, cross_in, 2, None, (3, 2), edge_one)
    inner = by_core(edge_in)
    moment_out, edge_zero = couple(bent_out, cross_out, 0, 0, (), edge_in)
    near = by_tile(edge_zero)

    row_shape = shape((1, pair, width), F32)
    held, bent_in, buffer_in = call(
        second_inner_kernel, (shape((4, pair, width), F32),) + bents(2), (), 2.7
    )(moment_out, moment_one, moment_in, inner, stiffness, send_table)
    base, ahead, keep_in, send_in = call(
        second_base_kernel, (row_shape, row_shape) + outs(3), (), 3.0
    )(moment_out, moment_one, held)
    got_in = by_core(send_in)
    cross_in = by_chip(buffer_in)
    zero, bent_out, buffer_out = call(second_edge_kernel, (row_shape,) + bents(1), (), EARLY)(
        base, ahead, near, next_near, stiffness, send_table
    )
    cross_out = by_chip(buffer_out)
    keep_out, send_out, bent_one, buffer_one = call(
        second_next_kernel, outs(1) + bents(1), (), EARLY, [VMEM] * 4 + [ANY]
    )(zero, held, stiffness, send_table, cross_in)
    cross_one = by_chip(buffer_one)
    got_out = by_core(send_out)
    moment_out, edge_zero = couple(bent_out, cross_out, 0, 0, (), buffer_one)
    near = by_tile(edge_zero)
    moment_in, inner = couple(bent_in, cross_in, 2, None, (3,), edge_zero)
    inner = by_core(inner)
    (moment_one,) = couple(bent_one, cross_one, 1, None, (), edge_zero)

    keep, send = call(last_kernel, outs(half), (), 2.5)(
        moment_out, moment_one, moment_in, inner
    )
    got = by_core(send)
    whole = shape(slot_field.shape, F32)
    writers = [pltpu.VMEM(slot_field.shape, F32), pltpu.SemaphoreType.DMA((own // CHUNK,))]
    first_apply, token = call(
        merge_kernel, (whole, TOKEN), writers, 1.9, [VMEM] * 4 + [ANY], 6, (ANY, VMEM)
    )(keep_out, keep_in, got_out, got_in, keep)
    part, line = call(
        cut_kernel, (shape((own, width), BF16), row_block), (), 0.3, [VMEM, VMEM, ANY]
    )(near, keep, token)
    far_halo = by_core(part)
    second_apply = call(last_merge_kernel, whole, writers, 1.9, [VMEM] * 4, 6, ANY)(
        keep, got, line, far_halo
    )
    return first_apply, second_apply


def solution(mesh):
    return jax.shard_map(
        body,
        mesh=mesh,
        in_specs=(P("chaos", "tile", None), P(None, "tile", None), P(), P(), P(), P(), P()),
        out_specs=(P("chaos", "tile", None), P("chaos", "tile", None)),
        check_vma=False,
    )
```
